128 devices in a mesh: rec: 4 (over y), tm: 32 (over x, z, core).
Axes of the slice: x: 4, y: 4, z: 4, core: 2. Of those that a mesh axis runs over, the one named last changes fastest.
Arguments:
- token_values: bfloat16 [4, 8192, 2048], P('rec', 'tm'), may hold values from -6 to 6
- write_keys: bfloat16 [4, 8192, 128], P('rec', 'tm'), may hold values from -0.125 to 0.125
- read_queries: bfloat16 [4, 8192, 128], P('rec', 'tm'), may hold values from -6 to 6
- step_sizes: float32 [4, 32, 8192], P('rec', None, 'tm'), may hold values from 0.25 to 3
- decay_log: float32 [32], replicated
- skip_gain: float32 [32], replicated, may hold values from 0.5 to 2
- out_weight: bfloat16 [2048, 1024], replicated, may hold values from -0.125 to 0.125
- out_grad: bfloat16 [4, 8192, 1024], P('rec', 'tm'), may hold values from -6 to 6
Outputs:
- grad_values: float32 [4, 8192, 2048], P('rec', 'tm')
- grad_keys: float32 [4, 8192, 128], P('rec', 'tm')
- grad_queries: float32 [4, 8192, 128], P('rec', 'tm')
- grad_steps: float32 [4, 32, 8192], P('rec', None, 'tm')
- grad_decay: float32 [32], replicated
- grad_skip: float32 [32], replicated
- grad_weight: float32 [2048, 1024], P('tm')
The draws below stay inside these ranges and needn't reach their ends.
All inputs are finite; a program needn't handle non-finite values.
Results may differ from the reference program's by a relative error of at most 0.0029.
Values sent between devices are 32-bit elements; how exact they have to be, the bound alone decides.
A program may use at most 256 MiB of HBM per device.

```python
import math
import jax
import jax.numpy as jnp
from jax import lax

D_MODEL = 1024
HEADS = 32
HEAD_CHANNELS = 64
STATE = 128
SPAN = 256
SHARD_PATCHES = 256
INNER = 2048
RECORDING_COUNT = 4
PATCH_LENGTH = 8192


def draw_decay_log(key, part):
    low_end = math.log(0.3)
    high_end = math.log(max(PATCH_LENGTH / 30.0, 3.0))
    spread = jax.random.uniform(key, (HEADS,), jnp.float32, low_end, high_end)
    return spread - math.log(PATCH_LENGTH)


def draw_step_sizes(key, part):
    base_key = jax.random.fold_in(key, 1)
    spike_random_key = jax.random.fold_in(key, 2)
    base_offset = jax.random.uniform(base_key, (RECORDING_COUNT, HEADS, PATCH_LENGTH), jnp.float32, 0.25, 0.3)
    spike_draw = jax.random.randint(spike_random_key, (RECORDING_COUNT, 1, PATCH_LENGTH), 0, SHARD_PATCHES) == 0
    return jnp.where(spike_draw, 3.0, base_offset).astype(jnp.float32)


def levels(key, shape, cuts, low, high):
    gain = 1.0
    for axis_at, blocks in cuts:
        draws = jax.random.uniform(jax.random.fold_in(jax.random.fold_in(key, 6), axis_at), (blocks,), jnp.float32, low / len(cuts), high / len(cuts))
        gain = gain * jnp.repeat(jnp.exp(draws), shape[axis_at] // blocks).reshape((-1,) + (1,) * (len(shape) - 1 - axis_at))
    return gain


def noise(own_key, dims, scale, reach, cuts=(), dtype=jnp.bfloat16):
    entries = scale * jax.random.normal(own_key, dims, jnp.float32)
    if cuts:
        entries = entries * levels(own_key, dims, cuts, -0.22, 0.18)
    return jnp.clip(entries, -reach, reach).astype(dtype)


def setup_inputs(seed: int = 0) -> dict:
    arg_keys = jax.random.split(jax.random.key(seed), 9)
    token_values = noise(arg_keys[0], (RECORDING_COUNT, PATCH_LENGTH, INNER), 1.0, 6.0, ((0, 4), (1, 32)))
    write_keys = noise(arg_keys[1], (RECORDING_COUNT, PATCH_LENGTH, STATE), (STATE * SPAN // 16) ** -0.5, 0.125, ((0, 4), (1, 32)))
    read_queries = noise(arg_keys[2], (RECORDING_COUNT, PATCH_LENGTH, STATE), 1.0, 6.0, ((0, 4), (1, 32)))
    step_sizes = draw_step_sizes(jax.random.fold_in(arg_keys[8], 71), 0)
    decay_log = draw_decay_log(jax.random.fold_in(arg_keys[8], 71), 0)
    skip_gain = jnp.clip(jax.random.uniform(arg_keys[5], (HEADS,), jnp.float32, 0.5, 2.0), 0.5, 2.0)
    out_weight = noise(arg_keys[6], (INNER, D_MODEL), INNER ** -0.5, 0.125)
    out_grad = noise(arg_keys[7], (RECORDING_COUNT, PATCH_LENGTH, D_MODEL), 1.0, 6.0, ((0, 4), (1, 32)))
    return dict(token_values=token_values, write_keys=write_keys, read_queries=read_queries, step_sizes=step_sizes, decay_log=decay_log, skip_gain=skip_gain, out_weight=out_weight, out_grad=out_grad)


def block_terms(element):
    scaled, key_rows, queries, running = element
    row_iota = lax.broadcasted_iota(jnp.int32, (SPAN, SPAN), 0)
    col_iota = lax.broadcasted_iota(jnp.int32, (SPAN, SPAN), 1)
    causal = row_iota >= col_iota
    log_gap = running[:, :, None] - running[:, None, :]
    decay_mat = jnp.where(causal, jnp.exp(jnp.where(causal, log_gap, 0.0)), 0.0)
    scores = jnp.dot(queries, key_rows.T, precision=lax.Precision.HIGHEST)
    inside_offset = jnp.einsum('hij,jhp->ihp', decay_mat * scores[None], scaled, precision=lax.Precision.HIGHEST)
    to_end = jnp.exp(running[:, -1:] - running)
    weighted = scaled * to_end.T[:, :, None]
    block_state = jnp.einsum('jhp,jn->hpn', weighted, key_rows, precision=lax.Precision.HIGHEST)
    return (inside_offset, block_state)

def segment_forward(values, key_rows, queries, step_rows, decay_vec, skip_vec, state_in):
    head_count, length = step_rows.shape
    head_width = values.shape[1] // head_count
    state_width = key_rows.shape[1]
    blocks = length // SPAN
    step_rate = -jnp.exp(decay_vec)[:, None] * step_rows
    running = jnp.cumsum(step_rate.reshape(head_count, blocks, SPAN), axis=2).transpose(1, 0, 2)
    scaled = values.astype(jnp.float32).reshape(length, head_count, head_width) * step_rows.T[:, :, None]
    scaled = scaled.reshape(blocks, SPAN, head_count, head_width)
    key_blocks = key_rows.astype(jnp.float32).reshape(blocks, SPAN, state_width)
    query_blocks = queries.astype(jnp.float32).reshape(blocks, SPAN, state_width)
    inside_offset, block_states = lax.map(jax.checkpoint(block_terms), (scaled, key_blocks, query_blocks, running))
    totals = jnp.exp(running[:, :, -1])

    def advance(carried, element):
        total, block_state = element
        return (total[:, None, None] * carried + block_state, carried)
    end_state, before = lax.scan(advance, state_in, (totals, block_states))
    across = jnp.einsum('kin,khpn->kihp', query_blocks, before, precision=lax.Precision.HIGHEST)
    across = across * jnp.exp(running).transpose(0, 2, 1)[:, :, :, None]
    mixed_out = (inside_offset + across).reshape(length, head_count * head_width)
    mixed_out = mixed_out + jnp.repeat(skip_vec, head_width)[None, :] * values.astype(jnp.float32)
    return (mixed_out, end_state)

def reference(token_values, write_keys, read_queries, step_sizes, decay_log, skip_gain, out_weight, out_grad):
    zero_state = jnp.zeros((HEADS, HEAD_CHANNELS, STATE), jnp.float32)

    def per_record(record_items):
        values, key_rows, queries, step_rows, upstream = record_items

        def forward(v_arg, k_arg, q_arg, s_arg, d_arg, g_arg):
            return segment_forward(v_arg, k_arg, q_arg, s_arg, d_arg, g_arg, zero_state)[0]
        mixer_out, pullback = jax.vjp(forward, values.astype(jnp.float32), key_rows.astype(jnp.float32), queries.astype(jnp.float32), step_rows, decay_log, skip_gain)
        stored = mixer_out.astype(jnp.bfloat16)
        grad_mixer = jnp.dot(upstream, out_weight.T, preferred_element_type=jnp.float32)
        grads = pullback(grad_mixer)
        weight_term = jnp.dot(stored.T, upstream, preferred_element_type=jnp.float32)
        return tuple(grads) + (weight_term,)
    results = lax.map(per_record, (token_values, write_keys, read_queries, step_sizes, out_grad))
    return (results[0], results[1], results[2], results[3], lax.optimization_barrier(jnp.sum(results[4], axis=0)), lax.optimization_barrier(jnp.sum(results[5], axis=0)), lax.optimization_barrier(jnp.sum(results[6], axis=0)))
```

```python
import jax
import jax.numpy as jnp
from jax import lax
from jax.experimental import pallas as pl
from jax.experimental.pallas import tpu as pltpu
from jax.sharding import PartitionSpec as P

HEADS = 32
WIDTH = 64
PAIR = 2 * WIDTH
STATE = 128
SPAN = 256
INNER = HEADS * WIDTH
MODEL = 1024
CHIPS = 16
LOG2E = 1.4426950408889634
MESH = pl.DeviceIdType.MESH
HIGHEST = lax.Precision.HIGHEST
F32 = jnp.float32
BF16 = jnp.bfloat16


def nn(a, b, precision=None):
    return lax.dot_general(
        a, b, (((1,), (0,)), ((), ())), precision=precision, preferred_element_type=F32
    )


def nt(a, b, precision=None):
    return lax.dot_general(
        a, b, (((1,), (1,)), ((), ())), precision=precision, preferred_element_type=F32
    )


def column(row):
    i = lax.broadcasted_iota(jnp.int32, (HEADS, HEADS), 0)
    j = lax.broadcasted_iota(jnp.int32, (HEADS, HEADS), 1)
    whole = jnp.broadcast_to(row, (HEADS, HEADS))
    return jnp.sum(jnp.where(i == j, whole, 0.0), axis=1, keepdims=True)


def running_sums(dt, rate):
    s = lax.broadcasted_iota(jnp.int32, (SPAN, SPAN), 0)
    t = lax.broadcasted_iota(jnp.int32, (SPAN, SPAN), 1)
    upto = jnp.where(s <= t, 1.0, 0.0).astype(F32)
    return nn(-rate * dt, upto, HIGHEST)


def two_rows(ref, k):
    top = jnp.broadcast_to(ref[pl.ds(2 * k, 1), :], (WIDTH, ref.shape[1]))
    low = jnp.broadcast_to(ref[pl.ds(2 * k + 1, 1), :], (WIDTH, ref.shape[1]))
    return jnp.concatenate([top, low], axis=0)


def split(v):
    high = v.astype(BF16)
    return high, (v - high.astype(F32)).astype(BF16)


def entry_kernel(
    x_ref, k_ref, q_ref, dt_ref, dl_ref, w_ref, og_ref,
    t_ref, e_ref, d_ref, gt_ref, xt_ref, wrow, erow, drow, gbuf,
):
    dt = dt_ref[...]
    run = running_sums(dt, jnp.exp(column(dl_ref[...])))
    end = run[:, SPAN - 1 :]
    wrow[...] = jnp.exp(end - run) * dt
    erow[...] = jnp.exp(run)
    drow[...] = jnp.broadcast_to(jnp.exp(end), (HEADS, STATE))
    for h in range(HEADS):
        d_ref[h] = jnp.broadcast_to(drow[h : h + 1, :], (8, STATE))

    def chunk(m, carry):
        rows = pl.ds(pl.multiple_of(m * 512, 512), 512)
        gbuf[...] = nt(w_ref[rows, :], og_ref[...])
        for i in range(4):
            k = m * 4 + i
            at = pl.ds(pl.multiple_of(k * PAIR, PAIR), PAIR)
            g = gbuf[i * PAIR : (i + 1) * PAIR, :]
            gt_ref[at, :] = g
            high, low = split(g * two_rows(erow, k))
            e_ref[at, :] = nn(high, q_ref[...]) + nn(low, q_ref[...])
            xt = x_ref[:, at].T
            xt_ref[at, :] = xt
            high, low = split(xt.astype(F32) * two_rows(wrow, k))
            t_ref[at, :] = nn(high, k_ref[...]) + nn(low, k_ref[...])
        return carry

    lax.fori_loop(0, 4, chunk, 0)


def scan_kernel(
    t_ref, e_ref, d_ref, s_ref, ds_ref,
    tp, ep, dp, up, got, back, home, give_s, give_d,
    core_send, core_recv, out_send, out_recv, in_send, in_recv,
):
    rec, me = lax.axis_index("rec"), lax.axis_index("tm")
    c, g = lax.rem(me, 2), lax.div(me, 2)
    partner = me + 1 - 2 * c

    def peer(d):
        return lax.rem(g + d, CHIPS)

    barrier = pltpu.get_barrier_semaphore()
    pl.semaphore_signal(barrier, inc=1, device_id=(rec, partner), device_id_type=MESH)
    for d in range(1, CHIPS):
        pl.semaphore_signal(barrier, inc=1, device_id=(rec, peer(d) * 2 + c), device_id_type=MESH)
    pl.semaphore_wait(barrier, CHIPS)

    def core_copy(src, dst, i):
        return pltpu.make_async_remote_copy(
            src_ref=src, dst_ref=dst, send_sem=core_send.at[i], recv_sem=core_recv.at[i],
            device_id=(rec, partner), device_id_type=MESH,
        )

    mine, theirs = pl.ds(c * CHIPS, CHIPS), pl.ds((1 - c) * CHIPS, CHIPS)
    swaps = [
        core_copy(d_ref, dp, 0),
        core_copy(t_ref.at[theirs], tp, 1),
        core_copy(e_ref.at[theirs], ep, 2),
    ]
    for s in swaps:
        s.start()
    for s in swaps:
        s.wait()
    first = c == 0

    def both(a, b):
        return jnp.where(first, a, b), jnp.where(first, b, a)

    def combine(i, carry):
        h = c * CHIPS + i
        d0, d1 = both(d_ref[h], dp[h])
        t0, t1 = both(t_ref[h], tp[i])
        e0, e1 = both(e_ref[h], ep[i])
        up[i, 0:8] = d1[None] * t0 + t1
        up[i, 8:16] = e0 + d0[None] * e1
        up[i, 16] = d0 * d1
        return carry

    lax.fori_loop(0, CHIPS, combine, 0)

    def spread(src, dst, d, send, recv):
        return pltpu.make_async_remote_copy(
            src_ref=src.at[peer(d)], dst_ref=dst.at[g], send_sem=send.at[d], recv_sem=recv.at[d],
            device_id=(rec, peer(d) * 2 + c), device_id_type=MESH,
        )

    outs = [spread(up, got, d, out_send, out_recv) for d in range(1, CHIPS)]
    for o in outs:
        o.start()
    got[g] = up[g]
    for o in outs:
        o.wait()
    carried = jnp.zeros((8, 8, STATE), F32)
    for i in range(CHIPS):
        back[i, 0:8] = carried
        carried = got[i, 16][None] * carried + got[i, 0:8]
    carried = jnp.zeros((8, 8, STATE), F32)
    for i in range(CHIPS - 1, -1, -1):
        back[i, 8:16] = carried
        carried = got[i, 16][None] * carried + got[i, 8:16]
    ins = [spread(back, home, d, in_send, in_recv) for d in range(1, CHIPS)]
    for o in ins:
        o.start()
    home[g] = back[g]
    for o in ins:
        o.wait()

    def finish(i, carry):
        h = c * CHIPS + i
        d0, d1 = both(d_ref[h], dp[h])
        t0, t1 = both(t_ref[h], tp[i])
        e0, e1 = both(e_ref[h], ep[i])
        s0 = home[i, 0:8]
        s1 = d0[None] * s0 + t0
        b1 = home[i, 8:16]
        b0 = d1[None] * b1 + e1
        s_ref[h], give_s[i] = both(s0, s1)
        ds_ref[h], give_d[i] = both(b0, b1)
        return carry

    lax.fori_loop(0, CHIPS, finish, 0)
    gives = [core_copy(give_s, s_ref.at[mine], 3), core_copy(give_d, ds_ref.at[mine], 4)]
    for s in gives:
        s.start()
    for s in gives:
        s.wait()


def inner_kernel(
    x_ref, xt_ref, gt_ref, k_ref, q_ref, dt_ref, dl_ref, sk_ref, s_ref, ds_ref,
    gv_ref, gk_ref, gq_ref, gs_ref, sm_ref, st_ref,
    run2, crow, wrow, erow, skrow, scores, acc, qacc, kacc, frow, rrow, urow, xrow, vrow,
):
    dt = dt_ref[...]
    rate = jnp.exp(column(dl_ref[...]))
    run = running_sums(dt, rate)
    end = run[:, SPAN - 1 :]
    run2[...] = run * LOG2E
    crow[...] = run * LOG2E - jnp.log2(dt)
    wrow[...] = jnp.exp(end - run) * dt
    erow[...] = jnp.exp(run)
    skrow[...] = jnp.broadcast_to(column(sk_ref[...]), (HEADS, SPAN))
    j = lax.broadcasted_iota(jnp.int32, (SPAN, SPAN), 0)
    i = lax.broadcasted_iota(jnp.int32, (SPAN, SPAN), 1)
    causal = j <= i
    scores[...] = jnp.where(causal, nt(k_ref[...], q_ref[...]), 0.0)
    acc[...] = jnp.zeros_like(acc)
    qacc[...] = jnp.zeros_like(qacc)
    kacc[...] = jnp.zeros_like(kacc)
    half = SPAN // 2

    def pair(k, carry):
        at = pl.ds(pl.multiple_of(k * PAIR, PAIR), PAIR)
        xp = x_ref[:, at]
        xt = xt_ref[at, :]
        gf = gt_ref[at, :]
        gh, gl = split(gf)
        x2 = jnp.concatenate([xp, xp], axis=1)
        y_parts, yl_parts, dx_parts = [], [], []
        for e in range(2):
            row = run2[pl.ds(2 * k + e, 1), :]
            crow_b = jnp.broadcast_to(crow[pl.ds(2 * k + e, 1), :], (half, SPAN))
            ccol = crow_b.T
            d00 = jnp.exp2(jnp.minimum(row[:, :half] - ccol[:half], 2.0))
            d01 = jnp.exp2(row[:, half:] - ccol[:half])
            d11 = jnp.exp2(jnp.minimum(row[:, half:] - ccol[half:], 2.0))
            n00, l00 = split(d00 * scores[:half, :half])
            n01, l01 = split(d01 * scores[:half, half:])
            n11, l11 = split(d11 * scores[half:, half:])
            n10 = jnp.zeros((half, half), BF16)

            def square(a, b, d):
                top = jnp.concatenate([a, b], axis=1)
                return jnp.concatenate([top, jnp.concatenate([n10, d], axis=1)], axis=0)

            n = square(n00, n01, n11)
            part = slice(e * WIDTH, (e + 1) * WIDTH)
            y_parts.append(nn(xt[part], n))
            yl_parts.append(nn(xt[part], square(l00, l01, l11)))
            dx = nt(jnp.concatenate([gh[part], gl[part]], axis=0), n)
            dx_parts.append(dx[:WIDTH] + dx[WIDTH:])
            blank = jnp.zeros((WIDTH, SPAN), BF16)
            if e == 0:
                gz = jnp.concatenate([gh[part], blank, gl[part], blank], axis=0)
            else:
                gz = jnp.concatenate([blank, gh[part], blank, gl[part]], axis=0)
            dn = nn(x2, gz)
            acc[:half, :half] += dn[:half, :half] * d00
            acc[:half, half:] += dn[:half, half:] * d01
            acc[half:, half:] += dn[half:, half:] * d11
        xf = xt.astype(F32)
        wp = two_rows(wrow, k)
        ep = two_rows(erow, k)
        skp = two_rows(skrow, k)
        sp = s_ref[at, :]
        dsp = ds_ref[at, :]
        sh, sl = split(sp)
        dsh, dsl = split(dsp)
        y = jnp.concatenate(y_parts, axis=0) + (nt(sh, q_ref[...]) + nt(sl, q_ref[...])) * ep
        st_ref[at, :] = (y + jnp.concatenate(yl_parts, axis=0) + skp * xf).astype(BF16)
        dxs = (nt(dsh, k_ref[...]) + nt(dsl, k_ref[...])) * wp
        dx = jnp.concatenate(dx_parts, axis=0) + dxs
        gv_ref[:, at] = (dx + skp * gf).T
        ge = (gf * ep).astype(BF16)
        xw = (xf * wp).astype(BF16)
        qacc[...] += nn(sh.T, ge) + nn(sl.T, ge)
        kacc[...] += nn(dsh.T, xw) + nn(dsl.T, xw)
        for ref, value in ((frow, gf * y), (rrow, xf * dx), (urow, xf * dxs), (xrow, gf * xf), (vrow, sp * dsp)):
            for e in range(2):
                ref[pl.ds(2 * k + e, 1), :] = jnp.sum(
                    value[e * WIDTH : (e + 1) * WIDTH], axis=0, keepdims=True
                )
        return carry

    lax.fori_loop(0, HEADS // 2, pair, 0)
    dst = jnp.where(causal, acc[...], 0.0).astype(BF16)
    gk_ref[...] = nn(dst, q_ref[...]) + kacc[...].T
    gq_ref[...] = (nn(k_ref[...].T, dst) + qacc[...]).T
    upto = jnp.where(i <= j, 1.0, 0.0).astype(F32)
    tail = jnp.sum(urow[...], axis=1, keepdims=True)
    tail = tail + jnp.exp(end) * jnp.sum(vrow[...], axis=1, keepdims=True)
    da = nn(frow[...] - rrow[...], upto, HIGHEST) + tail
    gs_ref[...] = rrow[...] / dt - rate * da
    decay = jnp.sum(-rate * dt * da, axis=1, keepdims=True)
    skip = jnp.sum(xrow[...], axis=1, keepdims=True)
    lane = lax.broadcasted_iota(jnp.int32, (HEADS, 128), 1)
    sm_ref[...] = jnp.where(lane == 0, decay, jnp.where(lane == 1, skip, 0.0))


PARTS = ((0, 384, "xyz"), (384, 384, "yzx"), (768, 256, "zxy"))


def weight_kernel(
    st_ref, og_ref, sm_ref, gw_ref, smo_ref,
    f_st, f_og, r_st, r_og, lhs, rhs, dw,
    a0, a1, a2, b0, b1, b2, ra0, ra1, ra2, rb0, rb1, rb2, rc0, rc1, rc2,
    s_core, s_x, s_y, s_z,
    core_send, core_recv, send, recv, s_send, s_recv,
):
    y, me = lax.axis_index("rec"), lax.axis_index("tm")
    c, g = lax.rem(me, 2), lax.div(me, 2)
    x, z = lax.div(g, 4), lax.rem(g, 4)
    partner = me + 1 - 2 * c
    coord = {"x": x, "y": y, "z": z}

    def device(axis, value):
        if axis == "x":
            return (y, (value * 4 + z) * 2 + c)
        if axis == "z":
            return (y, (x * 4 + value) * 2 + c)
        return (value, me)

    def other(axis, d):
        return lax.rem(coord[axis] + d, 4)

    barrier = pltpu.get_barrier_semaphore()
    pl.semaphore_signal(barrier, inc=1, device_id=(y, partner), device_id_type=MESH)
    for axis in "xyz":
        for d in range(1, 4):
            pl.semaphore_signal(
                barrier, inc=1, device_id=device(axis, other(axis, d)), device_id_type=MESH
            )
    pl.semaphore_wait(barrier, 10)

    def core_copy(src, dst, n):
        return pltpu.make_async_remote_copy(
            src_ref=src, dst_ref=dst, send_sem=core_send.at[n], recv_sem=core_recv.at[n],
            device_id=(y, partner), device_id_type=MESH,
        )

    f_og[...] = og_ref[...].astype(F32)
    f_st[...] = st_ref[:, 1 - c].astype(F32)
    s_core[c] = sm_ref[...]
    swaps = [core_copy(f_og, r_og, 0), core_copy(f_st, r_st, 1), core_copy(s_core.at[c], s_core.at[c], 2)]
    for s in swaps:
        s.start()
    rhs[:SPAN] = og_ref[...]
    lhs[:, :SPAN] = st_ref[:, c].reshape(CHIPS * WIDTH, SPAN)
    for s in swaps:
        s.wait()
    rhs[SPAN:] = r_og[...].astype(BF16)
    lhs[:, SPAN:] = r_st[...].astype(BF16).reshape(CHIPS * WIDTH, SPAN)

    def product(m, carry):
        rows = pl.ds(pl.multiple_of(m * SPAN, SPAN), SPAN)
        dw[m] = nn(lhs[rows, :], rhs[...]).reshape(4, 4, 16, MODEL)
        return carry

    lax.fori_loop(0, 4, product, 0)

    def reach(axis, d, src, dst, n, sends=send, recvs=recv):
        return pltpu.make_async_remote_copy(
            src_ref=src, dst_ref=dst, send_sem=sends.at[n, d - 1], recv_sem=recvs.at[n, d - 1],
            device_id=device(axis, other(axis, d)), device_id_type=MESH,
        )

    def pick(dims, axis, value):
        return tuple(value if n == axis else slice(None) for n in dims)

    def reduce_start(p, phase, src, dims, axis, dst):
        copies = []
        for d in range(1, 4):
            at = pick(dims, axis, other(axis, d))
            if phase == 0:
                at = at + (slice(None), pl.ds(PARTS[p][0], PARTS[p][1]))
            copies.append(reach(axis, d, src.at[at], dst.at[d - 1], phase * 3 + p))
        for cp in copies:
            cp.start()
        return copies

    sums_a, sums_b = (a0, a1, a2), (b0, b1, b2)
    recv_a, recv_b, recv_c = (ra0, ra1, ra2), (rb0, rb1, rb2), (rc0, rc1, rc2)
    dims = "xzy"
    first = [
        reduce_start(p, 0, dw, dims, order[0], recv_a[p]) for p, (_, _, order) in enumerate(PARTS)
    ]
    small = s_core[0] + s_core[1]
    second = []
    for n, (axis, buf) in enumerate((("x", s_x), ("y", s_y), ("z", s_z))):
        buf[coord[axis]] = small
        copies = [
            reach(axis, d, buf.at[coord[axis]], buf.at[coord[axis]], n, s_send, s_recv) for d in range(1, 4)
        ]
        for cp in copies:
            cp.start()
        for cp in copies:
            cp.wait()
        small = (buf[0] + buf[1]) + (buf[2] + buf[3])
    smo_ref[...] = small
    for p, (low, wide, order) in enumerate(PARTS):
        for cp in first[p]:
            cp.wait()
        at = pick(dims, order[0], coord[order[0]]) + (slice(None), pl.ds(low, wide))
        got = recv_a[p]
        sums_a[p][...] = (dw[at] + got[0]) + (got[1] + got[2])
        rest = dims.replace(order[0], "")
        second.append(reduce_start(p, 1, sums_a[p], rest, order[1], recv_b[p]))
    third = []
    for p, (low, wide, order) in enumerate(PARTS):
        for cp in second[p]:
            cp.wait()
        rest = dims.replace(order[0], "")
        at = pick(rest, order[1], coord[order[1]])
        got = recv_b[p]
        sums_b[p][...] = (sums_a[p][at] + got[0]) + (got[1] + got[2])
        third.append(reduce_start(p, 2, sums_b[p], order[2], order[2], recv_c[p]))
    last = []
    rows = pl.ds(pl.multiple_of(y * 16, 16), 16)
    for p, (low, wide, order) in enumerate(PARTS):
        for cp in third[p]:
            cp.wait()
        got = recv_c[p]
        cols = pl.ds(low, wide)
        gw_ref[rows, cols] = (sums_b[p][coord[order[2]]] + got[0]) + (got[1] + got[2])
        copies = [
            reach("y", d, gw_ref.at[rows, cols], gw_ref.at[rows, cols], 9 + p) for d in range(1, 4)
        ]
        for cp in copies:
            cp.start()
        last.extend(copies)
    for cp in last:
        cp.wait()


def vmem(count):
    return [pl.BlockSpec(memory_space=pltpu.VMEM)] * count


def sds(shape, dtype=F32):
    return jax.ShapeDtypeStruct(shape, dtype)


def local(token_values, write_keys, read_queries, step_sizes, decay_log, skip_gain, out_weight, out_grad):
    x, k, q, dt, og = token_values[0], write_keys[0], read_queries[0], step_sizes[0], out_grad[0]
    dl, sk = decay_log.reshape(1, HEADS), skip_gain.reshape(1, HEADS)
    limit = 48 * 1024 * 1024
    t, e, d, gt, xt = pl.pallas_call(
        entry_kernel,
        out_shape=(
            sds((INNER, STATE)), sds((INNER, STATE)), sds((HEADS, 8, STATE)),
            sds((INNER, SPAN)), sds((INNER, SPAN), BF16),
        ),
        in_specs=vmem(7),
        out_specs=tuple(vmem(5)),
        scratch_shapes=[
            pltpu.VMEM((HEADS, SPAN), F32), pltpu.VMEM((HEADS, SPAN), F32), pltpu.VMEM((HEADS, STATE), F32),
            pltpu.VMEM((512, SPAN), F32),
        ],
        compiler_params=pltpu.CompilerParams(vmem_limit_bytes=limit),
        name="entry",
    )(x, k, q, dt, dl, out_weight, og)
    grid = (HEADS, 8, 8, STATE)
    s_in, ds_out = pl.pallas_call(
        scan_kernel,
        out_shape=(sds(grid), sds(grid)),
        in_specs=vmem(3),
        out_specs=tuple(vmem(2)),
        scratch_shapes=[
            pltpu.VMEM((CHIPS, 8, 8, STATE), F32),
            pltpu.VMEM((CHIPS, 8, 8, STATE), F32),
            pltpu.VMEM((HEADS, 8, STATE), F32),
            pltpu.VMEM((CHIPS, 17, 8, STATE), F32),
            pltpu.VMEM((CHIPS, 17, 8, STATE), F32),
            pltpu.VMEM((CHIPS, 16, 8, STATE), F32),
            pltpu.VMEM((CHIPS, 16, 8, STATE), F32),
            pltpu.VMEM((CHIPS, 8, 8, STATE), F32),
            pltpu.VMEM((CHIPS, 8, 8, STATE), F32),
            pltpu.SemaphoreType.DMA((5,)), pltpu.SemaphoreType.DMA((5,)),
            pltpu.SemaphoreType.DMA((CHIPS,)), pltpu.SemaphoreType.DMA((CHIPS,)),
            pltpu.SemaphoreType.DMA((CHIPS,)), pltpu.SemaphoreType.DMA((CHIPS,)),
        ],
        compiler_params=pltpu.CompilerParams(
            vmem_limit_bytes=limit, collective_id=0, has_side_effects=True
        ),
        name="scan",
    )(t.reshape(grid), e.reshape(grid), d)
    row = pltpu.VMEM((HEADS, SPAN), F32)
    gv, gk, gq, gs, small, stored = pl.pallas_call(
        inner_kernel,
        out_shape=(
            sds((SPAN, INNER)), sds((SPAN, STATE)), sds((SPAN, STATE)), sds((HEADS, SPAN)),
            sds((HEADS, 128)), sds((INNER, SPAN), BF16),
        ),
        in_specs=vmem(10),
        out_specs=tuple(vmem(6)),
        scratch_shapes=[
            row, row, row, row, row,
            pltpu.VMEM((SPAN, SPAN), F32), pltpu.VMEM((SPAN, SPAN), F32),
            pltpu.VMEM((STATE, SPAN), F32), pltpu.VMEM((STATE, SPAN), F32),
            row, row, row, row, pltpu.VMEM((HEADS, STATE), F32),
        ],
        compiler_params=pltpu.CompilerParams(vmem_limit_bytes=limit),
        name="inner",
    )(x, xt, gt, k, q, dt, dl, sk, s_in.reshape(INNER, STATE), ds_out.reshape(INNER, STATE))
    dma = pltpu.SemaphoreType.DMA
    wides = [w for _, w, _ in PARTS]
    gw, small = pl.pallas_call(
        weight_kernel,
        out_shape=(sds((64, MODEL)), sds((HEADS, 128))),
        in_specs=vmem(3),
        out_specs=tuple(vmem(2)),
        scratch_shapes=[
            pltpu.VMEM((CHIPS, WIDTH, SPAN), F32), pltpu.VMEM((SPAN, MODEL), F32),
            pltpu.VMEM((CHIPS, WIDTH, SPAN), F32), pltpu.VMEM((SPAN, MODEL), F32),
            pltpu.VMEM((CHIPS * WIDTH, 2 * SPAN), BF16), pltpu.VMEM((2 * SPAN, MODEL), BF16),
            pltpu.VMEM((4, 4, 4, 16, MODEL), F32),
            *[pltpu.VMEM((4, 4, 16, w), F32) for w in wides],
            *[pltpu.VMEM((4, 16, w), F32) for w in wides],
            *[pltpu.VMEM((3, 4, 4, 16, w), F32) for w in wides],
            *[pltpu.VMEM((3, 4, 16, w), F32) for w in wides],
            *[pltpu.VMEM((3, 16, w), F32) for w in wides],
            pltpu.VMEM((2, HEADS, 128), F32),
            *[pltpu.VMEM((4, HEADS, 128), F32)] * 3,
            dma((3,)), dma((3,)), dma((12, 3)), dma((12, 3)), dma((3, 3)), dma((3, 3)),
        ],
        compiler_params=pltpu.CompilerParams(
            vmem_limit_bytes=limit, collective_id=1, has_side_effects=True
        ),
        name="weight",
    )(stored.reshape(CHIPS, 2, WIDTH, SPAN), og, small)
    return gv[None], gk[None], gq[None], gs[None], small[:, 0], small[:, 1], gw


def solution(mesh):
    by_time = P("rec", "tm", None)
    by_head = P("rec", None, "tm")
    return jax.shard_map(
        local,
        mesh=mesh,
        in_specs=(by_time, by_time, by_time, by_head, P(), P(), P(), by_time),
        out_specs=(by_time, by_time, by_time, by_head, P(), P(), P("tm", None)),
        check_vma=False,
    )
```

```python
import jax
import jax.numpy as jnp
from jax import lax
from jax.experimental import pallas as pl
from jax.experimental.pallas import tpu as pltpu
from jax.sharding import PartitionSpec as P

HEADS = 32
WIDTH = 64
PAIR = 2 * WIDTH
STATE = 128
SPAN = 256
INNER = HEADS * WIDTH
MODEL = 1024
CHIPS = 16
LOG2E = 1.4426950408889634
MESH = pl.DeviceIdType.MESH
HIGHEST = lax.Precision.HIGHEST
F32 = jnp.float32
BF16 = jnp.bfloat16


def nn(a, b, precision=None):
    return lax.dot_general(
        a, b, (((1,), (0,)), ((), ())), precision=precision, preferred_element_type=F32
    )


def nt(a, b, precision=None):
    return lax.dot_general(
        a, b, (((1,), (1,)), ((), ())), precision=precision, preferred_element_type=F32
    )


def column(row):
    i = lax.broadcasted_iota(jnp.int32, (HEADS, HEADS), 0)
    j = lax.broadcasted_iota(jnp.int32, (HEADS, HEADS), 1)
    whole = jnp.broadcast_to(row, (HEADS, HEADS))
    return jnp.sum(jnp.where(i == j, whole, 0.0), axis=1, keepdims=True)


def running_sums(dt, rate):
    s = lax.broadcasted_iota(jnp.int32, (SPAN, SPAN), 0)
    t = lax.broadcasted_iota(jnp.int32, (SPAN, SPAN), 1)
    upto = jnp.where(s <= t, 1.0, 0.0).astype(F32)
    return nn(-rate * dt, upto, HIGHEST)


def two_rows(ref, k):
    top = jnp.broadcast_to(ref[pl.ds(2 * k, 1), :], (WIDTH, ref.shape[1]))
    low = jnp.broadcast_to(ref[pl.ds(2 * k + 1, 1), :], (WIDTH, ref.shape[1]))
    return jnp.concatenate([top, low], axis=0)


def split(v):
    high = v.astype(BF16)
    return high, (v - high.astype(F32)).astype(BF16)


PARTS = ((0, 384, "xyz"), (384, 384, "yzx"), (768, 256, "zxy"))
HALF = SPAN // 2


def tile(v):
    return v.reshape(8, 8, STATE)


def mixer_kernel(
    x_hbm, k_hbm, q_hbm, dt_hbm, dl_hbm, sk_hbm, w_hbm, og_hbm,
    gv_hbm, gk_ref, gq_ref, gs_ref, smo_ref, gw_ref,
    x_ref, k_ref, q_ref, dt_ref, dl_ref, sk_ref, w_ref, og_ref,
    run2, crow, wrow, erow, skrow, frow, rrow, urow, xrow, vrow,
    gbuf, xt_ref, gt_ref, t_ref, e_ref, d_ref, tp, ep, dp,
    upf, gotf, backf, homef, upb, gotb, backb, homeb,
    s_ref, ds_ref, give_s, give_d,
    scores, acc, qacc, kacc, ysum, yp, dxt, gv_ref,
    f_og, r_og, f_q, r_q, r_e, rhs, dw,
    a0, a1, a2, b0, b1, b2, ra0, ra1, ra2, rb0, rb1, rb2, rc0, rc1, rc2,
    s_core, s_x, s_y, s_z,
    in_sem, out_sem, core_send, core_recv, plane_send, plane_recv,
    first_send, first_recv, send, recv,
):
    y, me = lax.axis_index("rec"), lax.axis_index("tm")
    c, g = lax.rem(me, 2), lax.div(me, 2)
    x, z = lax.div(g, 4), lax.rem(g, 4)
    partner = me + 1 - 2 * c
    coord = {"x": x, "y": y, "z": z}
    own = c == 0

    loads = [
        pltpu.make_async_copy(src, dst, in_sem.at[n])
        for n, (src, dst) in enumerate((
            (dt_hbm, dt_ref), (dl_hbm, dl_ref), (x_hbm, x_ref), (k_hbm, k_ref),
            (q_hbm, q_ref), (og_hbm, og_ref), (w_hbm, w_ref), (sk_hbm, sk_ref),
        ))
    ]
    for n in loads:
        n.start()

    def device(axis, value):
        if axis == "x":
            return (y, (value * 4 + z) * 2 + c)
        if axis == "z":
            return (y, (x * 4 + value) * 2 + c)
        return (value, me)

    def other(axis, d):
        return lax.rem(coord[axis] + d, 4)

    def peer(d):
        return lax.rem(g + d, CHIPS)

    barrier = pltpu.get_barrier_semaphore()
    pl.semaphore_signal(barrier, inc=1, device_id=(y, partner), device_id_type=MESH)
    for d in range(1, CHIPS):
        pl.semaphore_signal(barrier, inc=1, device_id=(y, peer(d) * 2 + c), device_id_type=MESH)
    for d in range(1, 4):
        pl.semaphore_signal(barrier, inc=1, device_id=device("y", other("y", d)), device_id_type=MESH)

    def core_copy(src, dst, n):
        return pltpu.make_async_remote_copy(
            src_ref=src, dst_ref=dst, send_sem=core_send.at[n], recv_sem=core_recv.at[n],
            device_id=(y, partner), device_id_type=MESH,
        )

    def both(a, b):
        return jnp.where(own, a, b), jnp.where(own, b, a)

    loads[0].wait()
    loads[1].wait()
    dt = dt_ref[...]
    rate = jnp.exp(column(dl_ref[...]))
    run = running_sums(dt, rate)
    end = run[:, SPAN - 1 :]
    wrow[...] = jnp.exp(end - run) * dt
    erow[...] = jnp.exp(run)
    run2[...] = run * LOG2E
    crow[...] = run * LOG2E - jnp.log2(dt)
    vrow[...] = jnp.broadcast_to(jnp.exp(end), (HEADS, STATE))
    for h in range(HEADS):
        d_ref[h // 2, h % 2] = jnp.broadcast_to(vrow[h : h + 1, :], (8, STATE))

    loads[2].wait()
    loads[3].wait()

    def local_state(i, carry):
        at = pl.ds(pl.multiple_of(i * PAIR, PAIR), PAIR)
        xt = x_ref[:, at].T
        xt_ref[at, :] = xt
        high, low = split(xt.astype(F32) * two_rows(wrow, i))
        t_ref[i] = (nn(high, k_ref[...]) + nn(low, k_ref[...])).reshape(2, 8, 8, STATE)
        return carry

    lax.fori_loop(0, CHIPS, local_state, 0)
    pl.semaphore_wait(barrier, CHIPS + 3)
    swaps = [core_copy(d_ref, dp, 0), core_copy(t_ref.at[:, 1 - c], tp, 2)]
    for n in swaps:
        n.start()
    for n in loads[4:]:
        n.wait()
    for n in swaps:
        n.wait()

    def combine_forward(i, carry):
        d0, d1 = both(d_ref[i, c], dp[i, c])
        t0, t1 = both(t_ref[i, c], tp[i])
        upf[i, 0:8] = d1[None] * t0 + t1
        upf[i, 8] = d0 * d1
        return carry

    lax.fori_loop(0, CHIPS, combine_forward, 0)

    def spread(src, dst, n):
        return [
            pltpu.make_async_remote_copy(
                src_ref=src.at[peer(d)], dst_ref=dst.at[g],
                send_sem=plane_send.at[n, d], recv_sem=plane_recv.at[n, d],
                device_id=(y, peer(d) * 2 + c), device_id_type=MESH,
            )
            for d in range(1, CHIPS)
        ]

    def start(copies):
        for n in copies:
            n.start()
        return copies

    def wait(copies):
        for n in copies:
            n.wait()

    forward_out = start(spread(upf, gotf, 0))
    gotf[g] = upf[g]

    f_og[...] = og_ref[...].astype(F32)
    f_q[...] = q_ref[...].astype(F32)
    early = start([core_copy(f_og, r_og, 3), core_copy(f_q, r_q, 4), core_copy(erow, r_e, 5)])

    def cotangent(m, carry):
        rows = pl.ds(pl.multiple_of(m * 512, 512), 512)
        gbuf[...] = nt(w_ref[rows, :], og_ref[...])
        for n in range(4):
            i = m * 4 + n
            at = pl.ds(pl.multiple_of(i * PAIR, PAIR), PAIR)
            gm = gbuf[n * PAIR : (n + 1) * PAIR, :]
            gt_ref[at, :] = gm
            high, low = split(gm * two_rows(erow, i))
            e_ref[i] = (nn(high, q_ref[...]) + nn(low, q_ref[...])).reshape(2, 8, 8, STATE)
        return carry

    lax.fori_loop(0, 4, cotangent, 0)
    swap_e = start([core_copy(e_ref.at[:, 1 - c], ep, 6)])
    wait(swap_e)

    def combine_backward(i, carry):
        d0, d1 = both(d_ref[i, c], dp[i, c])
        e0, e1 = both(e_ref[i, c], ep[i])
        upb[i, 0:8] = e0 + d0[None] * e1
        upb[i, 8] = d0 * d1
        return carry

    lax.fori_loop(0, CHIPS, combine_backward, 0)
    wait(forward_out)
    carried = jnp.zeros((8, 8, STATE), F32)
    for i in range(CHIPS):
        backf[i] = carried
        carried = gotf[i, 8][None] * carried + gotf[i, 0:8]
    forward_in = start(spread(backf, homef, 1))
    homef[g] = backf[g]
    backward_out = start(spread(upb, gotb, 2))
    gotb[g] = upb[g]

    skrow[...] = jnp.broadcast_to(column(sk_ref[...]), (HEADS, SPAN))
    jj = lax.broadcasted_iota(jnp.int32, (SPAN, SPAN), 0)
    ii = lax.broadcasted_iota(jnp.int32, (SPAN, SPAN), 1)
    causal = jj <= ii
    scores[...] = jnp.where(causal, nt(k_ref[...], q_ref[...]), 0.0)
    acc[...] = jnp.zeros_like(acc)
    qacc[...] = jnp.zeros_like(qacc)
    kacc[...] = jnp.zeros_like(kacc)

    def row_sums(ref, value, i):
        for e in range(2):
            ref[pl.ds(2 * i + e, 1), :] = jnp.sum(
                value[e * WIDTH : (e + 1) * WIDTH], axis=0, keepdims=True
            )

    def inside(i, carry):
        at = pl.ds(pl.multiple_of(i * PAIR, PAIR), PAIR)
        xp = x_ref[:, at]
        xt = xt_ref[at, :]
        gf = gt_ref[at, :]
        gh, gl = split(gf)
        x2 = jnp.concatenate([xp, xp], axis=1)
        y_parts, yl_parts, dx_parts = [], [], []
        for e in range(2):
            row = run2[pl.ds(2 * i + e, 1), :]
            ccol = jnp.broadcast_to(crow[pl.ds(2 * i + e, 1), :], (HALF, SPAN)).T
            d00 = jnp.exp2(jnp.minimum(row[:, :HALF] - ccol[:HALF], 2.0))
            d01 = jnp.exp2(row[:, HALF:] - ccol[:HALF])
            d11 = jnp.exp2(jnp.minimum(row[:, HALF:] - ccol[HALF:], 2.0))
            n00, l00 = split(d00 * scores[:HALF, :HALF])
            n01, l01 = split(d01 * scores[:HALF, HALF:])
            n11, l11 = split(d11 * scores[HALF:, HALF:])
            n10 = jnp.zeros((HALF, HALF), BF16)

            def square(a, b, d):
                top = jnp.concatenate([a, b], axis=1)
                return jnp.concatenate([top, jnp.concatenate([n10, d], axis=1)], axis=0)

            n = square(n00, n01, n11)
            part = slice(e * WIDTH, (e + 1) * WIDTH)
            y_parts.append(nn(xt[part], n))
            yl_parts.append(nn(xt[part], square(l00, l01, l11)))
            dx = nt(jnp.concatenate([gh[part], gl[part]], axis=0), n)
            dx_parts.append(dx[:WIDTH] + dx[WIDTH:])
            blank = jnp.zeros((WIDTH, SPAN), BF16)
            if e == 0:
                gz = jnp.concatenate([gh[part], blank, gl[part], blank], axis=0)
            else:
                gz = jnp.concatenate([blank, gh[part], blank, gl[part]], axis=0)
            dn = nn(x2, gz)
            acc[:HALF, :HALF] += dn[:HALF, :HALF] * d00
            acc[:HALF, HALF:] += dn[:HALF, HALF:] * d01
            acc[HALF:, HALF:] += dn[HALF:, HALF:] * d11
        xf = xt.astype(F32)
        yy = jnp.concatenate(y_parts, axis=0)
        dx = jnp.concatenate(dx_parts, axis=0)
        whole = yy + jnp.concatenate(yl_parts, axis=0) + two_rows(skrow, i) * xf
        ysum[i] = whole.reshape(2, WIDTH, SPAN)
        dxt[at, :] = dx
        row_sums(frow, gf * yy, i)
        row_sums(rrow, xf * dx, i)
        row_sums(xrow, gf * xf, i)
        return carry

    lax.fori_loop(0, CHIPS // 2, inside, 0)
    wait(backward_out)
    carried = jnp.zeros((8, 8, STATE), F32)
    for i in range(CHIPS - 1, -1, -1):
        backb[i] = carried
        carried = gotb[i, 8][None] * carried + gotb[i, 0:8]
    backward_in = start(spread(backb, homeb, 3))
    homeb[g] = backb[g]
    lax.fori_loop(CHIPS // 2, CHIPS, inside, 0)
    wait(early)
    swap_y = start([core_copy(ysum.at[:, 1 - c], yp, 7)])
    rhs[:SPAN] = og_ref[...]
    rhs[SPAN:] = r_og[...].astype(BF16)
    s_mine, s_other = q_ref[...], r_q[...].astype(BF16)
    wait(swap_y)
    wait(forward_in)

    recv_a, recv_b, recv_c = (ra0, ra1, ra2), (rb0, rb1, rb2), (rc0, rc1, rc2)
    first = ([], [], [])

    def first_copy(p, axis, d, src, dst, n):
        return pltpu.make_async_remote_copy(
            src_ref=src, dst_ref=dst, send_sem=first_send.at[n], recv_sem=first_recv.at[n],
            device_id=device(axis, other(axis, d)), device_id_type=MESH,
        )

    def across(states, queries):
        high, low = split(states)
        return nt(high, queries) + nt(low, queries)

    for step, turn in enumerate((2, 1, 3, 0)):
        m = other("x", turn)
        own_states, other_states, own_rows, other_rows, own_y, other_y = [], [], [], [], [], []
        for n in range(4):
            i = m * 4 + n
            d0, _ = both(d_ref[i, c], dp[i, c])
            t0, _ = both(t_ref[i, c], tp[i])
            s0 = homef[i]
            s1 = d0[None] * s0 + t0
            mine, theirs = both(s0, s1)
            s_ref[i, c] = mine
            give_s[i] = theirs
            own_states.append(mine.reshape(WIDTH, STATE))
            other_states.append(theirs.reshape(WIDTH, STATE))
            own_rows.append(jnp.broadcast_to(erow[pl.ds(2 * i + c, 1), :], (WIDTH, SPAN)))
            other_rows.append(jnp.broadcast_to(r_e[pl.ds(2 * i + c, 1), :], (WIDTH, SPAN)))
            own_y.append(ysum[i, c])
            other_y.append(yp[i])

        def join(parts):
            return jnp.concatenate(parts, axis=0)

        left = join(own_y) + across(join(own_states), s_mine) * join(own_rows)
        right = join(other_y) + across(join(other_states), s_other) * join(other_rows)
        lhs = jnp.concatenate([left.astype(BF16), right.astype(BF16)], axis=1)
        dw[m] = nn(lhs, rhs[...]).reshape(4, 4, 16, MODEL)
        copies = []
        if turn:
            at = (slice(None), slice(None), slice(None), pl.ds(PARTS[0][0], PARTS[0][1]))
            cp = first_copy(0, "x", turn, dw.at[(m,) + at], ra0.at[turn - 1], turn - 1)
            first[0].append(cp)
            copies.append(cp)
        for d in range(1, 4):
            cols = (slice(None), pl.ds(PARTS[1][0], PARTS[1][1]))
            src = dw.at[(m, slice(None), other("y", d)) + cols]
            cp = first_copy(1, "y", d, src, ra1.at[d - 1, m], 3 + step * 3 + d - 1)
            first[1].append(cp)
            copies.append(cp)
            cols = (slice(None), pl.ds(PARTS[2][0], PARTS[2][1]))
            src = dw.at[(m, other("z", d), slice(None)) + cols]
            cp = first_copy(2, "z", d, src, ra2.at[d - 1, m], 15 + step * 3 + d - 1)
            first[2].append(cp)
            copies.append(cp)
        start(copies)

    swap_s = start([core_copy(give_s, s_ref.at[:, c], 8)])
    wait(backward_in)

    def finish_backward(i, carry):
        d0, d1 = both(d_ref[i, c], dp[i, c])
        e0, e1 = both(e_ref[i, c], ep[i])
        b1 = homeb[i]
        b0 = d1[None] * b1 + e1
        ds_ref[i, c], give_d[i] = both(b0, b1)
        return carry

    lax.fori_loop(0, CHIPS, finish_backward, 0)
    swap_d = start([core_copy(give_d, ds_ref.at[:, c], 9)])
    wait(swap_s)
    wait(swap_d)

    def outside(i, carry):
        at = pl.ds(pl.multiple_of(i * PAIR, PAIR), PAIR)
        xf = xt_ref[at, :].astype(F32)
        gf = gt_ref[at, :]
        wp = two_rows(wrow, i)
        ep2 = two_rows(erow, i)
        sp = s_ref[i].reshape(PAIR, STATE)
        dsp = ds_ref[i].reshape(PAIR, STATE)
        sh, sl = split(sp)
        dsh, dsl = split(dsp)
        yy = (nt(sh, q_ref[...]) + nt(sl, q_ref[...])) * ep2
        dxs = (nt(dsh, k_ref[...]) + nt(dsl, k_ref[...])) * wp
        gv_ref[:, at] = (dxt[at, :] + dxs + two_rows(skrow, i) * gf).T
        ge = (gf * ep2).astype(BF16)
        xw = (xf * wp).astype(BF16)
        qacc[...] += nn(sh.T, ge) + nn(sl.T, ge)
        kacc[...] += nn(dsh.T, xw) + nn(dsl.T, xw)
        fg, xd, sd = gf * yy, xf * dxs, sp * dsp
        for e in range(2):
            part = slice(e * WIDTH, (e + 1) * WIDTH)
            h = pl.ds(2 * i + e, 1)
            frow[h, :] += jnp.sum(fg[part], axis=0, keepdims=True)
            urow[h, :] = jnp.sum(xd[part], axis=0, keepdims=True)
            vrow[h, :] = jnp.sum(sd[part], axis=0, keepdims=True)
        return carry

    lax.fori_loop(0, CHIPS, outside, 0)
    store = pltpu.make_async_copy(gv_ref, gv_hbm, out_sem)
    store.start()
    dst = jnp.where(causal, acc[...], 0.0).astype(BF16)
    gk_ref[...] = nn(dst, q_ref[...]) + kacc[...].T
    gq_ref[...] = (nn(k_ref[...].T, dst) + qacc[...]).T
    upto = jnp.where(ii <= jj, 1.0, 0.0).astype(F32)
    decay = jnp.exp(run2[:, SPAN - 1 :] * (1.0 / LOG2E))
    dt = dt_ref[...]
    rate = jnp.exp(column(dl_ref[...]))
    tail = jnp.sum(urow[...], axis=1, keepdims=True)
    tail = tail + decay * jnp.sum(vrow[...], axis=1, keepdims=True)
    r = rrow[...] + urow[...]
    da = nn(frow[...] - r, upto, HIGHEST) + tail
    gs_ref[...] = r / dt - rate * da
    g_decay = jnp.sum(-rate * dt * da, axis=1, keepdims=True)
    g_skip = jnp.sum(xrow[...], axis=1, keepdims=True)
    lane = lax.broadcasted_iota(jnp.int32, (HEADS, 128), 1)
    s_core[c] = jnp.where(lane == 0, g_decay, jnp.where(lane == 1, g_skip, 0.0))
    wait(start([core_copy(s_core.at[c], s_core.at[c], 10)]))

    def reach(axis, d, src, dst, n):
        return pltpu.make_async_remote_copy(
            src_ref=src, dst_ref=dst, send_sem=send.at[n, d - 1], recv_sem=recv.at[n, d - 1],
            device_id=device(axis, other(axis, d)), device_id_type=MESH,
        )

    def small_start(axis, buf, value, n):
        buf[coord[axis]] = value
        mine = buf.at[coord[axis]]
        return start([reach(axis, d, mine, mine, n) for d in range(1, 4)])

    def small_sum(copies, buf):
        wait(copies)
        return (buf[0] + buf[1]) + (buf[2] + buf[3])

    def pick(dims, axis, value):
        return tuple(value if n == axis else slice(None) for n in dims)

    def reduce_start(src, dims, axis, dst, n):
        return start([
            reach(axis, d, src.at[pick(dims, axis, other(axis, d))], dst.at[d - 1], n) for d in range(1, 4)
        ])

    sums_a, sums_b = (a0, a1, a2), (b0, b1, b2)
    dims = "xzy"
    small = small_start("x", s_x, s_core[0] + s_core[1], 9)
    second, third, last = [], [], []
    for p, (low, wide, order) in enumerate(PARTS):
        wait(first[p])
        at = pick(dims, order[0], coord[order[0]]) + (slice(None), pl.ds(low, wide))
        got = recv_a[p]
        sums_a[p][...] = (dw[at] + got[0]) + (got[1] + got[2])
        rest = dims.replace(order[0], "")
        second.append(reduce_start(sums_a[p], rest, order[1], recv_b[p], p))
    small = small_start("y", s_y, small_sum(small, s_x), 10)
    for p, (low, wide, order) in enumerate(PARTS):
        wait(second[p])
        rest = dims.replace(order[0], "")
        at = pick(rest, order[1], coord[order[1]])
        got = recv_b[p]
        sums_b[p][...] = (sums_a[p][at] + got[0]) + (got[1] + got[2])
        third.append(reduce_start(sums_b[p], order[2], order[2], recv_c[p], 3 + p))
    small = small_start("z", s_z, small_sum(small, s_y), 11)
    rows = pl.ds(pl.multiple_of(y * 16, 16), 16)
    for p, (low, wide, order) in enumerate(PARTS):
        wait(third[p])
        got = recv_c[p]
        cols = pl.ds(low, wide)
        gw_ref[rows, cols] = (sums_b[p][coord[order[2]]] + got[0]) + (got[1] + got[2])
        mine = gw_ref.at[rows, cols]
        last.extend(start([reach("y", d, mine, mine, 6 + p) for d in range(1, 4)]))
    smo_ref[...] = small_sum(small, s_z)
    store.wait()
    wait(last)


def sds(shape, dtype=F32):
    return jax.ShapeDtypeStruct(shape, dtype)


def local(token_values, write_keys, read_queries, step_sizes, decay_log, skip_gain, out_weight, out_grad):
    x, k, q, dt, og = token_values[0], write_keys[0], read_queries[0], step_sizes[0], out_grad[0]
    dl, sk = decay_log.reshape(1, HEADS), skip_gain.reshape(1, HEADS)
    vm, dma = pltpu.VMEM, pltpu.SemaphoreType.DMA
    anywhere = pl.BlockSpec(memory_space=pl.ANY)
    inside = pl.BlockSpec(memory_space=pltpu.VMEM)
    row = vm((HEADS, SPAN), F32)
    heads = vm((CHIPS, 8, 8, STATE), F32)
    packed = vm((CHIPS, 9, 8, STATE), F32)
    pairs = vm((CHIPS, 2, 8, 8, STATE), F32)
    wides = [w for _, w, _ in PARTS]
    gv, gk, gq, gs, small, gw = pl.pallas_call(
        mixer_kernel,
        out_shape=(
            sds((SPAN, INNER)), sds((SPAN, STATE)), sds((SPAN, STATE)), sds((HEADS, SPAN)),
            sds((HEADS, 128)), sds((64, MODEL)),
        ),
        in_specs=[anywhere] * 8,
        out_specs=(anywhere,) + (inside,) * 5,
        scratch_shapes=[
            vm((SPAN, INNER), BF16), vm((SPAN, STATE), BF16), vm((SPAN, STATE), BF16), row,
            vm((1, HEADS), F32), vm((1, HEADS), F32), vm((INNER, MODEL), BF16), vm((SPAN, MODEL), BF16),
            row, row, row, row, row, row, row, row, row, vm((HEADS, STATE), F32),
            vm((512, SPAN), F32), vm((INNER, SPAN), BF16), vm((INNER, SPAN), F32),
            pairs, pairs, vm((CHIPS, 2, 8, STATE), F32), heads, heads, vm((CHIPS, 2, 8, STATE), F32),
            packed, packed, heads, heads, packed, packed, heads, heads,
            pairs, pairs, heads, heads,
            vm((SPAN, SPAN), F32), vm((SPAN, SPAN), F32), vm((STATE, SPAN), F32), vm((STATE, SPAN), F32),
            vm((CHIPS, 2, WIDTH, SPAN), F32), vm((CHIPS, WIDTH, SPAN), F32),
            vm((INNER, SPAN), F32), vm((SPAN, INNER), F32),
            vm((SPAN, MODEL), F32), vm((SPAN, MODEL), F32), vm((SPAN, STATE), F32), vm((SPAN, STATE), F32),
            row, vm((2 * SPAN, MODEL), BF16), vm((4, 4, 4, 16, MODEL), F32),
            *[vm((4, 4, 16, w), F32) for w in wides],
            *[vm((4, 16, w), F32) for w in wides],
            *[vm((3, 4, 4, 16, w), F32) for w in wides],
            *[vm((3, 4, 16, w), F32) for w in wides],
            *[vm((3, 16, w), F32) for w in wides],
            vm((2, HEADS, 128), F32),
            *[vm((4, HEADS, 128), F32)] * 3,
            dma((8,)), dma, dma((11,)), dma((11,)), dma((4, CHIPS)), dma((4, CHIPS)),
            dma((27,)), dma((27,)), dma((12, 3)), dma((12, 3)),
        ],
        compiler_params=pltpu.CompilerParams(
            vmem_limit_bytes=60 * 1024 * 1024, collective_id=0, has_side_effects=True
        ),
        name="mixer",
    )(x, k, q, dt, dl, sk, out_weight, og)
    return gv[None], gk[None], gq[None], gs[None], small[:, 0], small[:, 1], gw


def solution(mesh):
    by_time = P("rec", "tm", None)
    by_head = P("rec", None, "tm")
    return jax.shard_map(
        local,
        mesh=mesh,
        in_specs=(by_time, by_time, by_time, by_head, P(), P(), P(), by_time),
        out_specs=(by_time, by_time, by_time, by_head, P(), P(), P("tm", None)),
        check_vma=False,
    )
```

```python
import jax
import jax.numpy as jnp
from jax import lax
from jax.experimental import pallas as pl
from jax.experimental.pallas import tpu as pltpu
from jax.sharding import PartitionSpec as P

HEADS = 32
WIDTH = 64
PAIR = 2 * WIDTH
STATE = 128
SPAN = 256
INNER = HEADS * WIDTH
MODEL = 1024
CHIPS = 16
LOG2E = 1.4426950408889634
MESH = pl.DeviceIdType.MESH
HIGHEST = lax.Precision.HIGHEST
F32 = jnp.float32
BF16 = jnp.bfloat16


def nn(a, b, precision=None):
    return lax.dot_general(
        a, b, (((1,), (0,)), ((), ())), precision=precision, preferred_element_type=F32
    )


def nt(a, b, precision=None):
    return lax.dot_general(
        a, b, (((1,), (1,)), ((), ())), precision=precision, preferred_element_type=F32
    )


def column(row):
    i = lax.broadcasted_iota(jnp.int32, (HEADS, HEADS), 0)
    j = lax.broadcasted_iota(jnp.int32, (HEADS, HEADS), 1)
    whole = jnp.broadcast_to(row, (HEADS, HEADS))
    return jnp.sum(jnp.where(i == j, whole, 0.0), axis=1, keepdims=True)


def running_sums(dt, rate):
    s = lax.broadcasted_iota(jnp.int32, (SPAN, SPAN), 0)
    t = lax.broadcasted_iota(jnp.int32, (SPAN, SPAN), 1)
    upto = jnp.where(s <= t, 1.0, 0.0).astype(F32)
    return nn(-rate * dt, upto, HIGHEST)


def two_rows(ref, k):
    top = jnp.broadcast_to(ref[pl.ds(2 * k, 1), :], (WIDTH, ref.shape[1]))
    low = jnp.broadcast_to(ref[pl.ds(2 * k + 1, 1), :], (WIDTH, ref.shape[1]))
    return jnp.concatenate([top, low], axis=0)


def split(v):
    high = v.astype(BF16)
    return high, (v - high.astype(F32)).astype(BF16)


PARTS = ((640, "xyz"), (768, "yzx"), (640, "zxy"))
HALF = SPAN // 2


def tile(v):
    return v.reshape(8, 8, STATE)


def mixer_kernel(
    x_hbm, k_hbm, q_hbm, dt_hbm, dl_hbm, sk_hbm, w_hbm, og_hbm,
    gv_hbm, gk_ref, gq_ref, gs_ref, smo_ref, gw_ref,
    x_ref, k_ref, q_ref, dt_ref, dl_ref, sk_ref, w_ref, og_ref,
    run2, crow, wrow, erow, skrow, frow, rrow, urow, xrow, vrow,
    gbuf, xt_ref, gt_ref, t_ref, e_ref, d_ref, tp, ep, dp,
    upf, gotf, backf, homef, upb, gotb, backb, homeb,
    s_ref, ds_ref, give_s, give_d,
    scores, acc, qacc, kacc, ysum, yp, dxt, gv_ref,
    f_og, r_og, f_q, r_q, r_e, rhs, dw0, dw1, dw2,
    a0, a1, a2, b0, b1, b2, ra0, ra1, ra2, rb0, rb1, rb2, rc0, rc1, rc2, w0, w1, w2,
    s_core, s_x, s_y, s_z,
    in_sem, out_sem, core_send, core_recv, plane_send, plane_recv,
    first_send, first_recv, send, recv,
):
    y, me = lax.axis_index("rec"), lax.axis_index("tm")
    c, g = lax.rem(me, 2), lax.div(me, 2)
    x, z = lax.div(g, 4), lax.rem(g, 4)
    partner = me + 1 - 2 * c
    coord = {"x": x, "y": y, "z": z}
    own = c == 0

    loads = [
        pltpu.make_async_copy(src, dst, in_sem.at[n])
        for n, (src, dst) in enumerate((
            (dt_hbm, dt_ref), (dl_hbm, dl_ref), (x_hbm, x_ref), (k_hbm, k_ref),
            (q_hbm, q_ref), (og_hbm, og_ref), (w_hbm, w_ref), (sk_hbm, sk_ref),
        ))
    ]
    for n in loads:
        n.start()

    def device(axis, value):
        if axis == "x":
            return (y, (value * 4 + z) * 2 + c)
        if axis == "z":
            return (y, (x * 4 + value) * 2 + c)
        return (value, me)

    def other(axis, d):
        return lax.rem(coord[axis] + d, 4)

    def peer(d):
        return lax.rem(g + d, CHIPS)

    barrier = pltpu.get_barrier_semaphore()
    pl.semaphore_signal(barrier, inc=1, device_id=(y, partner), device_id_type=MESH)
    for d in range(1, CHIPS):
        pl.semaphore_signal(barrier, inc=1, device_id=(y, peer(d) * 2 + c), device_id_type=MESH)
    for d in range(1, 4):
        pl.semaphore_signal(barrier, inc=1, device_id=device("y", other("y", d)), device_id_type=MESH)

    def core_copy(src, dst, n):
        return pltpu.make_async_remote_copy(
            src_ref=src, dst_ref=dst, send_sem=core_send.at[n], recv_sem=core_recv.at[n],
            device_id=(y, partner), device_id_type=MESH,
        )

    def both(a, b):
        return jnp.where(own, a, b), jnp.where(own, b, a)

    def start(copies):
        for n in copies:
            n.start()
        return copies

    def wait(copies):
        for n in copies:
            n.wait()

    def spread(src, dst, n):
        return [
            pltpu.make_async_remote_copy(
                src_ref=src.at[peer(d)], dst_ref=dst.at[g],
                send_sem=plane_send.at[n, d], recv_sem=plane_recv.at[n, d],
                device_id=(y, peer(d) * 2 + c), device_id_type=MESH,
            )
            for d in range(1, CHIPS)
        ]

    loads[0].wait()
    loads[1].wait()
    dt = dt_ref[...]
    rate = jnp.exp(column(dl_ref[...]))
    run = running_sums(dt, rate)
    end = run[:, SPAN - 1 :]
    wrow[...] = jnp.exp(end - run) * dt
    erow[...] = jnp.exp(run)
    run2[...] = run * LOG2E
    crow[...] = run * LOG2E - jnp.log2(dt)
    vrow[...] = jnp.broadcast_to(jnp.exp(end), (HEADS, STATE))
    for h in range(HEADS):
        d_ref[h // 2, h % 2] = jnp.broadcast_to(vrow[h : h + 1, :], (8, STATE))

    loads[2].wait()
    loads[3].wait()

    def local_state(i, carry):
        at = pl.ds(pl.multiple_of(i * PAIR, PAIR), PAIR)
        xt = x_ref[:, at].T
        xt_ref[at, :] = xt
        high, low = split(xt.astype(F32) * two_rows(wrow, i))
        t_ref[i] = (nn(high, k_ref[...]) + nn(low, k_ref[...])).reshape(2, 8, 8, STATE)
        return carry

    lax.fori_loop(0, CHIPS, local_state, 0)
    def cotangent(m, carry):
        rows = pl.ds(pl.multiple_of(m * 512, 512), 512)
        gbuf[...] = nt(w_ref[rows, :], og_ref[...])
        for n in range(4):
            i = m * 4 + n
            at = pl.ds(pl.multiple_of(i * PAIR, PAIR), PAIR)
            gm = gbuf[n * PAIR : (n + 1) * PAIR, :]
            gt_ref[at, :] = gm
            high, low = split(gm * two_rows(erow, i))
            e_ref[i] = (nn(high, q_ref[...]) + nn(low, q_ref[...])).reshape(2, 8, 8, STATE)
        return carry

    wait(loads[4:])
    lax.fori_loop(0, 4, cotangent, 0)
    pl.semaphore_wait(barrier, CHIPS + 3)
    swaps = start([
        core_copy(d_ref, dp, 0), core_copy(t_ref.at[:, 1 - c], tp, 1), core_copy(e_ref.at[:, 1 - c], ep, 2)
    ])
    wait(swaps[:2])

    def combine_forward(i, carry):
        d0, d1 = both(d_ref[i, c], dp[i, c])
        t0, t1 = both(t_ref[i, c], tp[i])
        upf[i, 0:8] = d1[None] * t0 + t1
        upf[i, 8] = d0 * d1
        return carry

    lax.fori_loop(0, CHIPS, combine_forward, 0)

    forward_out = start(spread(upf, gotf, 0))
    gotf[g] = upf[g]

    wait(swaps[2:])

    def combine_backward(i, carry):
        d0, d1 = both(d_ref[i, c], dp[i, c])
        e0, e1 = both(e_ref[i, c], ep[i])
        upb[i, 0:8] = e0 + d0[None] * e1
        upb[i, 8] = d0 * d1
        return carry

    lax.fori_loop(0, CHIPS, combine_backward, 0)
    backward_out = start(spread(upb, gotb, 2))
    gotb[g] = upb[g]

    f_og[...] = og_ref[...].astype(F32)
    f_q[...] = q_ref[...].astype(F32)
    early = start([core_copy(f_og, r_og, 3), core_copy(f_q, r_q, 4), core_copy(erow, r_e, 5)])

    skrow[...] = jnp.broadcast_to(column(sk_ref[...]), (HEADS, SPAN))
    jj = lax.broadcasted_iota(jnp.int32, (SPAN, SPAN), 0)
    ii = lax.broadcasted_iota(jnp.int32, (SPAN, SPAN), 1)
    causal = jj <= ii
    scores[...] = jnp.where(causal, nt(k_ref[...], q_ref[...]), 0.0)
    acc[...] = jnp.zeros_like(acc)
    qacc[...] = jnp.zeros_like(qacc)
    kacc[...] = jnp.zeros_like(kacc)

    def row_sums(ref, value, i):
        for e in range(2):
            ref[pl.ds(2 * i + e, 1), :] = jnp.sum(
                value[e * WIDTH : (e + 1) * WIDTH], axis=0, keepdims=True
            )

    def inside(i, carry):
        at = pl.ds(pl.multiple_of(i * PAIR, PAIR), PAIR)
        xp = x_ref[:, at]
        xt = xt_ref[at, :]
        gf = gt_ref[at, :]
        gh, gl = split(gf)
        x2 = jnp.concatenate([xp, xp], axis=1)
        y_parts, yl_parts, dx_parts = [], [], []
        for e in range(2):
            row = run2[pl.ds(2 * i + e, 1), :]
            ccol = jnp.broadcast_to(crow[pl.ds(2 * i + e, 1), :], (HALF, SPAN)).T
            d00 = jnp.exp2(jnp.minimum(row[:, :HALF] - ccol[:HALF], 2.0))
            d01 = jnp.exp2(row[:, HALF:] - ccol[:HALF])
            d11 = jnp.exp2(jnp.minimum(row[:, HALF:] - ccol[HALF:], 2.0))
            n00, l00 = split(d00 * scores[:HALF, :HALF])
            n01, l01 = split(d01 * scores[:HALF, HALF:])
            n11, l11 = split(d11 * scores[HALF:, HALF:])
            n10 = jnp.zeros((HALF, HALF), BF16)

            def square(a, b, d):
                top = jnp.concatenate([a, b], axis=1)
                return jnp.concatenate([top, jnp.concatenate([n10, d], axis=1)], axis=0)

            n = square(n00, n01, n11)
            part = slice(e * WIDTH, (e + 1) * WIDTH)
            y_parts.append(nn(xt[part], n))
            yl_parts.append(nn(xt[part], square(l00, l01, l11)))
            dx = nt(jnp.concatenate([gh[part], gl[part]], axis=0), n)
            dx_parts.append(dx[:WIDTH] + dx[WIDTH:])
            blank = jnp.zeros((WIDTH, SPAN), BF16)
            if e == 0:
                gz = jnp.concatenate([gh[part], blank, gl[part], blank], axis=0)
            else:
                gz = jnp.concatenate([blank, gh[part], blank, gl[part]], axis=0)
            dn = nn(x2, gz)
            acc[:HALF, :HALF] += dn[:HALF, :HALF] * d00
            acc[:HALF, HALF:] += dn[:HALF, HALF:] * d01
            acc[HALF:, HALF:] += dn[HALF:, HALF:] * d11
        xf = xt.astype(F32)
        yy = jnp.concatenate(y_parts, axis=0)
        dx = jnp.concatenate(dx_parts, axis=0)
        whole = yy + jnp.concatenate(yl_parts, axis=0) + two_rows(skrow, i) * xf
        ysum[i] = whole.reshape(2, WIDTH, SPAN)
        dxt[at, :] = dx
        row_sums(frow, gf * yy, i)
        row_sums(rrow, xf * dx, i)
        row_sums(xrow, gf * xf, i)
        return carry

    lax.fori_loop(0, 6, inside, 0)
    wait(forward_out)
    carried = jnp.zeros((8, 8, STATE), F32)
    for i in range(CHIPS):
        backf[i] = carried
        carried = gotf[i, 8][None] * carried + gotf[i, 0:8]
    forward_in = start(spread(backf, homef, 1))
    homef[g] = backf[g]
    lax.fori_loop(6, 11, inside, 0)
    wait(backward_out)
    carried = jnp.zeros((8, 8, STATE), F32)
    for i in range(CHIPS - 1, -1, -1):
        backb[i] = carried
        carried = gotb[i, 8][None] * carried + gotb[i, 0:8]
    backward_in = start(spread(backb, homeb, 3))
    homeb[g] = backb[g]
    lax.fori_loop(11, CHIPS, inside, 0)
    wait(early)
    swap_y = start([core_copy(ysum.at[:, 1 - c], yp, 6)])
    rhs[:SPAN] = og_ref[...]
    rhs[SPAN:] = r_og[...].astype(BF16)
    s_mine, s_other = q_ref[...], r_q[...].astype(BF16)
    wait(swap_y)
    wait(forward_in)

    recv_a, recv_b, recv_c = (ra0, ra1, ra2), (rb0, rb1, rb2), (rc0, rc1, rc2)
    first = ([], [], [])

    def first_copy(axis, d, src, dst, n):
        return pltpu.make_async_remote_copy(
            src_ref=src, dst_ref=dst, send_sem=first_send.at[n], recv_sem=first_recv.at[n],
            device_id=device(axis, other(axis, d)), device_id_type=MESH,
        )

    def across(states, queries):
        high, low = split(states)
        return nt(high, queries) + nt(low, queries)

    for step, turn in enumerate((2, 1, 3, 0)):
        m = other("x", turn)
        own_states, other_states, own_rows, other_rows, own_y, other_y = [], [], [], [], [], []
        for n in range(4):
            i = m * 4 + n
            d0, _ = both(d_ref[i, c], dp[i, c])
            t0, _ = both(t_ref[i, c], tp[i])
            s0 = homef[i]
            s1 = d0[None] * s0 + t0
            mine, theirs = both(s0, s1)
            s_ref[i, c] = mine
            give_s[i] = theirs
            own_states.append(mine.reshape(WIDTH, STATE))
            other_states.append(theirs.reshape(WIDTH, STATE))
            own_rows.append(jnp.broadcast_to(erow[pl.ds(2 * i + c, 1), :], (WIDTH, SPAN)))
            other_rows.append(jnp.broadcast_to(r_e[pl.ds(2 * i + c, 1), :], (WIDTH, SPAN)))
            own_y.append(ysum[i, c])
            other_y.append(yp[i])

        def join(parts):
            return jnp.concatenate(parts, axis=0)

        left = join(own_y) + across(join(own_states), s_mine) * join(own_rows)
        right = join(other_y) + across(join(other_states), s_other) * join(other_rows)
        lhs = jnp.concatenate([left.astype(BF16), right.astype(BF16)], axis=1)
        whole = nn(lhs, rhs[...]).reshape(4, 4, 2, 8, MODEL)
        dw0[m] = whole[:, :, 0, :, :640]
        dw2[m] = whole[:, :, 1, :, 384:]
        for n in range(4):
            dw1[m, n, :, :, :384] = whole[:, n, 0, :, 640:]
            dw1[m, n, :, :, 384:] = whole[:, n, 1, :, :384]
        copies = []
        if turn:
            cp = first_copy("x", turn, dw0.at[m], ra0.at[turn - 1], turn - 1)
            first[0].append(cp)
            copies.append(cp)
        for d in range(1, 4):
            cp = first_copy("y", d, dw1.at[m, other("y", d)], ra1.at[d - 1, m], 3 + step * 3 + d - 1)
            first[1].append(cp)
            copies.append(cp)
            cp = first_copy("z", d, dw2.at[m, other("z", d)], ra2.at[d - 1, m], 15 + step * 3 + d - 1)
            first[2].append(cp)
            copies.append(cp)
        start(copies)

    swap_s = start([core_copy(give_s, s_ref.at[:, c], 7)])
    wait(backward_in)

    def finish_backward(i, carry):
        d0, d1 = both(d_ref[i, c], dp[i, c])
        e0, e1 = both(e_ref[i, c], ep[i])
        b1 = homeb[i]
        b0 = d1[None] * b1 + e1
        ds_ref[i, c], give_d[i] = both(b0, b1)
        return carry

    lax.fori_loop(0, CHIPS, finish_backward, 0)
    swap_d = start([core_copy(give_d, ds_ref.at[:, c], 8)])
    wait(swap_s)
    wait(swap_d)

    def outside(i, carry):
        at = pl.ds(pl.multiple_of(i * PAIR, PAIR), PAIR)
        xf = xt_ref[at, :].astype(F32)
        gf = gt_ref[at, :]
        wp = two_rows(wrow, i)
        ep2 = two_rows(erow, i)
        sp = s_ref[i].reshape(PAIR, STATE)
        dsp = ds_ref[i].reshape(PAIR, STATE)
        sh, sl = split(sp)
        dsh, dsl = split(dsp)
        yy = (nt(sh, q_ref[...]) + nt(sl, q_ref[...])) * ep2
        dxs = (nt(dsh, k_ref[...]) + nt(dsl, k_ref[...])) * wp
        gv_ref[:, at] = (dxt[at, :] + dxs + two_rows(skrow, i) * gf).T
        ge = (gf * ep2).astype(BF16)
        xw = (xf * wp).astype(BF16)
        qacc[...] += nn(sh.T, ge) + nn(sl.T, ge)
        kacc[...] += nn(dsh.T, xw) + nn(dsl.T, xw)
        fg, xd, sd = gf * yy, xf * dxs, sp * dsp
        for e in range(2):
            part = slice(e * WIDTH, (e + 1) * WIDTH)
            h = pl.ds(2 * i + e, 1)
            frow[h, :] += jnp.sum(fg[part], axis=0, keepdims=True)
            urow[h, :] = jnp.sum(xd[part], axis=0, keepdims=True)
            vrow[h, :] = jnp.sum(sd[part], axis=0, keepdims=True)
        return carry

    lax.fori_loop(0, CHIPS, outside, 0)
    store = pltpu.make_async_copy(gv_ref, gv_hbm, out_sem)
    store.start()
    dst = jnp.where(causal, acc[...], 0.0).astype(BF16)
    gk_ref[...] = nn(dst, q_ref[...]) + kacc[...].T
    gq_ref[...] = (nn(k_ref[...].T, dst) + qacc[...]).T
    upto = jnp.where(ii <= jj, 1.0, 0.0).astype(F32)
    decay = jnp.exp(run2[:, SPAN - 1 :] * (1.0 / LOG2E))
    dt = dt_ref[...]
    rate = jnp.exp(column(dl_ref[...]))
    tail = jnp.sum(urow[...], axis=1, keepdims=True)
    tail = tail + decay * jnp.sum(vrow[...], axis=1, keepdims=True)
    r = rrow[...] + urow[...]
    da = nn(frow[...] - r, upto, HIGHEST) + tail
    gs_ref[...] = r / dt - rate * da
    g_decay = jnp.sum(-rate * dt * da, axis=1, keepdims=True)
    g_skip = jnp.sum(xrow[...], axis=1, keepdims=True)
    lane = lax.broadcasted_iota(jnp.int32, (HEADS, 128), 1)
    s_core[c] = jnp.where(lane == 0, g_decay, jnp.where(lane == 1, g_skip, 0.0))
    wait(start([core_copy(s_core.at[c], s_core.at[c], 9)]))

    def reach(axis, d, src, dst, n):
        return pltpu.make_async_remote_copy(
            src_ref=src, dst_ref=dst, send_sem=send.at[n, d - 1], recv_sem=recv.at[n, d - 1],
            device_id=device(axis, other(axis, d)), device_id_type=MESH,
        )

    def small_start(axis, buf, value, n):
        buf[coord[axis]] = value
        mine = buf.at[coord[axis]]
        return start([reach(axis, d, mine, mine, n) for d in range(1, 4)])

    def small_sum(copies, buf):
        wait(copies)
        return (buf[0] + buf[1]) + (buf[2] + buf[3])

    def pick(dims, axis, value):
        return tuple(value if n == axis else slice(None) for n in dims)

    def reduce_start(src, dims, axis, dst, n):
        return start([
            reach(axis, d, src.at[pick(dims, axis, other(axis, d))], dst.at[d - 1], n) for d in range(1, 4)
        ])

    parts, sums_a, sums_b, rows = (dw0, dw1, dw2), (a0, a1, a2), (b0, b1, b2), (w0, w1, w2)
    layouts = ("xzy", "xyz", "xzy")
    small = small_start("x", s_x, s_core[0] + s_core[1], 9)
    second, third, last = [], [], []
    for p, (_, order) in enumerate(PARTS):
        wait(first[p])
        got = recv_a[p]
        mine = parts[p][pick(layouts[p], order[0], coord[order[0]])]
        sums_a[p][...] = (mine + got[0]) + (got[1] + got[2])
        rest = layouts[p].replace(order[0], "")
        second.append(reduce_start(sums_a[p], rest, order[1], recv_b[p], p))
    small = small_start("y", s_y, small_sum(small, s_x), 10)
    for p, (_, order) in enumerate(PARTS):
        wait(second[p])
        rest = layouts[p].replace(order[0], "")
        got = recv_b[p]
        mine = sums_a[p][pick(rest, order[1], coord[order[1]])]
        sums_b[p][...] = (mine + got[0]) + (got[1] + got[2])
        third.append(reduce_start(sums_b[p], order[2], order[2], recv_c[p], 3 + p))
    small = small_start("z", s_z, small_sum(small, s_y), 11)
    for p, (_, order) in enumerate(PARTS):
        wait(third[p])
        got = recv_c[p]
        rows[p][y] = (sums_b[p][coord[order[2]]] + got[0]) + (got[1] + got[2])
        last.extend(start([reach("y", d, rows[p].at[y], rows[p].at[y], 6 + p) for d in range(1, 4)]))
    smo_ref[...] = small_sum(small, s_z)
    store.wait()
    wait(last)
    for n in range(4):
        gw_ref[16 * n : 16 * n + 8, :640] = w0[n]
        gw_ref[16 * n : 16 * n + 8, 640:] = w1[n, :, :384]
        gw_ref[16 * n + 8 : 16 * n + 16, :384] = w1[n, :, 384:]
        gw_ref[16 * n + 8 : 16 * n + 16, 384:] = w2[n]


def output_kernel(
    gv, gk, gq, gs, small, gw, gv_out, gk_out, gq_out, gs_out, decay_out, skip_out, gw_out, sem
):
    quarter = SPAN // 4
    pairs = [(gv.at[pl.ds(n * quarter, quarter)], gv_out.at[pl.ds(n * quarter, quarter)]) for n in range(4)]
    pairs += [(gk, gk_out), (gq, gq_out), (gs, gs_out), (gw, gw_out)]
    copies = [pltpu.make_async_copy(a, b, sem.at[n]) for n, (a, b) in enumerate(pairs)]
    for n in copies:
        n.start()
    i = lax.broadcasted_iota(jnp.int32, (HEADS, HEADS), 0)
    j = lax.broadcasted_iota(jnp.int32, (HEADS, HEADS), 1)
    for n, ref in enumerate((decay_out, skip_out)):
        whole = jnp.broadcast_to(small[:, n : n + 1], (HEADS, HEADS))
        ref[...] = jnp.sum(jnp.where(i == j, whole, 0.0), axis=0, keepdims=True)
    for n in copies:
        n.wait()


def sds(shape, dtype=F32):
    return jax.ShapeDtypeStruct(shape, dtype)


def local(token_values, write_keys, read_queries, step_sizes, decay_log, skip_gain, out_weight, out_grad):
    x, k, q, dt, og = token_values[0], write_keys[0], read_queries[0], step_sizes[0], out_grad[0]
    dl, sk = decay_log.reshape(1, HEADS), skip_gain.reshape(1, HEADS)
    vm, dma = pltpu.VMEM, pltpu.SemaphoreType.DMA
    anywhere = pl.BlockSpec(memory_space=pl.ANY)
    inside = pl.BlockSpec(memory_space=pltpu.VMEM)
    row = vm((HEADS, SPAN), F32)
    heads = vm((CHIPS, 8, 8, STATE), F32)
    packed = vm((CHIPS, 9, 8, STATE), F32)
    pairs = vm((CHIPS, 2, 8, 8, STATE), F32)
    wides = [w for w, _ in PARTS]
    made = pl.pallas_call(
        mixer_kernel,
        out_shape=(
            sds((SPAN, INNER)), sds((SPAN, STATE)), sds((SPAN, STATE)), sds((HEADS, SPAN)),
            sds((HEADS, 128)), sds((64, MODEL)),
        ),
        in_specs=[anywhere] * 8,
        out_specs=(anywhere,) + (inside,) * 5,
        scratch_shapes=[
            vm((SPAN, INNER), BF16), vm((SPAN, STATE), BF16), vm((SPAN, STATE), BF16), row,
            vm((1, HEADS), F32), vm((1, HEADS), F32), vm((INNER, MODEL), BF16), vm((SPAN, MODEL), BF16),
            row, row, row, row, row, row, row, row, row, vm((HEADS, STATE), F32),
            vm((512, SPAN), F32), vm((INNER, SPAN), BF16), vm((INNER, SPAN), F32),
            pairs, pairs, vm((CHIPS, 2, 8, STATE), F32), heads, heads, vm((CHIPS, 2, 8, STATE), F32),
            packed, packed, heads, heads, packed, packed, heads, heads,
            pairs, pairs, heads, heads,
            vm((SPAN, SPAN), F32), vm((SPAN, SPAN), F32), vm((STATE, SPAN), F32), vm((STATE, SPAN), F32),
            vm((CHIPS, 2, WIDTH, SPAN), F32), vm((CHIPS, WIDTH, SPAN), F32),
            vm((INNER, SPAN), F32), vm((SPAN, INNER), F32),
            vm((SPAN, MODEL), F32), vm((SPAN, MODEL), F32), vm((SPAN, STATE), F32), vm((SPAN, STATE), F32),
            row, vm((2 * SPAN, MODEL), BF16), *[vm((4, 4, 4, 8, w), F32) for w in wides],
            *[vm((4, 4, 8, w), F32) for w in wides],
            *[vm((4, 8, w), F32) for w in wides],
            *[vm((3, 4, 4, 8, w), F32) for w in wides],
            *[vm((3, 4, 8, w), F32) for w in wides],
            *[vm((3, 8, w), F32) for w in wides],
            *[vm((4, 8, w), F32) for w in wides],
            vm((2, HEADS, 128), F32),
            *[vm((4, HEADS, 128), F32)] * 3,
            dma((8,)), dma, dma((10,)), dma((10,)), dma((4, CHIPS)), dma((4, CHIPS)),
            dma((27,)), dma((27,)), dma((12, 3)), dma((12, 3)),
        ],
        compiler_params=pltpu.CompilerParams(
            vmem_limit_bytes=60 * 1024 * 1024, collective_id=0, has_side_effects=True
        ),
        name="mixer",
    )(x, k, q, dt, dl, sk, out_weight, og)
    gv, gk, gq, gs, decay, skip, gw = pl.pallas_call(
        output_kernel,
        out_shape=(
            sds((SPAN, INNER)), sds((SPAN, STATE)), sds((SPAN, STATE)), sds((HEADS, SPAN)),
            sds((1, HEADS)), sds((1, HEADS)), sds((64, MODEL)),
        ),
        in_specs=[anywhere] * 4 + [inside, anywhere],
        out_specs=(anywhere,) * 4 + (inside,) * 2 + (anywhere,),
        scratch_shapes=[dma((8,))],
        compiler_params=pltpu.CompilerParams(vmem_limit_bytes=60 * 1024 * 1024),
        name="output",
    )(*made)
    return gv[None], gk[None], gq[None], gs[None], decay.reshape(HEADS), skip.reshape(HEADS), gw


def solution(mesh):
    by_time = P("rec", "tm", None)
    by_head = P("rec", None, "tm")
    return jax.shard_map(
        local,
        mesh=mesh,
        in_specs=(by_time, by_time, by_time, by_head, P(), P(), P(), by_time),
        out_specs=(by_time, by_time, by_time, by_head, P(), P(), P("tm", None)),
        check_vma=False,
    )
```

```python
import jax
import jax.numpy as jnp
from jax import lax
from jax.experimental import pallas as pl
from jax.experimental.pallas import tpu as pltpu
from jax.sharding import PartitionSpec as P

HEADS = 32
WIDTH = 64
PAIR = 2 * WIDTH
STATE = 128
SPAN = 256
INNER = HEADS * WIDTH
MODEL = 1024
CHIPS = 16
LOG2E = 1.4426950408889634
MESH = pl.DeviceIdType.MESH
HIGHEST = lax.Precision.HIGHEST
F32 = jnp.float32
BF16 = jnp.bfloat16


def nn(a, b, precision=None):
    return lax.dot_general(
        a, b, (((1,), (0,)), ((), ())), precision=precision, preferred_element_type=F32
    )


def nt(a, b, precision=None):
    return lax.dot_general(
        a, b, (((1,), (1,)), ((), ())), precision=precision, preferred_element_type=F32
    )


def column(row):
    i = lax.broadcasted_iota(jnp.int32, (HEADS, HEADS), 0)
    j = lax.broadcasted_iota(jnp.int32, (HEADS, HEADS), 1)
    whole = jnp.broadcast_to(row, (HEADS, HEADS))
    return jnp.sum(jnp.where(i == j, whole, 0.0), axis=1, keepdims=True)


def running_sums(dt, rate):
    s = lax.broadcasted_iota(jnp.int32, (SPAN, SPAN), 0)
    t = lax.broadcasted_iota(jnp.int32, (SPAN, SPAN), 1)
    upto = jnp.where(s <= t, 1.0, 0.0).astype(F32)
    return nn(-rate * dt, upto, HIGHEST)


def two_rows(ref, k):
    top = jnp.broadcast_to(ref[pl.ds(2 * k, 1), :], (WIDTH, ref.shape[1]))
    low = jnp.broadcast_to(ref[pl.ds(2 * k + 1, 1), :], (WIDTH, ref.shape[1]))
    return jnp.concatenate([top, low], axis=0)


def split(v):
    high = v.astype(BF16)
    return high, (v - high.astype(F32)).astype(BF16)


PARTS = ((640, "xyz"), (768, "yzx"), (640, "zxy"))
HALF = SPAN // 2


def tile(v):
    return v.reshape(8, 8, STATE)


def mixer_kernel(
    x_hbm, k_hbm, q_hbm, dt_hbm, dl_hbm, sk_hbm, w_hbm, og_hbm,
    gv_hbm, gk_ref, gq_ref, gs_ref, smo_ref, gw_ref,
    x_ref, k_ref, q_ref, dt_ref, dl_ref, sk_ref, w_ref, og_ref,
    run2, crow, wrow, erow, skrow, frow, rrow, urow, xrow, vrow,
    gbuf, xt_ref, gt_ref, t_ref, e_ref, d_ref, tp, ep, dp,
    upf, gotf, backf, homef, upb, gotb, backb, homeb,
    s_ref, ds_ref, give_s, give_d,
    scores, acc, qacc, kacc, ysum, yp, dxt, gv_ref,
    f_og, r_og, f_q, r_q, r_e, rhs, dw0, dw1, dw2,
    a0, a1, a2, b0, b1, b2, ra0, ra1, ra2, rb0, rb1, rb2, rc0, rc1, rc2, w0, w1, w2,
    s_core, s_x, s_y, s_z,
    in_sem, out_sem, core_send, core_recv, plane_send, plane_recv,
    first_send, first_recv, send, recv,
):
    y, me = lax.axis_index("rec"), lax.axis_index("tm")
    c, g = lax.rem(me, 2), lax.div(me, 2)
    x, z = lax.div(g, 4), lax.rem(g, 4)
    partner = me + 1 - 2 * c
    coord = {"x": x, "y": y, "z": z}
    own = c == 0

    loads = [
        pltpu.make_async_copy(src, dst, in_sem.at[n])
        for n, (src, dst) in enumerate((
            (dt_hbm, dt_ref), (dl_hbm, dl_ref), (x_hbm, x_ref), (k_hbm, k_ref),
            (q_hbm, q_ref), (og_hbm, og_ref), (w_hbm, w_ref), (sk_hbm, sk_ref),
        ))
    ]
    for n in loads:
        n.start()

    def device(axis, value):
        if axis == "x":
            return (y, (value * 4 + z) * 2 + c)
        if axis == "z":
            return (y, (x * 4 + value) * 2 + c)
        return (value, me)

    def other(axis, d):
        return lax.rem(coord[axis] + d, 4)

    def peer(d):
        return lax.rem(g + d, CHIPS)

    barrier = pltpu.get_barrier_semaphore()
    pl.semaphore_signal(barrier, inc=1, device_id=(y, partner), device_id_type=MESH)
    for d in range(1, CHIPS):
        pl.semaphore_signal(barrier, inc=1, device_id=(y, peer(d) * 2 + c), device_id_type=MESH)
    for d in range(1, 4):
        pl.semaphore_signal(barrier, inc=1, device_id=device("y", other("y", d)), device_id_type=MESH)

    def core_copy(src, dst, n):
        return pltpu.make_async_remote_copy(
            src_ref=src, dst_ref=dst, send_sem=core_send.at[n], recv_sem=core_recv.at[n],
            device_id=(y, partner), device_id_type=MESH,
        )

    def both(a, b):
        return jnp.where(own, a, b), jnp.where(own, b, a)

    def start(copies):
        for n in copies:
            n.start()
        return copies

    def wait(copies):
        for n in copies:
            n.wait()

    def spread(src, dst, n):
        return [
            pltpu.make_async_remote_copy(
                src_ref=src.at[peer(d)], dst_ref=dst.at[g],
                send_sem=plane_send.at[n, d], recv_sem=plane_recv.at[n, d],
                device_id=(y, peer(d) * 2 + c), device_id_type=MESH,
            )
            for d in range(1, CHIPS)
        ]

    loads[0].wait()
    loads[1].wait()
    dt = dt_ref[...]
    rate = jnp.exp(column(dl_ref[...]))
    run = running_sums(dt, rate)
    end = run[:, SPAN - 1 :]
    wrow[...] = jnp.exp(end - run) * dt
    erow[...] = jnp.exp(run)
    run2[...] = run * LOG2E
    crow[...] = run * LOG2E - jnp.log2(dt)
    vrow[...] = jnp.broadcast_to(jnp.exp(end), (HEADS, STATE))
    for h in range(HEADS):
        d_ref[h // 2, h % 2] = jnp.broadcast_to(vrow[h : h + 1, :], (8, STATE))

    loads[2].wait()
    loads[3].wait()

    def local_state(i, carry):
        at = pl.ds(pl.multiple_of(i * PAIR, PAIR), PAIR)
        xt = x_ref[:, at].T
        xt_ref[at, :] = xt
        high, low = split(xt.astype(F32) * two_rows(wrow, i))
        t_ref[i] = (nn(high, k_ref[...]) + nn(low, k_ref[...])).reshape(2, 8, 8, STATE)
        return carry

    lax.fori_loop(0, CHIPS, local_state, 0)
    pl.semaphore_wait(barrier, CHIPS + 3)
    wait(start([core_copy(d_ref, dp, 0), core_copy(t_ref.at[:, 1 - c], tp, 1)]))

    def combine_forward(i, carry):
        d0, d1 = both(d_ref[i, c], dp[i, c])
        t0, t1 = both(t_ref[i, c], tp[i])
        upf[i, 0:8] = d1[None] * t0 + t1
        upf[i, 8] = d0 * d1
        return carry

    lax.fori_loop(0, CHIPS, combine_forward, 0)

    forward_out = start(spread(upf, gotf, 0))
    gotf[g] = upf[g]

    wait(loads[4:])
    f_og[...] = og_ref[...].astype(F32)
    f_q[...] = q_ref[...].astype(F32)
    early = start([core_copy(f_og, r_og, 3), core_copy(f_q, r_q, 4), core_copy(erow, r_e, 5)])

    def cotangent(m, carry):
        rows = pl.ds(pl.multiple_of(m * 512, 512), 512)
        gbuf[...] = nt(w_ref[rows, :], og_ref[...])
        for n in range(4):
            i = m * 4 + n
            at = pl.ds(pl.multiple_of(i * PAIR, PAIR), PAIR)
            gm = gbuf[n * PAIR : (n + 1) * PAIR, :]
            gt_ref[at, :] = gm
            high, low = split(gm * two_rows(erow, i))
            e_ref[i] = (nn(high, q_ref[...]) + nn(low, q_ref[...])).reshape(2, 8, 8, STATE)
        return carry

    lax.fori_loop(0, 4, cotangent, 0)
    swap_e = start([core_copy(e_ref.at[:, 1 - c], ep, 2)])

    skrow[...] = jnp.broadcast_to(column(sk_ref[...]), (HEADS, SPAN))
    jj = lax.broadcasted_iota(jnp.int32, (SPAN, SPAN), 0)
    ii = lax.broadcasted_iota(jnp.int32, (SPAN, SPAN), 1)
    causal = jj <= ii
    scores[...] = jnp.where(causal, nt(k_ref[...], q_ref[...]), 0.0)
    acc[...] = jnp.zeros_like(acc)
    qacc[...] = jnp.zeros_like(qacc)
    kacc[...] = jnp.zeros_like(kacc)

    def row_sums(ref, value, i):
        for e in range(2):
            ref[pl.ds(2 * i + e, 1), :] = jnp.sum(
                value[e * WIDTH : (e + 1) * WIDTH], axis=0, keepdims=True
            )

    def inside(i, carry):
        at = pl.ds(pl.multiple_of(i * PAIR, PAIR), PAIR)
        xp = x_ref[:, at]
        xt = xt_ref[at, :]
        gf = gt_ref[at, :]
        gh, gl = split(gf)
        x2 = jnp.concatenate([xp, xp], axis=1)
        y_parts, yl_parts, dx_parts = [], [], []
        for e in range(2):
            row = run2[pl.ds(2 * i + e, 1), :]
            ccol = jnp.broadcast_to(crow[pl.ds(2 * i + e, 1), :], (HALF, SPAN)).T
            d00 = jnp.exp2(jnp.minimum(row[:, :HALF] - ccol[:HALF], 2.0))
            d01 = jnp.exp2(row[:, HALF:] - ccol[:HALF])
            d11 = jnp.exp2(jnp.minimum(row[:, HALF:] - ccol[HALF:], 2.0))
            n00, l00 = split(d00 * scores[:HALF, :HALF])
            n01, l01 = split(d01 * scores[:HALF, HALF:])
            n11, l11 = split(d11 * scores[HALF:, HALF:])
            n10 = jnp.zeros((HALF, HALF), BF16)

            def square(a, b, d):
                top = jnp.concatenate([a, b], axis=1)
                return jnp.concatenate([top, jnp.concatenate([n10, d], axis=1)], axis=0)

            n = square(n00, n01, n11)
            part = slice(e * WIDTH, (e + 1) * WIDTH)
            y_parts.append(nn(xt[part], n))
            yl_parts.append(nn(xt[part], square(l00, l01, l11)))
            dx = nt(jnp.concatenate([gh[part], gl[part]], axis=0), n)
            dx_parts.append(dx[:WIDTH] + dx[WIDTH:])
            blank = jnp.zeros((WIDTH, SPAN), BF16)
            if e == 0:
                gz = jnp.concatenate([gh[part], blank, gl[part], blank], axis=0)
            else:
                gz = jnp.concatenate([blank, gh[part], blank, gl[part]], axis=0)
            dn = nn(x2, gz)
            acc[:HALF, :HALF] += dn[:HALF, :HALF] * d00
            acc[:HALF, HALF:] += dn[:HALF, HALF:] * d01
            acc[HALF:, HALF:] += dn[HALF:, HALF:] * d11
        xf = xt.astype(F32)
        yy = jnp.concatenate(y_parts, axis=0)
        dx = jnp.concatenate(dx_parts, axis=0)
        whole = yy + jnp.concatenate(yl_parts, axis=0) + two_rows(skrow, i) * xf
        ysum[i] = whole.reshape(2, WIDTH, SPAN)
        dxt[at, :] = dx
        row_sums(frow, gf * yy, i)
        row_sums(rrow, xf * dx, i)
        row_sums(xrow, gf * xf, i)
        return carry

    lax.fori_loop(0, 3, inside, 0)
    wait(swap_e)

    def combine_backward(i, carry):
        d0, d1 = both(d_ref[i, c], dp[i, c])
        e0, e1 = both(e_ref[i, c], ep[i])
        upb[i, 0:8] = e0 + d0[None] * e1
        upb[i, 8] = d0 * d1
        return carry

    lax.fori_loop(0, CHIPS, combine_backward, 0)
    backward_out = start(spread(upb, gotb, 2))
    gotb[g] = upb[g]
    lax.fori_loop(3, 6, inside, 0)
    wait(forward_out)
    carried = jnp.zeros((8, 8, STATE), F32)
    for i in range(CHIPS):
        backf[i] = carried
        carried = gotf[i, 8][None] * carried + gotf[i, 0:8]
    forward_in = start(spread(backf, homef, 1))
    homef[g] = backf[g]
    lax.fori_loop(6, CHIPS, inside, 0)
    wait(early)
    swap_y = start([core_copy(ysum.at[:, 1 - c], yp, 6)])
    rhs[:SPAN] = og_ref[...]
    rhs[SPAN:] = r_og[...].astype(BF16)
    s_mine, s_other = q_ref[...], r_q[...].astype(BF16)
    wait(backward_out)
    carried = jnp.zeros((8, 8, STATE), F32)
    for i in range(CHIPS - 1, -1, -1):
        backb[i] = carried
        carried = gotb[i, 8][None] * carried + gotb[i, 0:8]
    backward_in = start(spread(backb, homeb, 3))
    homeb[g] = backb[g]
    wait(swap_y)
    wait(forward_in)

    recv_a, recv_b, recv_c = (ra0, ra1, ra2), (rb0, rb1, rb2), (rc0, rc1, rc2)
    first = ([], [], [])

    def first_copy(axis, d, src, dst, n):
        return pltpu.make_async_remote_copy(
            src_ref=src, dst_ref=dst, send_sem=first_send.at[n], recv_sem=first_recv.at[n],
            device_id=device(axis, other(axis, d)), device_id_type=MESH,
        )

    def across(states, queries):
        high, low = split(states)
        return nt(high, queries) + nt(low, queries)

    for step, turn in enumerate((2, 1, 3, 0)):
        m = other("x", turn)
        own_states, other_states, own_rows, other_rows, own_y, other_y = [], [], [], [], [], []
        for n in range(4):
            i = m * 4 + n
            d0, _ = both(d_ref[i, c], dp[i, c])
            t0, _ = both(t_ref[i, c], tp[i])
            s0 = homef[i]
            s1 = d0[None] * s0 + t0
            mine, theirs = both(s0, s1)
            s_ref[i, c] = mine
            give_s[i] = theirs
            own_states.append(mine.reshape(WIDTH, STATE))
            other_states.append(theirs.reshape(WIDTH, STATE))
            own_rows.append(jnp.broadcast_to(erow[pl.ds(2 * i + c, 1), :], (WIDTH, SPAN)))
            other_rows.append(jnp.broadcast_to(r_e[pl.ds(2 * i + c, 1), :], (WIDTH, SPAN)))
            own_y.append(ysum[i, c])
            other_y.append(yp[i])

        def join(parts):
            return jnp.concatenate(parts, axis=0)

        left = join(own_y) + across(join(own_states), s_mine) * join(own_rows)
        right = join(other_y) + across(join(other_states), s_other) * join(other_rows)
        lhs = jnp.concatenate([left.astype(BF16), right.astype(BF16)], axis=1)
        whole = nn(lhs, rhs[...]).reshape(4, 4, 2, 8, MODEL)
        dw0[m] = whole[:, :, 0, :, :640]
        dw2[m] = whole[:, :, 1, :, 384:]
        for n in range(4):
            dw1[m, n, :, :, :384] = whole[:, n, 0, :, 640:]
            dw1[m, n, :, :, 384:] = whole[:, n, 1, :, :384]
        copies = []
        if turn:
            cp = first_copy("x", turn, dw0.at[m], ra0.at[turn - 1], turn - 1)
            first[0].append(cp)
            copies.append(cp)
        for d in range(1, 4):
            cp = first_copy("y", d, dw1.at[m, other("y", d)], ra1.at[d - 1, m], 3 + step * 3 + d - 1)
            first[1].append(cp)
            copies.append(cp)
            cp = first_copy("z", d, dw2.at[m, other("z", d)], ra2.at[d - 1, m], 15 + step * 3 + d - 1)
            first[2].append(cp)
            copies.append(cp)
        start(copies)

    swap_s = start([core_copy(give_s, s_ref.at[:, c], 7)])
    wait(backward_in)

    def finish_backward(i, carry):
        d0, d1 = both(d_ref[i, c], dp[i, c])
        e0, e1 = both(e_ref[i, c], ep[i])
        b1 = homeb[i]
        b0 = d1[None] * b1 + e1
        ds_ref[i, c], give_d[i] = both(b0, b1)
        return carry

    lax.fori_loop(0, CHIPS, finish_backward, 0)
    swap_d = start([core_copy(give_d, ds_ref.at[:, c], 8)])
    wait(swap_s)
    wait(swap_d)

    def outside(i, carry):
        at = pl.ds(pl.multiple_of(i * PAIR, PAIR), PAIR)
        xf = xt_ref[at, :].astype(F32)
        gf = gt_ref[at, :]
        wp = two_rows(wrow, i)
        ep2 = two_rows(erow, i)
        sp = s_ref[i].reshape(PAIR, STATE)
        dsp = ds_ref[i].reshape(PAIR, STATE)
        sh, sl = split(sp)
        dsh, dsl = split(dsp)
        yy = (nt(sh, q_ref[...]) + nt(sl, q_ref[...])) * ep2
        dxs = (nt(dsh, k_ref[...]) + nt(dsl, k_ref[...])) * wp
        gv_ref[:, at] = (dxt[at, :] + dxs + two_rows(skrow, i) * gf).T
        ge = (gf * ep2).astype(BF16)
        xw = (xf * wp).astype(BF16)
        qacc[...] += nn(sh.T, ge) + nn(sl.T, ge)
        kacc[...] += nn(dsh.T, xw) + nn(dsl.T, xw)
        fg, xd, sd = gf * yy, xf * dxs, sp * dsp
        for e in range(2):
            part = slice(e * WIDTH, (e + 1) * WIDTH)
            h = pl.ds(2 * i + e, 1)
            frow[h, :] += jnp.sum(fg[part], axis=0, keepdims=True)
            urow[h, :] = jnp.sum(xd[part], axis=0, keepdims=True)
            vrow[h, :] = jnp.sum(sd[part], axis=0, keepdims=True)
        return carry

    lax.fori_loop(0, CHIPS, outside, 0)
    store = pltpu.make_async_copy(gv_ref, gv_hbm, out_sem)
    store.start()
    dst = jnp.where(causal, acc[...], 0.0).astype(BF16)
    gk_ref[...] = nn(dst, q_ref[...]) + kacc[...].T
    gq_ref[...] = (nn(k_ref[...].T, dst) + qacc[...]).T
    upto = jnp.where(ii <= jj, 1.0, 0.0).astype(F32)
    decay = jnp.exp(run2[:, SPAN - 1 :] * (1.0 / LOG2E))
    dt = dt_ref[...]
    rate = jnp.exp(column(dl_ref[...]))
    tail = jnp.sum(urow[...], axis=1, keepdims=True)
    tail = tail + decay * jnp.sum(vrow[...], axis=1, keepdims=True)
    r = rrow[...] + urow[...]
    da = nn(frow[...] - r, upto, HIGHEST) + tail
    gs_ref[...] = r / dt - rate * da
    g_decay = jnp.sum(-rate * dt * da, axis=1, keepdims=True)
    g_skip = jnp.sum(xrow[...], axis=1, keepdims=True)
    lane = lax.broadcasted_iota(jnp.int32, (HEADS, 128), 1)
    s_core[c] = jnp.where(lane == 0, g_decay, jnp.where(lane == 1, g_skip, 0.0))
    wait(start([core_copy(s_core.at[c], s_core.at[c], 9)]))

    def reach(axis, d, src, dst, n):
        return pltpu.make_async_remote_copy(
            src_ref=src, dst_ref=dst, send_sem=send.at[n, d - 1], recv_sem=recv.at[n, d - 1],
            device_id=device(axis, other(axis, d)), device_id_type=MESH,
        )

    def small_start(axis, buf, value, n):
        buf[coord[axis]] = value
        mine = buf.at[coord[axis]]
        return start([reach(axis, d, mine, mine, n) for d in range(1, 4)])

    def small_sum(copies, buf):
        wait(copies)
        return (buf[0] + buf[1]) + (buf[2] + buf[3])

    def pick(dims, axis, value):
        return tuple(value if n == axis else slice(None) for n in dims)

    def reduce_start(src, dims, axis, dst, n):
        return start([
            reach(axis, d, src.at[pick(dims, axis, other(axis, d))], dst.at[d - 1], n) for d in range(1, 4)
        ])

    parts, sums_a, sums_b, rows = (dw0, dw1, dw2), (a0, a1, a2), (b0, b1, b2), (w0, w1, w2)
    layouts = ("xzy", "xyz", "xzy")
    small = small_start("x", s_x, s_core[0] + s_core[1], 9)
    second, third, last = [], [], []
    for p, (_, order) in enumerate(PARTS):
        wait(first[p])
        got = recv_a[p]
        mine = parts[p][pick(layouts[p], order[0], coord[order[0]])]
        sums_a[p][...] = (mine + got[0]) + (got[1] + got[2])
        rest = layouts[p].replace(order[0], "")
        second.append(reduce_start(sums_a[p], rest, order[1], recv_b[p], p))
    small = small_start("y", s_y, small_sum(small, s_x), 10)
    for p, (_, order) in enumerate(PARTS):
        wait(second[p])
        rest = layouts[p].replace(order[0], "")
        got = recv_b[p]
        mine = sums_a[p][pick(rest, order[1], coord[order[1]])]
        sums_b[p][...] = (mine + got[0]) + (got[1] + got[2])
        third.append(reduce_start(sums_b[p], order[2], order[2], recv_c[p], 3 + p))
    small = small_start("z", s_z, small_sum(small, s_y), 11)
    for p, (_, order) in enumerate(PARTS):
        wait(third[p])
        got = recv_c[p]
        rows[p][y] = (sums_b[p][coord[order[2]]] + got[0]) + (got[1] + got[2])
        last.extend(start([reach("y", d, rows[p].at[y], rows[p].at[y], 6 + p) for d in range(1, 4)]))
    smo_ref[...] = small_sum(small, s_z)
    store.wait()
    wait(last)
    for n in range(4):
        gw_ref[16 * n : 16 * n + 8, :640] = w0[n]
        gw_ref[16 * n : 16 * n + 8, 640:] = w1[n, :, :384]
        gw_ref[16 * n + 8 : 16 * n + 16, :384] = w1[n, :, 384:]
        gw_ref[16 * n + 8 : 16 * n + 16, 384:] = w2[n]


def output_kernel(
    gv, gk, gq, gs, small, gw, gv_out, gk_out, gq_out, gs_out, decay_out, skip_out, gw_out,
    vv, vk, vq, vs, vw, into, out,
):
    quarter = SPAN // 4
    parts = [pl.ds(n * quarter, quarter) for n in range(4)]
    moves = [(gv.at[n], vv.at[n], gv_out.at[n]) for n in parts]
    moves += [(gw, vw, gw_out), (gk, vk, gk_out), (gq, vq, gq_out), (gs, vs, gs_out)]
    reads = [pltpu.make_async_copy(a, b, into.at[n]) for n, (a, b, _) in enumerate(moves)]
    writes = [pltpu.make_async_copy(b, a, out.at[n]) for n, (_, b, a) in enumerate(moves)]
    for n in reads:
        n.start()
    i = lax.broadcasted_iota(jnp.int32, (HEADS, HEADS), 0)
    j = lax.broadcasted_iota(jnp.int32, (HEADS, HEADS), 1)
    for n, ref in enumerate((decay_out, skip_out)):
        whole = jnp.broadcast_to(small[:, n : n + 1], (HEADS, HEADS))
        ref[...] = jnp.sum(jnp.where(i == j, whole, 0.0), axis=0, keepdims=True)
    for a, b in zip(reads, writes):
        a.wait()
        b.start()
    for n in writes:
        n.wait()


def sds(shape, dtype=F32):
    return jax.ShapeDtypeStruct(shape, dtype)


def local(token_values, write_keys, read_queries, step_sizes, decay_log, skip_gain, out_weight, out_grad):
    x, k, q, dt, og = token_values[0], write_keys[0], read_queries[0], step_sizes[0], out_grad[0]
    dl, sk = decay_log.reshape(1, HEADS), skip_gain.reshape(1, HEADS)
    vm, dma = pltpu.VMEM, pltpu.SemaphoreType.DMA
    anywhere = pl.BlockSpec(memory_space=pl.ANY)
    inside = pl.BlockSpec(memory_space=pltpu.VMEM)
    row = vm((HEADS, SPAN), F32)
    heads = vm((CHIPS, 8, 8, STATE), F32)
    packed = vm((CHIPS, 9, 8, STATE), F32)
    pairs = vm((CHIPS, 2, 8, 8, STATE), F32)
    wides = [w for w, _ in PARTS]
    made = pl.pallas_call(
        mixer_kernel,
        out_shape=(
            sds((SPAN, INNER)), sds((SPAN, STATE)), sds((SPAN, STATE)), sds((HEADS, SPAN)),
            sds((HEADS, 128)), sds((64, MODEL)),
        ),
        in_specs=[anywhere] * 8,
        out_specs=(anywhere,) + (inside,) * 5,
        scratch_shapes=[
            vm((SPAN, INNER), BF16), vm((SPAN, STATE), BF16), vm((SPAN, STATE), BF16), row,
            vm((1, HEADS), F32), vm((1, HEADS), F32), vm((INNER, MODEL), BF16), vm((SPAN, MODEL), BF16),
            row, row, row, row, row, row, row, row, row, vm((HEADS, STATE), F32),
            vm((512, SPAN), F32), vm((INNER, SPAN), BF16), vm((INNER, SPAN), F32),
            pairs, pairs, vm((CHIPS, 2, 8, STATE), F32), heads, heads, vm((CHIPS, 2, 8, STATE), F32),
            packed, packed, heads, heads, packed, packed, heads, heads,
            pairs, pairs, heads, heads,
            vm((SPAN, SPAN), F32), vm((SPAN, SPAN), F32), vm((STATE, SPAN), F32), vm((STATE, SPAN), F32),
            vm((CHIPS, 2, WIDTH, SPAN), F32), vm((CHIPS, WIDTH, SPAN), F32),
            vm((INNER, SPAN), F32), vm((SPAN, INNER), F32),
            vm((SPAN, MODEL), F32), vm((SPAN, MODEL), F32), vm((SPAN, STATE), F32), vm((SPAN, STATE), F32),
            row, vm((2 * SPAN, MODEL), BF16), *[vm((4, 4, 4, 8, w), F32) for w in wides],
            *[vm((4, 4, 8, w), F32) for w in wides],
            *[vm((4, 8, w), F32) for w in wides],
            *[vm((3, 4, 4, 8, w), F32) for w in wides],
            *[vm((3, 4, 8, w), F32) for w in wides],
            *[vm((3, 8, w), F32) for w in wides],
            *[vm((4, 8, w), F32) for w in wides],
            vm((2, HEADS, 128), F32),
            *[vm((4, HEADS, 128), F32)] * 3,
            dma((8,)), dma, dma((10,)), dma((10,)), dma((4, CHIPS)), dma((4, CHIPS)),
            dma((27,)), dma((27,)), dma((12, 3)), dma((12, 3)),
        ],
        compiler_params=pltpu.CompilerParams(
            vmem_limit_bytes=60 * 1024 * 1024, collective_id=0, has_side_effects=True
        ),
        name="mixer",
    )(x, k, q, dt, dl, sk, out_weight, og)
    gv, gk, gq, gs, decay, skip, gw = pl.pallas_call(
        output_kernel,
        out_shape=(
            sds((SPAN, INNER)), sds((SPAN, STATE)), sds((SPAN, STATE)), sds((HEADS, SPAN)),
            sds((1, HEADS)), sds((1, HEADS)), sds((64, MODEL)),
        ),
        in_specs=[anywhere] * 4 + [inside, anywhere],
        out_specs=(anywhere,) * 4 + (inside,) * 2 + (anywhere,),
        scratch_shapes=[
            vm((SPAN, INNER), F32), vm((SPAN, STATE), F32), vm((SPAN, STATE), F32), row,
            vm((64, MODEL), F32), dma((8,)), dma((8,)),
        ],
        compiler_params=pltpu.CompilerParams(vmem_limit_bytes=60 * 1024 * 1024),
        name="output",
    )(*made)
    return gv[None], gk[None], gq[None], gs[None], decay.reshape(HEADS), skip.reshape(HEADS), gw


def solution(mesh):
    by_time = P("rec", "tm", None)
    by_head = P("rec", None, "tm")
    return jax.shard_map(
        local,
        mesh=mesh,
        in_specs=(by_time, by_time, by_time, by_head, P(), P(), P(), by_time),
        out_specs=(by_time, by_time, by_time, by_head, P(), P(), P("tm", None)),
        check_vma=False,
    )
```

```python
import jax
import jax.numpy as jnp
from jax import lax
from jax.experimental import pallas as pl
from jax.experimental.pallas import tpu as pltpu
from jax.sharding import PartitionSpec as P

HEADS = 32
WIDTH = 64
PAIR = 2 * WIDTH
STATE = 128
SPAN = 256
INNER = HEADS * WIDTH
MODEL = 1024
CHIPS = 16
LOG2E = 1.4426950408889634
MESH = pl.DeviceIdType.MESH
HIGHEST = lax.Precision.HIGHEST
F32 = jnp.float32
BF16 = jnp.bfloat16


def nn(a, b, precision=None):
    return lax.dot_general(
        a, b, (((1,), (0,)), ((), ())), precision=precision, preferred_element_type=F32
    )


def nt(a, b, precision=None):
    return lax.dot_general(
        a, b, (((1,), (1,)), ((), ())), precision=precision, preferred_element_type=F32
    )


def column(row):
    i = lax.broadcasted_iota(jnp.int32, (HEADS, HEADS), 0)
    j = lax.broadcasted_iota(jnp.int32, (HEADS, HEADS), 1)
    whole = jnp.broadcast_to(row, (HEADS, HEADS))
    return jnp.sum(jnp.where(i == j, whole, 0.0), axis=1, keepdims=True)


def running_sums(dt, rate):
    s = lax.broadcasted_iota(jnp.int32, (SPAN, SPAN), 0)
    t = lax.broadcasted_iota(jnp.int32, (SPAN, SPAN), 1)
    upto = jnp.where(s <= t, 1.0, 0.0).astype(F32)
    return nn(-rate * dt, upto, HIGHEST)


def two_rows(ref, k):
    top = jnp.broadcast_to(ref[pl.ds(2 * k, 1), :], (WIDTH, ref.shape[1]))
    low = jnp.broadcast_to(ref[pl.ds(2 * k + 1, 1), :], (WIDTH, ref.shape[1]))
    return jnp.concatenate([top, low], axis=0)


def split(v):
    high = v.astype(BF16)
    return high, (v - high.astype(F32)).astype(BF16)


PARTS = ((640, "xyz"), (768, "yzx"), (640, "zxy"))
HALF = SPAN // 2


def tile(v):
    return v.reshape(8, 8, STATE)


def mixer_kernel(
    x_hbm, k_hbm, q_hbm, dt_hbm, dl_hbm, sk_hbm, w_hbm, og_hbm,
    gv_hbm, gk_ref, gq_ref, gs_ref, smo_ref, gw_ref,
    x_ref, k_ref, q_ref, dt_ref, dl_ref, sk_ref, w_ref, og_ref,
    run2, crow, wrow, erow, skrow, frow, rrow, urow, xrow, vrow,
    gbuf, xt_ref, gt_ref, t_ref, e_ref, d_ref, tp, ep, dp,
    upf, gotf, backf, homef, upb, gotb, backb, homeb,
    s_ref, ds_ref, give_s, give_d,
    scores, acc, qacc, kacc, ysum, yp, dxt, gv_ref,
    f_og, r_og, f_q, r_q, r_e, rhs, dw0, dw1, dw2,
    a0, a1, a2, b0, b1, b2, ra0, ra1, ra2, rb0, rb1, rb2, rc0, rc1, rc2, w0, w1, w2, q0, q1, q2,
    s_core, s_x, s_y, s_z,
    in_sem, out_sem, core_send, core_recv, plane_send, plane_recv,
    first_send, first_recv, send, recv,
):
    y, me = lax.axis_index("rec"), lax.axis_index("tm")
    c, g = lax.rem(me, 2), lax.div(me, 2)
    x, z = lax.div(g, 4), lax.rem(g, 4)
    partner = me + 1 - 2 * c
    coord = {"x": x, "y": y, "z": z}
    own = c == 0

    loads = [
        pltpu.make_async_copy(src, dst, in_sem.at[n])
        for n, (src, dst) in enumerate((
            (dt_hbm, dt_ref), (dl_hbm, dl_ref), (x_hbm, x_ref), (k_hbm, k_ref),
            (q_hbm, q_ref), (og_hbm, og_ref), (w_hbm, w_ref), (sk_hbm, sk_ref),
        ))
    ]
    for n in loads:
        n.start()

    def device(axis, value):
        if axis == "x":
            return (y, (value * 4 + z) * 2 + c)
        if axis == "z":
            return (y, (x * 4 + value) * 2 + c)
        return (value, me)

    def other(axis, d):
        return lax.rem(coord[axis] + d, 4)

    def peer(d):
        return lax.rem(g + d, CHIPS)

    barrier = pltpu.get_barrier_semaphore()
    pl.semaphore_signal(barrier, inc=1, device_id=(y, partner), device_id_type=MESH)
    for d in range(1, CHIPS):
        pl.semaphore_signal(barrier, inc=1, device_id=(y, peer(d) * 2 + c), device_id_type=MESH)
    for d in range(1, 4):
        pl.semaphore_signal(barrier, inc=1, device_id=device("y", other("y", d)), device_id_type=MESH)

    def core_copy(src, dst, n):
        return pltpu.make_async_remote_copy(
            src_ref=src, dst_ref=dst, send_sem=core_send.at[n], recv_sem=core_recv.at[n],
            device_id=(y, partner), device_id_type=MESH,
        )

    def both(a, b):
        return jnp.where(own, a, b), jnp.where(own, b, a)

    def start(copies):
        for n in copies:
            n.start()
        return copies

    def wait(copies):
        for n in copies:
            n.wait()

    def spread(src, dst, n):
        return [
            pltpu.make_async_remote_copy(
                src_ref=src.at[peer(d)], dst_ref=dst.at[g],
                send_sem=plane_send.at[n, d], recv_sem=plane_recv.at[n, d],
                device_id=(y, peer(d) * 2 + c), device_id_type=MESH,
            )
            for d in range(1, CHIPS)
        ]

    loads[0].wait()
    loads[1].wait()
    dt = dt_ref[...]
    rate = jnp.exp(column(dl_ref[...]))
    run = running_sums(dt, rate)
    end = run[:, SPAN - 1 :]
    wrow[...] = jnp.exp(end - run) * dt
    erow[...] = jnp.exp(run)
    run2[...] = run * LOG2E
    crow[...] = run * LOG2E - jnp.log2(dt)
    vrow[...] = jnp.broadcast_to(jnp.exp(end), (HEADS, STATE))
    for h in range(HEADS):
        d_ref[h // 2, h % 2] = jnp.broadcast_to(vrow[h : h + 1, :], (8, STATE))

    loads[2].wait()
    loads[3].wait()

    def local_state(i, carry):
        at = pl.ds(pl.multiple_of(i * PAIR, PAIR), PAIR)
        xt = x_ref[:, at].T
        xt_ref[at, :] = xt
        high, low = split(xt.astype(F32) * two_rows(wrow, i))
        t_ref[i] = (nn(high, k_ref[...]) + nn(low, k_ref[...])).reshape(2, 8, 8, STATE)
        return carry

    lax.fori_loop(0, CHIPS, local_state, 0)
    pl.semaphore_wait(barrier, CHIPS + 3)
    wait(start([core_copy(d_ref, dp, 0), core_copy(t_ref.at[:, 1 - c], tp, 1)]))

    def combine_forward(i, carry):
        d0, d1 = both(d_ref[i, c], dp[i, c])
        t0, t1 = both(t_ref[i, c], tp[i])
        upf[i, 0:8] = d1[None] * t0 + t1
        upf[i, 8] = d0 * d1
        return carry

    lax.fori_loop(0, CHIPS, combine_forward, 0)

    forward_out = start(spread(upf, gotf, 0))
    gotf[g] = upf[g]

    wait(loads[4:])
    f_og[...] = og_ref[...].astype(F32)
    f_q[...] = q_ref[...].astype(F32)
    early = start([core_copy(f_og, r_og, 3), core_copy(f_q, r_q, 4), core_copy(erow, r_e, 5)])

    def cotangent(m, carry):
        rows = pl.ds(pl.multiple_of(m * 512, 512), 512)
        gbuf[...] = nt(w_ref[rows, :], og_ref[...])
        for n in range(4):
            i = m * 4 + n
            at = pl.ds(pl.multiple_of(i * PAIR, PAIR), PAIR)
            gm = gbuf[n * PAIR : (n + 1) * PAIR, :]
            gt_ref[at, :] = gm
            high, low = split(gm * two_rows(erow, i))
            e_ref[i] = (nn(high, q_ref[...]) + nn(low, q_ref[...])).reshape(2, 8, 8, STATE)
        return carry

    lax.fori_loop(0, 4, cotangent, 0)
    swap_e = start([core_copy(e_ref.at[:, 1 - c], ep, 2)])

    skrow[...] = jnp.broadcast_to(column(sk_ref[...]), (HEADS, SPAN))
    jj = lax.broadcasted_iota(jnp.int32, (SPAN, SPAN), 0)
    ii = lax.broadcasted_iota(jnp.int32, (SPAN, SPAN), 1)
    causal = jj <= ii
    scores[...] = jnp.where(causal, nt(k_ref[...], q_ref[...]), 0.0)
    acc[...] = jnp.zeros_like(acc)
    qacc[...] = jnp.zeros_like(qacc)
    kacc[...] = jnp.zeros_like(kacc)

    def row_sums(ref, value, i):
        for e in range(2):
            ref[pl.ds(2 * i + e, 1), :] = jnp.sum(
                value[e * WIDTH : (e + 1) * WIDTH], axis=0, keepdims=True
            )

    def inside(i, carry):
        at = pl.ds(pl.multiple_of(i * PAIR, PAIR), PAIR)
        xp = x_ref[:, at]
        xt = xt_ref[at, :]
        gf = gt_ref[at, :]
        gh, gl = split(gf)
        x2 = jnp.concatenate([xp, xp], axis=1)
        y_parts, yl_parts, dx_parts = [], [], []
        for e in range(2):
            row = run2[pl.ds(2 * i + e, 1), :]
            ccol = jnp.broadcast_to(crow[pl.ds(2 * i + e, 1), :], (HALF, SPAN)).T
            d00 = jnp.exp2(jnp.minimum(row[:, :HALF] - ccol[:HALF], 2.0))
            d01 = jnp.exp2(row[:, HALF:] - ccol[:HALF])
            d11 = jnp.exp2(jnp.minimum(row[:, HALF:] - ccol[HALF:], 2.0))
            n00, l00 = split(d00 * scores[:HALF, :HALF])
            n01, l01 = split(d01 * scores[:HALF, HALF:])
            n11, l11 = split(d11 * scores[HALF:, HALF:])
            n10 = jnp.zeros((HALF, HALF), BF16)

            def square(a, b, d):
                top = jnp.concatenate([a, b], axis=1)
                return jnp.concatenate([top, jnp.concatenate([n10, d], axis=1)], axis=0)

            n = square(n00, n01, n11)
            part = slice(e * WIDTH, (e + 1) * WIDTH)
            y_parts.append(nn(xt[part], n))
            yl_parts.append(nn(xt[part], square(l00, l01, l11)))
            dx = nt(jnp.concatenate([gh[part], gl[part]], axis=0), n)
            dx_parts.append(dx[:WIDTH] + dx[WIDTH:])
            blank = jnp.zeros((WIDTH, SPAN), BF16)
            if e == 0:
                gz = jnp.concatenate([gh[part], blank, gl[part], blank], axis=0)
            else:
                gz = jnp.concatenate([blank, gh[part], blank, gl[part]], axis=0)
            dn = nn(x2, gz)
            acc[:HALF, :HALF] += dn[:HALF, :HALF] * d00
            acc[:HALF, HALF:] += dn[:HALF, HALF:] * d01
            acc[HALF:, HALF:] += dn[HALF:, HALF:] * d11
        xf = xt.astype(F32)
        yy = jnp.concatenate(y_parts, axis=0)
        dx = jnp.concatenate(dx_parts, axis=0)
        whole = yy + jnp.concatenate(yl_parts, axis=0) + two_rows(skrow, i) * xf
        ysum[i] = whole.reshape(2, WIDTH, SPAN)
        dxt[at, :] = dx
        row_sums(frow, gf * yy, i)
        row_sums(rrow, xf * dx, i)
        row_sums(xrow, gf * xf, i)
        return carry

    lax.fori_loop(0, 3, inside, 0)
    wait(swap_e)

    def combine_backward(i, carry):
        d0, d1 = both(d_ref[i, c], dp[i, c])
        e0, e1 = both(e_ref[i, c], ep[i])
        upb[i, 0:8] = e0 + d0[None] * e1
        upb[i, 8] = d0 * d1
        return carry

    lax.fori_loop(0, CHIPS, combine_backward, 0)
    backward_out = start(spread(upb, gotb, 2))
    gotb[g] = upb[g]
    lax.fori_loop(3, 6, inside, 0)
    wait(forward_out)
    carried = jnp.zeros((8, 8, STATE), F32)
    for i in range(CHIPS):
        backf[i] = carried
        carried = gotf[i, 8][None] * carried + gotf[i, 0:8]
    forward_in = start(spread(backf, homef, 1))
    homef[g] = backf[g]
    lax.fori_loop(6, CHIPS, inside, 0)
    wait(early)
    swap_y = start([core_copy(ysum.at[:, 1 - c], yp, 6)])
    rhs[:SPAN] = og_ref[...]
    rhs[SPAN:] = r_og[...].astype(BF16)
    s_mine, s_other = q_ref[...], r_q[...].astype(BF16)
    wait(backward_out)
    carried = jnp.zeros((8, 8, STATE), F32)
    for i in range(CHIPS - 1, -1, -1):
        backb[i] = carried
        carried = gotb[i, 8][None] * carried + gotb[i, 0:8]
    backward_in = start(spread(backb, homeb, 3))
    homeb[g] = backb[g]
    wait(swap_y)
    wait(forward_in)

    recv_a, recv_b, recv_c = (ra0, ra1, ra2), (rb0, rb1, rb2), (rc0, rc1, rc2)
    first, used = ([], [], []), []
    low, high = pl.ds(0, 2), pl.ds(2, 2)

    def first_copy(axis, d, src, dst):
        n = len(used)
        used.append(n)
        return pltpu.make_async_remote_copy(
            src_ref=src, dst_ref=dst, send_sem=first_send.at[n], recv_sem=first_recv.at[n],
            device_id=device(axis, other(axis, d)), device_id_type=MESH,
        )

    def send_far(axis, piece, relay):
        return start([first_copy(axis, 1, piece.at[low], relay.at[0]), first_copy(axis, 3, piece.at[high], relay.at[1])])

    def send_sums(axis, far, up, down, relay, got0, got1):
        wait(far)
        relay[0] = relay[0] + up[:2]
        relay[1] = relay[1] + down[2:]
        return start([first_copy(axis, 1, relay.at[0], got0.at[low]), first_copy(axis, 3, relay.at[1], got1.at[high])])

    def across(states, queries):
        high, low = split(states)
        return nt(high, queries) + nt(low, queries)

    fars = []
    for turn in (2, 1, 3, 0):
        m = other("x", turn)
        own_states, other_states, own_rows, other_rows, own_y, other_y = [], [], [], [], [], []
        for n in range(4):
            i = m * 4 + n
            d0, _ = both(d_ref[i, c], dp[i, c])
            t0, _ = both(t_ref[i, c], tp[i])
            s0 = homef[i]
            s1 = d0[None] * s0 + t0
            mine, theirs = both(s0, s1)
            s_ref[i, c] = mine
            give_s[i] = theirs
            own_states.append(mine.reshape(WIDTH, STATE))
            other_states.append(theirs.reshape(WIDTH, STATE))
            own_rows.append(jnp.broadcast_to(erow[pl.ds(2 * i + c, 1), :], (WIDTH, SPAN)))
            other_rows.append(jnp.broadcast_to(r_e[pl.ds(2 * i + c, 1), :], (WIDTH, SPAN)))
            own_y.append(ysum[i, c])
            other_y.append(yp[i])

        def join(parts):
            return jnp.concatenate(parts, axis=0)

        left = join(own_y) + across(join(own_states), s_mine) * join(own_rows)
        right = join(other_y) + across(join(other_states), s_other) * join(other_rows)
        lhs = jnp.concatenate([left.astype(BF16), right.astype(BF16)], axis=1)
        whole = nn(lhs, rhs[...]).reshape(4, 4, 2, 8, MODEL)
        dw0[m] = whole[:, :, 0, :, :640]
        dw2[m] = whole[:, :, 1, :, 384:]
        for n in range(4):
            dw1[m, n, :, :, :384] = whole[:, n, 0, :, 640:]
            dw1[m, n, :, :, 384:] = whole[:, n, 1, :, :384]
        if turn == 2:
            far_x = send_far("x", dw0.at[m], q0)
        elif turn == 1:
            first[0].extend(start([first_copy("x", 1, dw0.at[m, high], ra0.at[0, high])]))
        elif turn == 3:
            first[0].extend(start([first_copy("x", 3, dw0.at[m, low], ra0.at[1, low])]))
        pairs = []
        for p, axis, dw, ra, q in ((1, "y", dw1, ra1, q1), (2, "z", dw2, ra2, q2)):
            pairs.append(send_far(axis, dw.at[m, other(axis, 2)], q.at[m]))
            first[p].extend(start([
                first_copy(axis, 1, dw.at[m, other(axis, 1), high], ra.at[0, m, high]),
                first_copy(axis, 3, dw.at[m, other(axis, 3), low], ra.at[1, m, low]),
            ]))
        fars.append((m, pairs))

    def relay_sums(step):
        m, pairs = fars[step]
        for far, (p, axis, dw, ra, q) in zip(pairs, ((1, "y", dw1, ra1, q1), (2, "z", dw2, ra2, q2))):
            up, down = dw[m, other(axis, 1)], dw[m, other(axis, 3)]
            first[p].extend(send_sums(axis, far, up, down, q.at[m], ra.at[0, m], ra.at[1, m]))

    swap_s = start([core_copy(give_s, s_ref.at[:, c], 7)])
    relay_sums(0)
    first[0].extend(send_sums("x", far_x, dw0[other("x", 1)], dw0[other("x", 3)], q0, ra0.at[0], ra0.at[1]))
    wait(backward_in)

    def finish_backward(i, carry):
        d0, d1 = both(d_ref[i, c], dp[i, c])
        e0, e1 = both(e_ref[i, c], ep[i])
        b1 = homeb[i]
        b0 = d1[None] * b1 + e1
        ds_ref[i, c], give_d[i] = both(b0, b1)
        return carry

    lax.fori_loop(0, CHIPS, finish_backward, 0)
    swap_d = start([core_copy(give_d, ds_ref.at[:, c], 8)])
    relay_sums(1)
    wait(swap_s)
    wait(swap_d)

    def outside(i, carry):
        at = pl.ds(pl.multiple_of(i * PAIR, PAIR), PAIR)
        xf = xt_ref[at, :].astype(F32)
        gf = gt_ref[at, :]
        wp = two_rows(wrow, i)
        ep2 = two_rows(erow, i)
        sp = s_ref[i].reshape(PAIR, STATE)
        dsp = ds_ref[i].reshape(PAIR, STATE)
        sh, sl = split(sp)
        dsh, dsl = split(dsp)
        yy = (nt(sh, q_ref[...]) + nt(sl, q_ref[...])) * ep2
        dxs = (nt(dsh, k_ref[...]) + nt(dsl, k_ref[...])) * wp
        gv_ref[:, at] = (dxt[at, :] + dxs + two_rows(skrow, i) * gf).T
        ge = (gf * ep2).astype(BF16)
        xw = (xf * wp).astype(BF16)
        qacc[...] += nn(sh.T, ge) + nn(sl.T, ge)
        kacc[...] += nn(dsh.T, xw) + nn(dsl.T, xw)
        fg, xd, sd = gf * yy, xf * dxs, sp * dsp
        for e in range(2):
            part = slice(e * WIDTH, (e + 1) * WIDTH)
            h = pl.ds(2 * i + e, 1)
            frow[h, :] += jnp.sum(fg[part], axis=0, keepdims=True)
            urow[h, :] = jnp.sum(xd[part], axis=0, keepdims=True)
            vrow[h, :] = jnp.sum(sd[part], axis=0, keepdims=True)
        return carry

    lax.fori_loop(0, 7, outside, 0)
    relay_sums(2)
    relay_sums(3)
    lax.fori_loop(7, CHIPS, outside, 0)
    store = pltpu.make_async_copy(gv_ref, gv_hbm, out_sem)
    store.start()
    dst = jnp.where(causal, acc[...], 0.0).astype(BF16)
    gk_ref[...] = nn(dst, q_ref[...]) + kacc[...].T
    gq_ref[...] = (nn(k_ref[...].T, dst) + qacc[...]).T
    upto = jnp.where(ii <= jj, 1.0, 0.0).astype(F32)
    decay = jnp.exp(run2[:, SPAN - 1 :] * (1.0 / LOG2E))
    dt = dt_ref[...]
    rate = jnp.exp(column(dl_ref[...]))
    tail = jnp.sum(urow[...], axis=1, keepdims=True)
    tail = tail + decay * jnp.sum(vrow[...], axis=1, keepdims=True)
    r = rrow[...] + urow[...]
    da = nn(frow[...] - r, upto, HIGHEST) + tail
    gs_ref[...] = r / dt - rate * da
    g_decay = jnp.sum(-rate * dt * da, axis=1, keepdims=True)
    g_skip = jnp.sum(xrow[...], axis=1, keepdims=True)
    lane = lax.broadcasted_iota(jnp.int32, (HEADS, 128), 1)
    s_core[c] = jnp.where(lane == 0, g_decay, jnp.where(lane == 1, g_skip, 0.0))
    wait(start([core_copy(s_core.at[c], s_core.at[c], 9)]))

    def reach(axis, d, src, dst, n):
        return pltpu.make_async_remote_copy(
            src_ref=src, dst_ref=dst, send_sem=send.at[n, d - 1], recv_sem=recv.at[n, d - 1],
            device_id=device(axis, other(axis, d)), device_id_type=MESH,
        )

    def small_start(axis, buf, value, n):
        buf[coord[axis]] = value
        mine = buf.at[coord[axis]]
        return start([reach(axis, d, mine, mine, n) for d in range(1, 4)])

    def small_sum(copies, buf):
        wait(copies)
        return (buf[0] + buf[1]) + (buf[2] + buf[3])

    def pick(dims, axis, value):
        return tuple(value if n == axis else slice(None) for n in dims)

    def reduce_start(src, dims, axis, dst, n):
        return start([
            reach(axis, d, src.at[pick(dims, axis, other(axis, d))], dst.at[d - 1], n) for d in range(1, 4)
        ])

    parts, sums_a, sums_b, rows = (dw0, dw1, dw2), (a0, a1, a2), (b0, b1, b2), (w0, w1, w2)
    layouts = ("xzy", "xyz", "xzy")
    small = small_start("x", s_x, s_core[0] + s_core[1], 9)
    second, third, last = [], [], []
    for p, (_, order) in enumerate(PARTS):
        wait(first[p])
        got = recv_a[p]
        mine = parts[p][pick(layouts[p], order[0], coord[order[0]])]
        sums_a[p][...] = mine + (got[0] + got[1])
        rest = layouts[p].replace(order[0], "")
        second.append(reduce_start(sums_a[p], rest, order[1], recv_b[p], p))
    small = small_start("y", s_y, small_sum(small, s_x), 10)
    for p, (_, order) in enumerate(PARTS):
        wait(second[p])
        rest = layouts[p].replace(order[0], "")
        got = recv_b[p]
        mine = sums_a[p][pick(rest, order[1], coord[order[1]])]
        sums_b[p][...] = (mine + got[0]) + (got[1] + got[2])
        third.append(reduce_start(sums_b[p], order[2], order[2], recv_c[p], 3 + p))
    small = small_start("z", s_z, small_sum(small, s_y), 11)
    for p, (_, order) in enumerate(PARTS):
        wait(third[p])
        got = recv_c[p]
        rows[p][y] = (sums_b[p][coord[order[2]]] + got[0]) + (got[1] + got[2])
        last.extend(start([reach("y", d, rows[p].at[y], rows[p].at[y], 6 + p) for d in range(1, 4)]))
    smo_ref[...] = small_sum(small, s_z)
    store.wait()
    wait(last)
    for n in range(4):
        gw_ref[16 * n : 16 * n + 8, :640] = w0[n]
        gw_ref[16 * n : 16 * n + 8, 640:] = w1[n, :, :384]
        gw_ref[16 * n + 8 : 16 * n + 16, :384] = w1[n, :, 384:]
        gw_ref[16 * n + 8 : 16 * n + 16, 384:] = w2[n]


def output_kernel(
    gv, gk, gq, gs, small, gw, gv_out, gk_out, gq_out, gs_out, decay_out, skip_out, gw_out,
    vv, vk, vq, vs, vm, vw, vd, vp, into, out,
):
    size = SPAN // 8
    parts = [pl.ds(n * size, size) for n in range(8)]
    moves = [(gv.at[n], vv.at[n], gv_out.at[n]) for n in parts]
    moves += [(gw, vw, gw_out), (gk, vk, gk_out), (gq, vq, gq_out), (gs, vs, gs_out)]
    first = pltpu.make_async_copy(small, vm, into.at[12])
    reads = [pltpu.make_async_copy(a, b, into.at[n]) for n, (a, b, _) in enumerate(moves)]
    writes = [pltpu.make_async_copy(b, a, out.at[n]) for n, (_, b, a) in enumerate(moves)]
    writes += [pltpu.make_async_copy(vd, decay_out, out.at[12]), pltpu.make_async_copy(vp, skip_out, out.at[13])]
    first.start()
    for n in reads:
        n.start()
    first.wait()
    i = lax.broadcasted_iota(jnp.int32, (HEADS, HEADS), 0)
    j = lax.broadcasted_iota(jnp.int32, (HEADS, HEADS), 1)
    for n, ref in enumerate((vd, vp)):
        whole = jnp.broadcast_to(vm[:, n : n + 1], (HEADS, HEADS))
        ref[...] = jnp.sum(jnp.where(i == j, whole, 0.0), axis=0, keepdims=True)
        writes[12 + n].start()
    for a, b in zip(reads, writes):
        a.wait()
        b.start()
    for n in writes:
        n.wait()


def sds(shape, dtype=F32):
    return jax.ShapeDtypeStruct(shape, dtype)


def local(token_values, write_keys, read_queries, step_sizes, decay_log, skip_gain, out_weight, out_grad):
    x, k, q, dt, og = token_values[0], write_keys[0], read_queries[0], step_sizes[0], out_grad[0]
    dl, sk = decay_log.reshape(1, HEADS), skip_gain.reshape(1, HEADS)
    vm, dma = pltpu.VMEM, pltpu.SemaphoreType.DMA
    anywhere = pl.BlockSpec(memory_space=pl.ANY)
    inside = pl.BlockSpec(memory_space=pltpu.VMEM)
    row = vm((HEADS, SPAN), F32)
    heads = vm((CHIPS, 8, 8, STATE), F32)
    packed = vm((CHIPS, 9, 8, STATE), F32)
    pairs = vm((CHIPS, 2, 8, 8, STATE), F32)
    wides = [w for w, _ in PARTS]
    made = pl.pallas_call(
        mixer_kernel,
        out_shape=(
            sds((SPAN, INNER)), sds((SPAN, STATE)), sds((SPAN, STATE)), sds((HEADS, SPAN)),
            sds((HEADS, 128)), sds((64, MODEL)),
        ),
        in_specs=[anywhere] * 8,
        out_specs=(anywhere,) + (inside,) * 5,
        scratch_shapes=[
            vm((SPAN, INNER), BF16), vm((SPAN, STATE), BF16), vm((SPAN, STATE), BF16), row,
            vm((1, HEADS), F32), vm((1, HEADS), F32), vm((INNER, MODEL), BF16), vm((SPAN, MODEL), BF16),
            row, row, row, row, row, row, row, row, row, vm((HEADS, STATE), F32),
            vm((512, SPAN), F32), vm((INNER, SPAN), BF16), vm((INNER, SPAN), F32),
            pairs, pairs, vm((CHIPS, 2, 8, STATE), F32), heads, heads, vm((CHIPS, 2, 8, STATE), F32),
            packed, packed, heads, heads, packed, packed, heads, heads,
            pairs, pairs, heads, heads,
            vm((SPAN, SPAN), F32), vm((SPAN, SPAN), F32), vm((STATE, SPAN), F32), vm((STATE, SPAN), F32),
            vm((CHIPS, 2, WIDTH, SPAN), F32), vm((CHIPS, WIDTH, SPAN), F32),
            vm((INNER, SPAN), F32), vm((SPAN, INNER), F32),
            vm((SPAN, MODEL), F32), vm((SPAN, MODEL), F32), vm((SPAN, STATE), F32), vm((SPAN, STATE), F32),
            row, vm((2 * SPAN, MODEL), BF16), *[vm((4, 4, 4, 8, w), F32) for w in wides],
            *[vm((4, 4, 8, w), F32) for w in wides],
            *[vm((4, 8, w), F32) for w in wides],
            *[vm((2, 4, 4, 8, w), F32) for w in wides],
            *[vm((3, 4, 8, w), F32) for w in wides],
            *[vm((3, 8, w), F32) for w in wides],
            *[vm((4, 8, w), F32) for w in wides],
            vm((2, 2, 4, 8, wides[0]), F32), vm((4, 2, 2, 8, wides[1]), F32), vm((4, 2, 2, 8, wides[2]), F32),
            vm((2, HEADS, 128), F32),
            *[vm((4, HEADS, 128), F32)] * 3,
            dma((8,)), dma, dma((10,)), dma((10,)), dma((4, CHIPS)), dma((4, CHIPS)),
            dma((54,)), dma((54,)), dma((12, 3)), dma((12, 3)),
        ],
        compiler_params=pltpu.CompilerParams(
            vmem_limit_bytes=60 * 1024 * 1024, collective_id=0, has_side_effects=True
        ),
        name="mixer",
    )(x, k, q, dt, dl, sk, out_weight, og)
    gv, gk, gq, gs, decay, skip, gw = pl.pallas_call(
        output_kernel,
        out_shape=(
            sds((SPAN, INNER)), sds((SPAN, STATE)), sds((SPAN, STATE)), sds((HEADS, SPAN)),
            sds((1, HEADS)), sds((1, HEADS)), sds((64, MODEL)),
        ),
        in_specs=[anywhere] * 6,
        out_specs=(anywhere,) * 7,
        scratch_shapes=[
            vm((SPAN, INNER), F32), vm((SPAN, STATE), F32), vm((SPAN, STATE), F32), row,
            vm((HEADS, 128), F32), vm((64, MODEL), F32), vm((1, HEADS), F32), vm((1, HEADS), F32),
            dma((13,)), dma((14,)),
        ],
        compiler_params=pltpu.CompilerParams(vmem_limit_bytes=60 * 1024 * 1024),
        name="output",
    )(*made)
    return gv[None], gk[None], gq[None], gs[None], decay.reshape(HEADS), skip.reshape(HEADS), gw


def solution(mesh):
    by_time = P("rec", "tm", None)
    by_head = P("rec", None, "tm")
    return jax.shard_map(
        local,
        mesh=mesh,
        in_specs=(by_time, by_time, by_time, by_head, P(), P(), P(), by_time),
        out_specs=(by_time, by_time, by_time, by_head, P(), P(), P("tm", None)),
        check_vma=False,
    )
```

```python
import jax
import jax.numpy as jnp
from jax import lax
from jax.experimental import pallas as pl
from jax.experimental.pallas import tpu as pltpu
from jax.sharding import PartitionSpec as P

HEADS = 32
WIDTH = 64
PAIR = 2 * WIDTH
STATE = 128
SPAN = 256
INNER = HEADS * WIDTH
MODEL = 1024
CHIPS = 16
LOG2E = 1.4426950408889634
MESH = pl.DeviceIdType.MESH
HIGHEST = lax.Precision.HIGHEST
F32 = jnp.float32
BF16 = jnp.bfloat16


def nn(a, b, precision=None):
    return lax.dot_general(
        a, b, (((1,), (0,)), ((), ())), precision=precision, preferred_element_type=F32
    )


def nt(a, b, precision=None):
    return lax.dot_general(
        a, b, (((1,), (1,)), ((), ())), precision=precision, preferred_element_type=F32
    )


def column(row):
    i = lax.broadcasted_iota(jnp.int32, (HEADS, HEADS), 0)
    j = lax.broadcasted_iota(jnp.int32, (HEADS, HEADS), 1)
    whole = jnp.broadcast_to(row, (HEADS, HEADS))
    return jnp.sum(jnp.where(i == j, whole, 0.0), axis=1, keepdims=True)


def running_sums(dt, rate):
    s = lax.broadcasted_iota(jnp.int32, (SPAN, SPAN), 0)
    t = lax.broadcasted_iota(jnp.int32, (SPAN, SPAN), 1)
    upto = jnp.where(s <= t, 1.0, 0.0).astype(F32)
    return nn(-rate * dt, upto, HIGHEST)


def two_rows(ref, k):
    top = jnp.broadcast_to(ref[pl.ds(2 * k, 1), :], (WIDTH, ref.shape[1]))
    low = jnp.broadcast_to(ref[pl.ds(2 * k + 1, 1), :], (WIDTH, ref.shape[1]))
    return jnp.concatenate([top, low], axis=0)


def split(v):
    high = v.astype(BF16)
    return high, (v - high.astype(F32)).astype(BF16)


PARTS = ((768, "xyz"), (640, "yzx"), (640, "zxy"))
HALF = SPAN // 2


def tile(v):
    return v.reshape(8, 8, STATE)


def mixer_kernel(
    x_hbm, k_hbm, q_hbm, dt_hbm, dl_hbm, sk_hbm, w_hbm, og_hbm,
    gv_hbm, gk_ref, gq_ref, gs_ref, smo_ref, gw_ref,
    x_ref, k_ref, q_ref, dt_ref, dl_ref, sk_ref, w_ref, og_ref,
    run2, crow, wrow, erow, skrow, frow, rrow, urow, xrow, vrow,
    gbuf, xt_ref, gt_ref, t_ref, e_ref, d_ref, tp, ep, dp,
    upf, gotf, backf, homef, upb, gotb, backb, homeb,
    s_ref, ds_ref, give_s, give_d,
    scores, acc, qacc, kacc, ysum, yp, dxt, gv_ref,
    f_og, r_og, f_q, r_q, r_e, rhs, dw0, dw1, dw2,
    a0, a1, a2, b0, b1, b2, ra0, ra1, ra2, rb0, rb1, rb2, rc0, rc1, rc2, w0, w1, w2, q0, q1, q2,
    s_core, s_x, s_y, s_z,
    in_sem, out_sem, core_send, core_recv, plane_send, plane_recv,
    first_send, first_recv, send, recv,
):
    y, me = lax.axis_index("rec"), lax.axis_index("tm")
    c, g = lax.rem(me, 2), lax.div(me, 2)
    x, z = lax.div(g, 4), lax.rem(g, 4)
    partner = me + 1 - 2 * c
    coord = {"x": x, "y": y, "z": z}
    own = c == 0

    loads = [
        pltpu.make_async_copy(src, dst, in_sem.at[n])
        for n, (src, dst) in enumerate((
            (dt_hbm, dt_ref), (dl_hbm, dl_ref), (x_hbm, x_ref), (k_hbm, k_ref),
            (q_hbm, q_ref), (og_hbm, og_ref), (w_hbm, w_ref), (sk_hbm, sk_ref),
        ))
    ]
    for n in loads:
        n.start()

    def device(axis, value):
        if axis == "x":
            return (y, (value * 4 + z) * 2 + c)
        if axis == "z":
            return (y, (x * 4 + value) * 2 + c)
        return (value, me)

    def other(axis, d):
        return lax.rem(coord[axis] + d, 4)

    def peer(d):
        return lax.rem(g + d, CHIPS)

    barrier = pltpu.get_barrier_semaphore()
    pl.semaphore_signal(barrier, inc=1, device_id=(y, partner), device_id_type=MESH)
    for d in range(1, CHIPS):
        pl.semaphore_signal(barrier, inc=1, device_id=(y, peer(d) * 2 + c), device_id_type=MESH)
    for d in range(1, 4):
        pl.semaphore_signal(barrier, inc=1, device_id=device("y", other("y", d)), device_id_type=MESH)

    def core_copy(src, dst, n):
        return pltpu.make_async_remote_copy(
            src_ref=src, dst_ref=dst, send_sem=core_send.at[n], recv_sem=core_recv.at[n],
            device_id=(y, partner), device_id_type=MESH,
        )

    def both(a, b):
        return jnp.where(own, a, b), jnp.where(own, b, a)

    def start(copies):
        for n in copies:
            n.start()
        return copies

    def wait(copies):
        for n in copies:
            n.wait()

    def spread(src, dst, n):
        return [
            pltpu.make_async_remote_copy(
                src_ref=src.at[peer(d)], dst_ref=dst.at[g],
                send_sem=plane_send.at[n, d], recv_sem=plane_recv.at[n, d],
                device_id=(y, peer(d) * 2 + c), device_id_type=MESH,
            )
            for d in range(1, CHIPS)
        ]

    loads[0].wait()
    loads[1].wait()
    dt = dt_ref[...]
    rate = jnp.exp(column(dl_ref[...]))
    run = running_sums(dt, rate)
    end = run[:, SPAN - 1 :]
    wrow[...] = jnp.exp(end - run) * dt
    erow[...] = jnp.exp(run)
    run2[...] = run * LOG2E
    crow[...] = run * LOG2E - jnp.log2(dt)
    vrow[...] = jnp.broadcast_to(jnp.exp(end), (HEADS, STATE))
    for h in range(HEADS):
        d_ref[h // 2, h % 2] = jnp.broadcast_to(vrow[h : h + 1, :], (8, STATE))

    loads[2].wait()
    loads[3].wait()

    def local_state(i, carry):
        at = pl.ds(pl.multiple_of(i * PAIR, PAIR), PAIR)
        xt = x_ref[:, at].T
        xt_ref[at, :] = xt
        high, low = split(xt.astype(F32) * two_rows(wrow, i))
        t_ref[i] = (nn(high, k_ref[...]) + nn(low, k_ref[...])).reshape(2, 8, 8, STATE)
        return carry

    lax.fori_loop(0, CHIPS, local_state, 0)
    pl.semaphore_wait(barrier, CHIPS + 3)
    wait(start([core_copy(d_ref, dp, 0), core_copy(t_ref.at[:, 1 - c], tp, 1)]))

    def combine_forward(i, carry):
        d0, d1 = both(d_ref[i, c], dp[i, c])
        t0, t1 = both(t_ref[i, c], tp[i])
        upf[i, 0:8] = d1[None] * t0 + t1
        upf[i, 8] = d0 * d1
        return carry

    lax.fori_loop(0, CHIPS, combine_forward, 0)

    forward_out = start(spread(upf, gotf, 0))
    gotf[g] = upf[g]

    wait(loads[4:])
    f_og[...] = og_ref[...].astype(F32)
    f_q[...] = q_ref[...].astype(F32)
    early = start([core_copy(f_og, r_og, 3), core_copy(f_q, r_q, 4), core_copy(erow, r_e, 5)])

    def cotangent(m, carry):
        rows = pl.ds(pl.multiple_of(m * 512, 512), 512)
        gbuf[...] = nt(w_ref[rows, :], og_ref[...])
        for n in range(4):
            i = m * 4 + n
            at = pl.ds(pl.multiple_of(i * PAIR, PAIR), PAIR)
            gm = gbuf[n * PAIR : (n + 1) * PAIR, :]
            gt_ref[at, :] = gm
            high, low = split(gm * two_rows(erow, i))
            e_ref[i] = (nn(high, q_ref[...]) + nn(low, q_ref[...])).reshape(2, 8, 8, STATE)
        return carry

    lax.fori_loop(0, 4, cotangent, 0)
    swap_e = start([core_copy(e_ref.at[:, 1 - c], ep, 2)])

    skrow[...] = jnp.broadcast_to(column(sk_ref[...]), (HEADS, SPAN))
    jj = lax.broadcasted_iota(jnp.int32, (SPAN, SPAN), 0)
    ii = lax.broadcasted_iota(jnp.int32, (SPAN, SPAN), 1)
    causal = jj <= ii
    scores[...] = jnp.where(causal, nt(k_ref[...], q_ref[...]), 0.0)
    acc[...] = jnp.zeros_like(acc)
    qacc[...] = jnp.zeros_like(qacc)
    kacc[...] = jnp.zeros_like(kacc)

    def row_sums(ref, value, i):
        for e in range(2):
            ref[pl.ds(2 * i + e, 1), :] = jnp.sum(
                value[e * WIDTH : (e + 1) * WIDTH], axis=0, keepdims=True
            )

    def inside(i, carry):
        at = pl.ds(pl.multiple_of(i * PAIR, PAIR), PAIR)
        xp = x_ref[:, at]
        xt = xt_ref[at, :]
        gf = gt_ref[at, :]
        gh, gl = split(gf)
        x2 = jnp.concatenate([xp, xp], axis=1)
        y_parts, yl_parts, dx_parts = [], [], []
        for e in range(2):
            row = run2[pl.ds(2 * i + e, 1), :]
            ccol = jnp.broadcast_to(crow[pl.ds(2 * i + e, 1), :], (HALF, SPAN)).T
            d00 = jnp.exp2(jnp.minimum(row[:, :HALF] - ccol[:HALF], 2.0))
            d01 = jnp.exp2(row[:, HALF:] - ccol[:HALF])
            d11 = jnp.exp2(jnp.minimum(row[:, HALF:] - ccol[HALF:], 2.0))
            n00, l00 = split(d00 * scores[:HALF, :HALF])
            n01, l01 = split(d01 * scores[:HALF, HALF:])
            n11, l11 = split(d11 * scores[HALF:, HALF:])
            n10 = jnp.zeros((HALF, HALF), BF16)

            def square(a, b, d):
                top = jnp.concatenate([a, b], axis=1)
                return jnp.concatenate([top, jnp.concatenate([n10, d], axis=1)], axis=0)

            n = square(n00, n01, n11)
            part = slice(e * WIDTH, (e + 1) * WIDTH)
            y_parts.append(nn(xt[part], n))
            yl_parts.append(nn(xt[part], square(l00, l01, l11)))
            dx = nt(jnp.concatenate([gh[part], gl[part]], axis=0), n)
            dx_parts.append(dx[:WIDTH] + dx[WIDTH:])
            blank = jnp.zeros((WIDTH, SPAN), BF16)
            if e == 0:
                gz = jnp.concatenate([gh[part], blank, gl[part], blank], axis=0)
            else:
                gz = jnp.concatenate([blank, gh[part], blank, gl[part]], axis=0)
            dn = nn(x2, gz)
            acc[:HALF, :HALF] += dn[:HALF, :HALF] * d00
            acc[:HALF, HALF:] += dn[:HALF, HALF:] * d01
            acc[HALF:, HALF:] += dn[HALF:, HALF:] * d11
        xf = xt.astype(F32)
        yy = jnp.concatenate(y_parts, axis=0)
        dx = jnp.concatenate(dx_parts, axis=0)
        whole = yy + jnp.concatenate(yl_parts, axis=0) + two_rows(skrow, i) * xf
        ysum[i] = whole.reshape(2, WIDTH, SPAN)
        dxt[at, :] = dx
        row_sums(frow, gf * yy, i)
        row_sums(rrow, xf * dx, i)
        row_sums(xrow, gf * xf, i)
        return carry

    wait(swap_e)

    def combine_backward(i, carry):
        d0, d1 = both(d_ref[i, c], dp[i, c])
        e0, e1 = both(e_ref[i, c], ep[i])
        upb[i, 0:8] = e0 + d0[None] * e1
        upb[i, 8] = d0 * d1
        return carry

    lax.fori_loop(0, CHIPS, combine_backward, 0)
    backward_out = start(spread(upb, gotb, 2))
    gotb[g] = upb[g]
    wait(forward_out)
    carried = jnp.zeros((8, 8, STATE), F32)
    for i in range(CHIPS):
        backf[i] = carried
        carried = gotf[i, 8][None] * carried + gotf[i, 0:8]
    forward_in = start(spread(backf, homef, 1))
    homef[g] = backf[g]
    lax.fori_loop(0, CHIPS, inside, 0)
    wait(early)
    swap_y = start([core_copy(ysum.at[:, 1 - c], yp, 6)])
    rhs[:SPAN] = og_ref[...]
    rhs[SPAN:] = r_og[...].astype(BF16)
    s_mine, s_other = q_ref[...], r_q[...].astype(BF16)
    wait(backward_out)
    carried = jnp.zeros((8, 8, STATE), F32)
    for i in range(CHIPS - 1, -1, -1):
        backb[i] = carried
        carried = gotb[i, 8][None] * carried + gotb[i, 0:8]
    backward_in = start(spread(backb, homeb, 3))
    homeb[g] = backb[g]
    wait(swap_y)
    wait(forward_in)

    recv_a, recv_b, recv_c = (ra0, ra1, ra2), (rb0, rb1, rb2), (rc0, rc1, rc2)
    first, used = ([], [], []), []
    low, high = pl.ds(0, 2), pl.ds(2, 2)

    def first_copy(axis, d, src, dst):
        n = len(used)
        used.append(n)
        return pltpu.make_async_remote_copy(
            src_ref=src, dst_ref=dst, send_sem=first_send.at[n], recv_sem=first_recv.at[n],
            device_id=device(axis, other(axis, d)), device_id_type=MESH,
        )

    def send_far(axis, piece, relay):
        return start([first_copy(axis, 1, piece.at[low], relay.at[0]), first_copy(axis, 3, piece.at[high], relay.at[1])])

    def send_sums(axis, far, up, down, relay, got0, got1):
        wait(far)
        relay[0] = relay[0] + up[:2]
        relay[1] = relay[1] + down[2:]
        return start([first_copy(axis, 1, relay.at[0], got0.at[low]), first_copy(axis, 3, relay.at[1], got1.at[high])])

    def across(states, queries):
        high, low = split(states)
        return nt(high, queries) + nt(low, queries)

    fars = []
    for turn in (2, 1, 3, 0):
        m = other("x", turn)
        own_states, other_states, own_rows, other_rows, own_y, other_y = [], [], [], [], [], []
        for n in range(4):
            i = m * 4 + n
            d0, _ = both(d_ref[i, c], dp[i, c])
            t0, _ = both(t_ref[i, c], tp[i])
            s0 = homef[i]
            s1 = d0[None] * s0 + t0
            mine, theirs = both(s0, s1)
            s_ref[i, c] = mine
            give_s[i] = theirs
            own_states.append(mine.reshape(WIDTH, STATE))
            other_states.append(theirs.reshape(WIDTH, STATE))
            own_rows.append(jnp.broadcast_to(erow[pl.ds(2 * i + c, 1), :], (WIDTH, SPAN)))
            other_rows.append(jnp.broadcast_to(r_e[pl.ds(2 * i + c, 1), :], (WIDTH, SPAN)))
            own_y.append(ysum[i, c])
            other_y.append(yp[i])

        def join(parts):
            return jnp.concatenate(parts, axis=0)

        left = join(own_y) + across(join(own_states), s_mine) * join(own_rows)
        right = join(other_y) + across(join(other_states), s_other) * join(other_rows)
        lhs = jnp.concatenate([left.astype(BF16), right.astype(BF16)], axis=1)
        whole = nn(lhs, rhs[...]).reshape(4, 4, 2, 8, MODEL)
        dw0[m] = whole[:, :, 0, :, :768]
        dw2[m] = whole[:, :, 1, :, 384:]
        for n in range(4):
            dw1[m, n, :, :, :256] = whole[:, n, 0, :, 768:]
            dw1[m, n, :, :, 256:] = whole[:, n, 1, :, :384]
        if turn == 2:
            far_x = send_far("x", dw0.at[m], q0)
        elif turn == 1:
            first[0].extend(start([first_copy("x", 1, dw0.at[m, high], ra0.at[0, high])]))
        elif turn == 3:
            first[0].extend(start([first_copy("x", 3, dw0.at[m, low], ra0.at[1, low])]))
        pairs = []
        for p, axis, dw, ra, q in ((1, "y", dw1, ra1, q1), (2, "z", dw2, ra2, q2)):
            pairs.append(send_far(axis, dw.at[m, other(axis, 2)], q.at[m]))
            first[p].extend(start([
                first_copy(axis, 1, dw.at[m, other(axis, 1), high], ra.at[0, m, high]),
                first_copy(axis, 3, dw.at[m, other(axis, 3), low], ra.at[1, m, low]),
            ]))
        fars.append((m, pairs))

    def relay_sums(step):
        m, pairs = fars[step]
        for far, (p, axis, dw, ra, q) in zip(pairs, ((1, "y", dw1, ra1, q1), (2, "z", dw2, ra2, q2))):
            up, down = dw[m, other(axis, 1)], dw[m, other(axis, 3)]
            first[p].extend(send_sums(axis, far, up, down, q.at[m], ra.at[0, m], ra.at[1, m]))

    swap_s = start([core_copy(give_s, s_ref.at[:, c], 7)])
    relay_sums(0)
    first[0].extend(send_sums("x", far_x, dw0[other("x", 1)], dw0[other("x", 3)], q0, ra0.at[0], ra0.at[1]))
    relay_sums(1)
    relay_sums(2)
    relay_sums(3)
    wait(backward_in)

    def finish_backward(i, carry):
        d0, d1 = both(d_ref[i, c], dp[i, c])
        e0, e1 = both(e_ref[i, c], ep[i])
        b1 = homeb[i]
        b0 = d1[None] * b1 + e1
        ds_ref[i, c], give_d[i] = both(b0, b1)
        return carry

    lax.fori_loop(0, CHIPS, finish_backward, 0)
    swap_d = start([core_copy(give_d, ds_ref.at[:, c], 8)])
    wait(swap_s)
    wait(swap_d)

    def outside(i, carry):
        at = pl.ds(pl.multiple_of(i * PAIR, PAIR), PAIR)
        xf = xt_ref[at, :].astype(F32)
        gf = gt_ref[at, :]
        wp = two_rows(wrow, i)
        ep2 = two_rows(erow, i)
        sp = s_ref[i].reshape(PAIR, STATE)
        dsp = ds_ref[i].reshape(PAIR, STATE)
        sh, sl = split(sp)
        dsh, dsl = split(dsp)
        yy = (nt(sh, q_ref[...]) + nt(sl, q_ref[...])) * ep2
        dxs = (nt(dsh, k_ref[...]) + nt(dsl, k_ref[...])) * wp
        gv_ref[:, at] = (dxt[at, :] + dxs + two_rows(skrow, i) * gf).T
        ge = (gf * ep2).astype(BF16)
        xw = (xf * wp).astype(BF16)
        qacc[...] += nn(sh.T, ge) + nn(sl.T, ge)
        kacc[...] += nn(dsh.T, xw) + nn(dsl.T, xw)
        fg, xd, sd = gf * yy, xf * dxs, sp * dsp
        for e in range(2):
            part = slice(e * WIDTH, (e + 1) * WIDTH)
            h = pl.ds(2 * i + e, 1)
            frow[h, :] += jnp.sum(fg[part], axis=0, keepdims=True)
            urow[h, :] = jnp.sum(xd[part], axis=0, keepdims=True)
            vrow[h, :] = jnp.sum(sd[part], axis=0, keepdims=True)
        return carry

    lax.fori_loop(0, 4, outside, 0)
    lax.fori_loop(4, 8, outside, 0)
    def reach(axis, d, src, dst, n):
        return pltpu.make_async_remote_copy(
            src_ref=src, dst_ref=dst, send_sem=send.at[n, d - 1], recv_sem=recv.at[n, d - 1],
            device_id=device(axis, other(axis, d)), device_id_type=MESH,
        )

    def small_start(axis, buf, value, n):
        buf[coord[axis]] = value
        mine = buf.at[coord[axis]]
        return start([reach(axis, d, mine, mine, n) for d in range(1, 4)])

    def small_sum(copies, buf):
        wait(copies)
        return (buf[0] + buf[1]) + (buf[2] + buf[3])

    def pick(dims, axis, value):
        return tuple(value if n == axis else slice(None) for n in dims)

    def reduce_start(src, dims, axis, dst, n):
        return start([
            reach(axis, d, src.at[pick(dims, axis, other(axis, d))], dst.at[d - 1], n) for d in range(1, 4)
        ])

    parts, sums_a, sums_b, rows = (dw0, dw1, dw2), (a0, a1, a2), (b0, b1, b2), (w0, w1, w2)
    layouts = ("xzy", "xyz", "xzy")
    second, third, last = [], [], []
    for p, (_, order) in enumerate(PARTS):
        wait(first[p])
        got = recv_a[p]
        mine = parts[p][pick(layouts[p], order[0], coord[order[0]])]
        sums_a[p][...] = mine + (got[0] + got[1])
        rest = layouts[p].replace(order[0], "")
        second.append(reduce_start(sums_a[p], rest, order[1], recv_b[p], p))

    lax.fori_loop(8, CHIPS, outside, 0)
    store = pltpu.make_async_copy(gv_ref, gv_hbm, out_sem)
    store.start()
    dst = jnp.where(causal, acc[...], 0.0).astype(BF16)
    gk_ref[...] = nn(dst, q_ref[...]) + kacc[...].T
    gq_ref[...] = (nn(k_ref[...].T, dst) + qacc[...]).T
    upto = jnp.where(ii <= jj, 1.0, 0.0).astype(F32)
    decay = jnp.exp(run2[:, SPAN - 1 :] * (1.0 / LOG2E))
    dt = dt_ref[...]
    rate = jnp.exp(column(dl_ref[...]))
    tail = jnp.sum(urow[...], axis=1, keepdims=True)
    tail = tail + decay * jnp.sum(vrow[...], axis=1, keepdims=True)
    r = rrow[...] + urow[...]
    da = nn(frow[...] - r, upto, HIGHEST) + tail
    gs_ref[...] = r / dt - rate * da
    g_decay = jnp.sum(-rate * dt * da, axis=1, keepdims=True)
    g_skip = jnp.sum(xrow[...], axis=1, keepdims=True)
    lane = lax.broadcasted_iota(jnp.int32, (HEADS, 128), 1)
    s_core[c] = jnp.where(lane == 0, g_decay, jnp.where(lane == 1, g_skip, 0.0))
    wait(start([core_copy(s_core.at[c], s_core.at[c], 9)]))
    small = small_start("x", s_x, s_core[0] + s_core[1], 9)
    for p, (_, order) in enumerate(PARTS):
        wait(second[p])
        rest = layouts[p].replace(order[0], "")
        got = recv_b[p]
        mine = sums_a[p][pick(rest, order[1], coord[order[1]])]
        sums_b[p][...] = (mine + got[0]) + (got[1] + got[2])
        third.append(reduce_start(sums_b[p], order[2], order[2], recv_c[p], 3 + p))
    small = small_start("y", s_y, small_sum(small, s_x), 10)
    for p, (_, order) in enumerate(PARTS):
        wait(third[p])
        got = recv_c[p]
        rows[p][y] = (sums_b[p][coord[order[2]]] + got[0]) + (got[1] + got[2])
        last.extend(start([reach("y", d, rows[p].at[y], rows[p].at[y], 6 + p) for d in range(1, 4)]))
    small = small_start("z", s_z, small_sum(small, s_y), 11)
    smo_ref[...] = small_sum(small, s_z)
    store.wait()
    wait(last)
    for n in range(4):
        gw_ref[16 * n : 16 * n + 8, :768] = w0[n]
        gw_ref[16 * n : 16 * n + 8, 768:] = w1[n, :, :256]
        gw_ref[16 * n + 8 : 16 * n + 16, :384] = w1[n, :, 256:]
        gw_ref[16 * n + 8 : 16 * n + 16, 384:] = w2[n]


def output_kernel(
    gv, gk, gq, gs, small, gw, gv_out, gk_out, gq_out, gs_out, decay_out, skip_out, gw_out,
    vv, vk, vq, vs, vm, vw, vd, vp, into, out,
):
    size = SPAN // 8
    parts = [pl.ds(n * size, size) for n in range(8)]
    moves = [(gv.at[n], vv.at[n], gv_out.at[n]) for n in parts]
    moves += [(gw, vw, gw_out), (gk, vk, gk_out), (gq, vq, gq_out), (gs, vs, gs_out)]
    first = pltpu.make_async_copy(small, vm, into.at[12])
    reads = [pltpu.make_async_copy(a, b, into.at[n]) for n, (a, b, _) in enumerate(moves)]
    writes = [pltpu.make_async_copy(b, a, out.at[n]) for n, (_, b, a) in enumerate(moves)]
    writes += [pltpu.make_async_copy(vd, decay_out, out.at[12]), pltpu.make_async_copy(vp, skip_out, out.at[13])]
    first.start()
    for n in reads:
        n.start()
    first.wait()
    i = lax.broadcasted_iota(jnp.int32, (HEADS, HEADS), 0)
    j = lax.broadcasted_iota(jnp.int32, (HEADS, HEADS), 1)
    for n, ref in enumerate((vd, vp)):
        whole = jnp.broadcast_to(vm[:, n : n + 1], (HEADS, HEADS))
        ref[...] = jnp.sum(jnp.where(i == j, whole, 0.0), axis=0, keepdims=True)
        writes[12 + n].start()
    for a, b in zip(reads, writes):
        a.wait()
        b.start()
    for n in writes:
        n.wait()


def sds(shape, dtype=F32):
    return jax.ShapeDtypeStruct(shape, dtype)


def local(token_values, write_keys, read_queries, step_sizes, decay_log, skip_gain, out_weight, out_grad):
    x, k, q, dt, og = token_values[0], write_keys[0], read_queries[0], step_sizes[0], out_grad[0]
    dl, sk = decay_log.reshape(1, HEADS), skip_gain.reshape(1, HEADS)
    vm, dma = pltpu.VMEM, pltpu.SemaphoreType.DMA
    anywhere = pl.BlockSpec(memory_space=pl.ANY)
    inside = pl.BlockSpec(memory_space=pltpu.VMEM)
    row = vm((HEADS, SPAN), F32)
    heads = vm((CHIPS, 8, 8, STATE), F32)
    packed = vm((CHIPS, 9, 8, STATE), F32)
    pairs = vm((CHIPS, 2, 8, 8, STATE), F32)
    wides = [w for w, _ in PARTS]
    made = pl.pallas_call(
        mixer_kernel,
        out_shape=(
            sds((SPAN, INNER)), sds((SPAN, STATE)), sds((SPAN, STATE)), sds((HEADS, SPAN)),
            sds((HEADS, 128)), sds((64, MODEL)),
        ),
        in_specs=[anywhere] * 8,
        out_specs=(anywhere,) + (inside,) * 5,
        scratch_shapes=[
            vm((SPAN, INNER), BF16), vm((SPAN, STATE), BF16), vm((SPAN, STATE), BF16), row,
            vm((1, HEADS), F32), vm((1, HEADS), F32), vm((INNER, MODEL), BF16), vm((SPAN, MODEL), BF16),
            row, row, row, row, row, row, row, row, row, vm((HEADS, STATE), F32),
            vm((512, SPAN), F32), vm((INNER, SPAN), BF16), vm((INNER, SPAN), F32),
            pairs, pairs, vm((CHIPS, 2, 8, STATE), F32), heads, heads, vm((CHIPS, 2, 8, STATE), F32),
            packed, packed, heads, heads, packed, packed, heads, heads,
            pairs, pairs, heads, heads,
            vm((SPAN, SPAN), F32), vm((SPAN, SPAN), F32), vm((STATE, SPAN), F32), vm((STATE, SPAN), F32),
            vm((CHIPS, 2, WIDTH, SPAN), F32), vm((CHIPS, WIDTH, SPAN), F32),
            vm((INNER, SPAN), F32), vm((SPAN, INNER), F32),
            vm((SPAN, MODEL), F32), vm((SPAN, MODEL), F32), vm((SPAN, STATE), F32), vm((SPAN, STATE), F32),
            row, vm((2 * SPAN, MODEL), BF16), *[vm((4, 4, 4, 8, w), F32) for w in wides],
            *[vm((4, 4, 8, w), F32) for w in wides],
            *[vm((4, 8, w), F32) for w in wides],
            *[vm((2, 4, 4, 8, w), F32) for w in wides],
            *[vm((3, 4, 8, w), F32) for w in wides],
            *[vm((3, 8, w), F32) for w in wides],
            *[vm((4, 8, w), F32) for w in wides],
            vm((2, 2, 4, 8, wides[0]), F32), vm((4, 2, 2, 8, wides[1]), F32), vm((4, 2, 2, 8, wides[2]), F32),
            vm((2, HEADS, 128), F32),
            *[vm((4, HEADS, 128), F32)] * 3,
            dma((8,)), dma, dma((10,)), dma((10,)), dma((4, CHIPS)), dma((4, CHIPS)),
            dma((54,)), dma((54,)), dma((12, 3)), dma((12, 3)),
        ],
        compiler_params=pltpu.CompilerParams(
            vmem_limit_bytes=60 * 1024 * 1024, collective_id=0, has_side_effects=True
        ),
        name="mixer",
    )(x, k, q, dt, dl, sk, out_weight, og)
    gv, gk, gq, gs, decay, skip, gw = pl.pallas_call(
        output_kernel,
        out_shape=(
            sds((SPAN, INNER)), sds((SPAN, STATE)), sds((SPAN, STATE)), sds((HEADS, SPAN)),
            sds((1, HEADS)), sds((1, HEADS)), sds((64, MODEL)),
        ),
        in_specs=[anywhere] * 6,
        out_specs=(anywhere,) * 7,
        scratch_shapes=[
            vm((SPAN, INNER), F32), vm((SPAN, STATE), F32), vm((SPAN, STATE), F32), row,
            vm((HEADS, 128), F32), vm((64, MODEL), F32), vm((1, HEADS), F32), vm((1, HEADS), F32),
            dma((13,)), dma((14,)),
        ],
        compiler_params=pltpu.CompilerParams(vmem_limit_bytes=60 * 1024 * 1024),
        name="output",
    )(*made)
    return gv[None], gk[None], gq[None], gs[None], decay.reshape(HEADS), skip.reshape(HEADS), gw


def solution(mesh):
    by_time = P("rec", "tm", None)
    by_head = P("rec", None, "tm")
    return jax.shard_map(
        local,
        mesh=mesh,
        in_specs=(by_time, by_time, by_time, by_head, P(), P(), P(), by_time),
        out_specs=(by_time, by_time, by_time, by_head, P(), P(), P("tm", None)),
        check_vma=False,
    )
```

```python
import jax
import jax.numpy as jnp
from jax import lax
from jax.experimental import pallas as pl
from jax.experimental.pallas import tpu as pltpu
from jax.sharding import PartitionSpec as P

HEADS = 32
WIDTH = 64
PAIR = 2 * WIDTH
STATE = 128
SPAN = 256
INNER = HEADS * WIDTH
MODEL = 1024
CHIPS = 16
LOG2E = 1.4426950408889634
MESH = pl.DeviceIdType.MESH
HIGHEST = lax.Precision.HIGHEST
F32 = jnp.float32
BF16 = jnp.bfloat16


def nn(a, b, precision=None):
    return lax.dot_general(
        a, b, (((1,), (0,)), ((), ())), precision=precision, preferred_element_type=F32
    )


def nt(a, b, precision=None):
    return lax.dot_general(
        a, b, (((1,), (1,)), ((), ())), precision=precision, preferred_element_type=F32
    )


def column(row):
    i = lax.broadcasted_iota(jnp.int32, (HEADS, HEADS), 0)
    j = lax.broadcasted_iota(jnp.int32, (HEADS, HEADS), 1)
    whole = jnp.broadcast_to(row, (HEADS, HEADS))
    return jnp.sum(jnp.where(i == j, whole, 0.0), axis=1, keepdims=True)


def running_sums(dt, rate):
    s = lax.broadcasted_iota(jnp.int32, (SPAN, SPAN), 0)
    t = lax.broadcasted_iota(jnp.int32, (SPAN, SPAN), 1)
    upto = jnp.where(s <= t, 1.0, 0.0).astype(F32)
    return nn(-rate * dt, upto, HIGHEST)


def two_rows(ref, k):
    top = jnp.broadcast_to(ref[pl.ds(2 * k, 1), :], (WIDTH, ref.shape[1]))
    low = jnp.broadcast_to(ref[pl.ds(2 * k + 1, 1), :], (WIDTH, ref.shape[1]))
    return jnp.concatenate([top, low], axis=0)


def split(v):
    high = v.astype(BF16)
    return high, (v - high.astype(F32)).astype(BF16)


PARTS = ((768, "xyz"), (640, "yzx"), (640, "zxy"))
HALF = SPAN // 2


def tile(v):
    return v.reshape(8, 8, STATE)


def mixer_kernel(
    x_hbm, k_hbm, q_hbm, dt_hbm, dl_hbm, sk_hbm, w_hbm, og_hbm,
    gv_hbm, gk_hbm, gq_hbm, gs_hbm, smo_hbm, gw_hbm,
    x_ref, k_ref, q_ref, dt_ref, dl_ref, sk_ref, w_ref, og_ref,
    run2, crow, wrow, erow, skrow, frow, rrow, urow, xrow, vrow,
    gbuf, xt_ref, gt_ref, t_ref, e_ref, d_ref, tp, ep, dp,
    upf, gotf, backf, homef, upb, gotb, backb, homeb,
    s_ref, ds_ref, give_s, give_d,
    scores, acc, qacc, kacc, ysum, yp, dxt, gv_ref, gk_ref, gq_ref, gs_ref, smo_ref, gw_ref,
    f_og, r_og, f_q, r_q, r_e, rhs, dw0, dw1, dw2,
    a0, a1, a2, b0, b1, b2, ra0, ra1, ra2, rb0, rb1, rb2, rc0, rc1, rc2, w0, w1, w2, q0, q1, q2,
    s_core, s_x, s_y, s_z,
    in_sem, out_sem, core_send, core_recv, plane_send, plane_recv,
    first_send, first_recv, send, recv,
):
    y, me = lax.axis_index("rec"), lax.axis_index("tm")
    c, g = lax.rem(me, 2), lax.div(me, 2)
    x, z = lax.div(g, 4), lax.rem(g, 4)
    partner = me + 1 - 2 * c
    coord = {"x": x, "y": y, "z": z}
    own = c == 0

    loads = [
        pltpu.make_async_copy(src, dst, in_sem.at[n])
        for n, (src, dst) in enumerate((
            (dt_hbm, dt_ref), (dl_hbm, dl_ref), (x_hbm, x_ref), (k_hbm, k_ref),
            (q_hbm, q_ref), (og_hbm, og_ref), (w_hbm, w_ref), (sk_hbm, sk_ref),
        ))
    ]
    for n in loads:
        n.start()

    def device(axis, value):
        if axis == "x":
            return (y, (value * 4 + z) * 2 + c)
        if axis == "z":
            return (y, (x * 4 + value) * 2 + c)
        return (value, me)

    def other(axis, d):
        return lax.rem(coord[axis] + d, 4)

    def peer(d):
        return lax.rem(g + d, CHIPS)

    barrier = pltpu.get_barrier_semaphore()
    pl.semaphore_signal(barrier, inc=1, device_id=(y, partner), device_id_type=MESH)
    for d in range(1, CHIPS):
        pl.semaphore_signal(barrier, inc=1, device_id=(y, peer(d) * 2 + c), device_id_type=MESH)
    for d in range(1, 4):
        pl.semaphore_signal(barrier, inc=1, device_id=device("y", other("y", d)), device_id_type=MESH)

    def core_copy(src, dst, n):
        return pltpu.make_async_remote_copy(
            src_ref=src, dst_ref=dst, send_sem=core_send.at[n], recv_sem=core_recv.at[n],
            device_id=(y, partner), device_id_type=MESH,
        )

    def both(a, b):
        return jnp.where(own, a, b), jnp.where(own, b, a)

    def start(copies):
        for n in copies:
            n.start()
        return copies

    def wait(copies):
        for n in copies:
            n.wait()

    def spread(src, dst, n):
        return [
            pltpu.make_async_remote_copy(
                src_ref=src.at[peer(d)], dst_ref=dst.at[g],
                send_sem=plane_send.at[n, d], recv_sem=plane_recv.at[n, d],
                device_id=(y, peer(d) * 2 + c), device_id_type=MESH,
            )
            for d in range(1, CHIPS)
        ]

    loads[0].wait()
    loads[1].wait()
    dt = dt_ref[...]
    rate = jnp.exp(column(dl_ref[...]))
    run = running_sums(dt, rate)
    end = run[:, SPAN - 1 :]
    wrow[...] = jnp.exp(end - run) * dt
    erow[...] = jnp.exp(run)
    run2[...] = run * LOG2E
    crow[...] = run * LOG2E - jnp.log2(dt)
    vrow[...] = jnp.broadcast_to(jnp.exp(end), (HEADS, STATE))
    for h in range(HEADS):
        d_ref[h // 2, h % 2] = jnp.broadcast_to(vrow[h : h + 1, :], (8, STATE))

    loads[2].wait()
    loads[3].wait()

    def local_state(i, carry):
        at = pl.ds(pl.multiple_of(i * PAIR, PAIR), PAIR)
        xt = x_ref[:, at].T
        xt_ref[at, :] = xt
        high, low = split(xt.astype(F32) * two_rows(wrow, i))
        t_ref[i] = (nn(high, k_ref[...]) + nn(low, k_ref[...])).reshape(2, 8, 8, STATE)
        return carry

    lax.fori_loop(0, CHIPS, local_state, 0)
    pl.semaphore_wait(barrier, CHIPS + 3)
    wait(start([core_copy(d_ref, dp, 0), core_copy(t_ref.at[:, 1 - c], tp, 1)]))

    def combine_forward(i, carry):
        d0, d1 = both(d_ref[i, c], dp[i, c])
        t0, t1 = both(t_ref[i, c], tp[i])
        upf[i, 0:8] = d1[None] * t0 + t1
        upf[i, 8] = d0 * d1
        return carry

    lax.fori_loop(0, CHIPS, combine_forward, 0)

    forward_out = start(spread(upf, gotf, 0))
    gotf[g] = upf[g]

    wait(loads[4:])
    f_og[...] = og_ref[...].astype(F32)
    f_q[...] = q_ref[...].astype(F32)
    early = start([core_copy(f_og, r_og, 3), core_copy(f_q, r_q, 4), core_copy(erow, r_e, 5)])

    def cotangent(m, carry):
        rows = pl.ds(pl.multiple_of(m * 512, 512), 512)
        gbuf[...] = nt(w_ref[rows, :], og_ref[...])
        for n in range(4):
            i = m * 4 + n
            at = pl.ds(pl.multiple_of(i * PAIR, PAIR), PAIR)
            gm = gbuf[n * PAIR : (n + 1) * PAIR, :]
            gt_ref[at, :] = gm
            high, low = split(gm * two_rows(erow, i))
            e_ref[i] = (nn(high, q_ref[...]) + nn(low, q_ref[...])).reshape(2, 8, 8, STATE)
        return carry

    lax.fori_loop(0, 4, cotangent, 0)
    swap_e = start([core_copy(e_ref.at[:, 1 - c], ep, 2)])

    skrow[...] = jnp.broadcast_to(column(sk_ref[...]), (HEADS, SPAN))
    jj = lax.broadcasted_iota(jnp.int32, (SPAN, SPAN), 0)
    ii = lax.broadcasted_iota(jnp.int32, (SPAN, SPAN), 1)
    causal = jj <= ii
    scores[...] = jnp.where(causal, nt(k_ref[...], q_ref[...]), 0.0)
    acc[...] = jnp.zeros_like(acc)
    qacc[...] = jnp.zeros_like(qacc)
    kacc[...] = jnp.zeros_like(kacc)

    def row_sums(ref, value, i):
        for e in range(2):
            ref[pl.ds(2 * i + e, 1), :] = jnp.sum(
                value[e * WIDTH : (e + 1) * WIDTH], axis=0, keepdims=True
            )

    def inside(i, carry):
        at = pl.ds(pl.multiple_of(i * PAIR, PAIR), PAIR)
        xp = x_ref[:, at]
        xt = xt_ref[at, :]
        gf = gt_ref[at, :]
        gh, gl = split(gf)
        x2 = jnp.concatenate([xp, xp], axis=1)
        y_parts, yl_parts, dx_parts = [], [], []
        for e in range(2):
            row = run2[pl.ds(2 * i + e, 1), :]
            ccol = jnp.broadcast_to(crow[pl.ds(2 * i + e, 1), :], (HALF, SPAN)).T
            d00 = jnp.exp2(jnp.minimum(row[:, :HALF] - ccol[:HALF], 2.0))
            d01 = jnp.exp2(row[:, HALF:] - ccol[:HALF])
            d11 = jnp.exp2(jnp.minimum(row[:, HALF:] - ccol[HALF:], 2.0))
            n00, l00 = split(d00 * scores[:HALF, :HALF])
            n01, l01 = split(d01 * scores[:HALF, HALF:])
            n11, l11 = split(d11 * scores[HALF:, HALF:])
            n10 = jnp.zeros((HALF, HALF), BF16)

            def square(a, b, d):
                top = jnp.concatenate([a, b], axis=1)
                return jnp.concatenate([top, jnp.concatenate([n10, d], axis=1)], axis=0)

            n = square(n00, n01, n11)
            part = slice(e * WIDTH, (e + 1) * WIDTH)
            y_parts.append(nn(xt[part], n))
            yl_parts.append(nn(xt[part], square(l00, l01, l11)))
            dx = nt(jnp.concatenate([gh[part], gl[part]], axis=0), n)
            dx_parts.append(dx[:WIDTH] + dx[WIDTH:])
            blank = jnp.zeros((WIDTH, SPAN), BF16)
            if e == 0:
                gz = jnp.concatenate([gh[part], blank, gl[part], blank], axis=0)
            else:
                gz = jnp.concatenate([blank, gh[part], blank, gl[part]], axis=0)
            dn = nn(x2, gz)
            acc[:HALF, :HALF] += dn[:HALF, :HALF] * d00
            acc[:HALF, HALF:] += dn[:HALF, HALF:] * d01
            acc[HALF:, HALF:] += dn[HALF:, HALF:] * d11
        xf = xt.astype(F32)
        yy = jnp.concatenate(y_parts, axis=0)
        dx = jnp.concatenate(dx_parts, axis=0)
        whole = yy + jnp.concatenate(yl_parts, axis=0) + two_rows(skrow, i) * xf
        ysum[i] = whole.reshape(2, WIDTH, SPAN)
        dxt[at, :] = dx
        row_sums(frow, gf * yy, i)
        row_sums(rrow, xf * dx, i)
        row_sums(xrow, gf * xf, i)
        return carry

    wait(swap_e)

    def combine_backward(i, carry):
        d0, d1 = both(d_ref[i, c], dp[i, c])
        e0, e1 = both(e_ref[i, c], ep[i])
        upb[i, 0:8] = e0 + d0[None] * e1
        upb[i, 8] = d0 * d1
        return carry

    lax.fori_loop(0, CHIPS, combine_backward, 0)
    backward_out = start(spread(upb, gotb, 2))
    gotb[g] = upb[g]
    wait(forward_out)
    carried = jnp.zeros((8, 8, STATE), F32)
    for i in range(CHIPS):
        backf[i] = carried
        carried = gotf[i, 8][None] * carried + gotf[i, 0:8]
    forward_in = start(spread(backf, homef, 1))
    homef[g] = backf[g]
    lax.fori_loop(0, CHIPS, inside, 0)
    wait(early)
    swap_y = start([core_copy(ysum.at[:, 1 - c], yp, 6)])
    rhs[:SPAN] = og_ref[...]
    rhs[SPAN:] = r_og[...].astype(BF16)
    s_mine, s_other = q_ref[...], r_q[...].astype(BF16)
    wait(backward_out)
    carried = jnp.zeros((8, 8, STATE), F32)
    for i in range(CHIPS - 1, -1, -1):
        backb[i] = carried
        carried = gotb[i, 8][None] * carried + gotb[i, 0:8]
    backward_in = start(spread(backb, homeb, 3))
    homeb[g] = backb[g]
    wait(swap_y)
    wait(forward_in)

    recv_a, recv_b, recv_c = (ra0, ra1, ra2), (rb0, rb1, rb2), (rc0, rc1, rc2)
    first, used = ([], [], []), []
    low, high = pl.ds(0, 2), pl.ds(2, 2)

    def first_copy(axis, d, src, dst):
        n = len(used)
        used.append(n)
        return pltpu.make_async_remote_copy(
            src_ref=src, dst_ref=dst, send_sem=first_send.at[n], recv_sem=first_recv.at[n],
            device_id=device(axis, other(axis, d)), device_id_type=MESH,
        )

    def send_far(axis, piece, relay):
        return start([first_copy(axis, 1, piece.at[low], relay.at[0]), first_copy(axis, 3, piece.at[high], relay.at[1])])

    def send_sums(axis, far, up, down, relay, got0, got1):
        wait(far)
        relay[0] = relay[0] + up[:2]
        relay[1] = relay[1] + down[2:]
        return start([first_copy(axis, 1, relay.at[0], got0.at[low]), first_copy(axis, 3, relay.at[1], got1.at[high])])

    def across(states, queries):
        high, low = split(states)
        return nt(high, queries) + nt(low, queries)

    fars = []
    for turn in (2, 1, 3, 0):
        m = other("x", turn)
        own_states, other_states, own_rows, other_rows, own_y, other_y = [], [], [], [], [], []
        for n in range(4):
            i = m * 4 + n
            d0, _ = both(d_ref[i, c], dp[i, c])
            t0, _ = both(t_ref[i, c], tp[i])
            s0 = homef[i]
            s1 = d0[None] * s0 + t0
            mine, theirs = both(s0, s1)
            s_ref[i, c] = mine
            give_s[i] = theirs
            own_states.append(mine.reshape(WIDTH, STATE))
            other_states.append(theirs.reshape(WIDTH, STATE))
            own_rows.append(jnp.broadcast_to(erow[pl.ds(2 * i + c, 1), :], (WIDTH, SPAN)))
            other_rows.append(jnp.broadcast_to(r_e[pl.ds(2 * i + c, 1), :], (WIDTH, SPAN)))
            own_y.append(ysum[i, c])
            other_y.append(yp[i])

        def join(parts):
            return jnp.concatenate(parts, axis=0)

        left = join(own_y) + across(join(own_states), s_mine) * join(own_rows)
        right = join(other_y) + across(join(other_states), s_other) * join(other_rows)
        lhs = jnp.concatenate([left.astype(BF16), right.astype(BF16)], axis=1)
        whole = nn(lhs, rhs[...]).reshape(4, 4, 2, 8, MODEL)
        dw0[m] = whole[:, :, 0, :, :768]
        dw2[m] = whole[:, :, 1, :, 384:]
        for n in range(4):
            dw1[m, n, :, :, :256] = whole[:, n, 0, :, 768:]
            dw1[m, n, :, :, 256:] = whole[:, n, 1, :, :384]
        if turn == 2:
            far_x = send_far("x", dw0.at[m], q0)
        elif turn == 1:
            first[0].extend(start([first_copy("x", 1, dw0.at[m, high], ra0.at[0, high])]))
        elif turn == 3:
            first[0].extend(start([first_copy("x", 3, dw0.at[m, low], ra0.at[1, low])]))
        pairs = []
        for p, axis, dw, ra, q in ((1, "y", dw1, ra1, q1), (2, "z", dw2, ra2, q2)):
            pairs.append(send_far(axis, dw.at[m, other(axis, 2)], q.at[m]))
            first[p].extend(start([
                first_copy(axis, 1, dw.at[m, other(axis, 1), high], ra.at[0, m, high]),
                first_copy(axis, 3, dw.at[m, other(axis, 3), low], ra.at[1, m, low]),
            ]))
        fars.append((m, pairs))

    def relay_sums(step):
        m, pairs = fars[step]
        for far, (p, axis, dw, ra, q) in zip(pairs, ((1, "y", dw1, ra1, q1), (2, "z", dw2, ra2, q2))):
            up, down = dw[m, other(axis, 1)], dw[m, other(axis, 3)]
            first[p].extend(send_sums(axis, far, up, down, q.at[m], ra.at[0, m], ra.at[1, m]))

    swap_s = start([core_copy(give_s, s_ref.at[:, c], 7)])
    relay_sums(0)
    first[0].extend(send_sums("x", far_x, dw0[other("x", 1)], dw0[other("x", 3)], q0, ra0.at[0], ra0.at[1]))
    relay_sums(1)
    relay_sums(2)
    relay_sums(3)
    wait(backward_in)

    def finish_backward(i, carry):
        d0, d1 = both(d_ref[i, c], dp[i, c])
        e0, e1 = both(e_ref[i, c], ep[i])
        b1 = homeb[i]
        b0 = d1[None] * b1 + e1
        ds_ref[i, c], give_d[i] = both(b0, b1)
        return carry

    lax.fori_loop(0, CHIPS, finish_backward, 0)
    swap_d = start([core_copy(give_d, ds_ref.at[:, c], 8)])
    wait(swap_s)
    wait(swap_d)

    def outside(i, carry):
        at = pl.ds(pl.multiple_of(i * PAIR, PAIR), PAIR)
        xf = xt_ref[at, :].astype(F32)
        gf = gt_ref[at, :]
        wp = two_rows(wrow, i)
        ep2 = two_rows(erow, i)
        sp = s_ref[i].reshape(PAIR, STATE)
        dsp = ds_ref[i].reshape(PAIR, STATE)
        sh, sl = split(sp)
        dsh, dsl = split(dsp)
        yy = (nt(sh, q_ref[...]) + nt(sl, q_ref[...])) * ep2
        dxs = (nt(dsh, k_ref[...]) + nt(dsl, k_ref[...])) * wp
        gv_ref[:, at] = (dxt[at, :] + dxs + two_rows(skrow, i) * gf).T
        ge = (gf * ep2).astype(BF16)
        xw = (xf * wp).astype(BF16)
        qacc[...] += nn(sh.T, ge) + nn(sl.T, ge)
        kacc[...] += nn(dsh.T, xw) + nn(dsl.T, xw)
        fg, xd, sd = gf * yy, xf * dxs, sp * dsp
        for e in range(2):
            part = slice(e * WIDTH, (e + 1) * WIDTH)
            h = pl.ds(2 * i + e, 1)
            frow[h, :] += jnp.sum(fg[part], axis=0, keepdims=True)
            urow[h, :] = jnp.sum(xd[part], axis=0, keepdims=True)
            vrow[h, :] = jnp.sum(sd[part], axis=0, keepdims=True)
        return carry

    lax.fori_loop(0, 4, outside, 0)
    lax.fori_loop(4, 8, outside, 0)
    def reach(axis, d, src, dst, n):
        return pltpu.make_async_remote_copy(
            src_ref=src, dst_ref=dst, send_sem=send.at[n, d - 1], recv_sem=recv.at[n, d - 1],
            device_id=device(axis, other(axis, d)), device_id_type=MESH,
        )

    def small_start(axis, buf, value, n):
        buf[coord[axis]] = value
        mine = buf.at[coord[axis]]
        return start([reach(axis, d, mine, mine, n) for d in range(1, 4)])

    def small_sum(copies, buf):
        wait(copies)
        return (buf[0] + buf[1]) + (buf[2] + buf[3])

    def pick(dims, axis, value):
        return tuple(value if n == axis else slice(None) for n in dims)

    def reduce_start(src, dims, axis, dst, n):
        return start([
            reach(axis, d, src.at[pick(dims, axis, other(axis, d))], dst.at[d - 1], n) for d in range(1, 4)
        ])

    parts, sums_a, sums_b, rows = (dw0, dw1, dw2), (a0, a1, a2), (b0, b1, b2), (w0, w1, w2)
    layouts = ("xzy", "xyz", "xzy")
    second, third, last = [], [], []
    for p, (_, order) in enumerate(PARTS):
        wait(first[p])
        got = recv_a[p]
        mine = parts[p][pick(layouts[p], order[0], coord[order[0]])]
        sums_a[p][...] = mine + (got[0] + got[1])
        rest = layouts[p].replace(order[0], "")
        second.append(reduce_start(sums_a[p], rest, order[1], recv_b[p], p))

    lax.fori_loop(8, CHIPS, outside, 0)
    stores = [
        pltpu.make_async_copy(a, b, out_sem.at[n])
        for n, (a, b) in enumerate((
            (gv_ref, gv_hbm), (gk_ref, gk_hbm), (gq_ref, gq_hbm), (gs_ref, gs_hbm), (smo_ref, smo_hbm), (gw_ref, gw_hbm),
        ))
    ]
    stores[0].start()
    dst = jnp.where(causal, acc[...], 0.0).astype(BF16)
    gk_ref[...] = nn(dst, q_ref[...]) + kacc[...].T
    gq_ref[...] = (nn(k_ref[...].T, dst) + qacc[...]).T
    upto = jnp.where(ii <= jj, 1.0, 0.0).astype(F32)
    decay = jnp.exp(run2[:, SPAN - 1 :] * (1.0 / LOG2E))
    dt = dt_ref[...]
    rate = jnp.exp(column(dl_ref[...]))
    tail = jnp.sum(urow[...], axis=1, keepdims=True)
    tail = tail + decay * jnp.sum(vrow[...], axis=1, keepdims=True)
    r = rrow[...] + urow[...]
    da = nn(frow[...] - r, upto, HIGHEST) + tail
    gs_ref[...] = r / dt - rate * da
    start(stores[1:4])
    g_decay = jnp.sum(-rate * dt * da, axis=1, keepdims=True)
    g_skip = jnp.sum(xrow[...], axis=1, keepdims=True)
    lane = lax.broadcasted_iota(jnp.int32, (HEADS, 128), 1)
    s_core[c] = jnp.where(lane == 0, g_decay, jnp.where(lane == 1, g_skip, 0.0))
    wait(start([core_copy(s_core.at[c], s_core.at[c], 9)]))
    small = small_start("x", s_x, s_core[0] + s_core[1], 9)
    for p, (_, order) in enumerate(PARTS):
        wait(second[p])
        rest = layouts[p].replace(order[0], "")
        got = recv_b[p]
        mine = sums_a[p][pick(rest, order[1], coord[order[1]])]
        sums_b[p][...] = (mine + got[0]) + (got[1] + got[2])
        third.append(reduce_start(sums_b[p], order[2], order[2], recv_c[p], 3 + p))
    small = small_start("y", s_y, small_sum(small, s_x), 10)
    for p, (_, order) in enumerate(PARTS):
        wait(third[p])
        got = recv_c[p]
        rows[p][y] = (sums_b[p][coord[order[2]]] + got[0]) + (got[1] + got[2])
        last.extend(start([reach("y", d, rows[p].at[y], rows[p].at[y], 6 + p) for d in range(1, 4)]))
    small = small_start("z", s_z, small_sum(small, s_y), 11)
    smo_ref[...] = small_sum(small, s_z)
    stores[4].start()
    wait(last)
    for n in range(4):
        gw_ref[16 * n : 16 * n + 8, :768] = w0[n]
        gw_ref[16 * n : 16 * n + 8, 768:] = w1[n, :, :256]
        gw_ref[16 * n + 8 : 16 * n + 16, :384] = w1[n, :, 256:]
        gw_ref[16 * n + 8 : 16 * n + 16, 384:] = w2[n]
    stores[5].start()
    wait(stores)


def output_kernel(
    gv, gk, gq, gs, small, gw, gv_out, gk_out, gq_out, gs_out, decay_out, skip_out, gw_out,
    vv, vk, vq, vs, vm, vw, vd, vp, into, out,
):
    size = SPAN // 8
    parts = [pl.ds(n * size, size) for n in range(8)]
    moves = [(gv.at[n], vv.at[n], gv_out.at[n]) for n in parts]
    moves += [(gw, vw, gw_out), (gk, vk, gk_out), (gq, vq, gq_out), (gs, vs, gs_out)]
    first = pltpu.make_async_copy(small, vm, into.at[12])
    reads = [pltpu.make_async_copy(a, b, into.at[n]) for n, (a, b, _) in enumerate(moves)]
    writes = [pltpu.make_async_copy(b, a, out.at[n]) for n, (_, b, a) in enumerate(moves)]
    writes += [pltpu.make_async_copy(vd, decay_out, out.at[12]), pltpu.make_async_copy(vp, skip_out, out.at[13])]
    first.start()
    for n in reads:
        n.start()
    first.wait()
    i = lax.broadcasted_iota(jnp.int32, (HEADS, HEADS), 0)
    j = lax.broadcasted_iota(jnp.int32, (HEADS, HEADS), 1)
    for n, ref in enumerate((vd, vp)):
        whole = jnp.broadcast_to(vm[:, n : n + 1], (HEADS, HEADS))
        ref[...] = jnp.sum(jnp.where(i == j, whole, 0.0), axis=0, keepdims=True)
        writes[12 + n].start()
    for a, b in zip(reads, writes):
        a.wait()
        b.start()
    for n in writes:
        n.wait()


def sds(shape, dtype=F32):
    return jax.ShapeDtypeStruct(shape, dtype)


def local(token_values, write_keys, read_queries, step_sizes, decay_log, skip_gain, out_weight, out_grad):
    x, k, q, dt, og = token_values[0], write_keys[0], read_queries[0], step_sizes[0], out_grad[0]
    dl, sk = decay_log.reshape(1, HEADS), skip_gain.reshape(1, HEADS)
    vm, dma = pltpu.VMEM, pltpu.SemaphoreType.DMA
    anywhere = pl.BlockSpec(memory_space=pl.ANY)
    inside = pl.BlockSpec(memory_space=pltpu.VMEM)
    row = vm((HEADS, SPAN), F32)
    heads = vm((CHIPS, 8, 8, STATE), F32)
    packed = vm((CHIPS, 9, 8, STATE), F32)
    pairs = vm((CHIPS, 2, 8, 8, STATE), F32)
    wides = [w for w, _ in PARTS]
    made = pl.pallas_call(
        mixer_kernel,
        out_shape=(
            sds((SPAN, INNER)), sds((SPAN, STATE)), sds((SPAN, STATE)), sds((HEADS, SPAN)),
            sds((HEADS, 128)), sds((64, MODEL)),
        ),
        in_specs=[anywhere] * 8,
        out_specs=(anywhere,) * 6,
        scratch_shapes=[
            vm((SPAN, INNER), BF16), vm((SPAN, STATE), BF16), vm((SPAN, STATE), BF16), row,
            vm((1, HEADS), F32), vm((1, HEADS), F32), vm((INNER, MODEL), BF16), vm((SPAN, MODEL), BF16),
            row, row, row, row, row, row, row, row, row, vm((HEADS, STATE), F32),
            vm((512, SPAN), F32), vm((INNER, SPAN), BF16), vm((INNER, SPAN), F32),
            pairs, pairs, vm((CHIPS, 2, 8, STATE), F32), heads, heads, vm((CHIPS, 2, 8, STATE), F32),
            packed, packed, heads, heads, packed, packed, heads, heads,
            pairs, pairs, heads, heads,
            vm((SPAN, SPAN), F32), vm((SPAN, SPAN), F32), vm((STATE, SPAN), F32), vm((STATE, SPAN), F32),
            vm((CHIPS, 2, WIDTH, SPAN), F32), vm((CHIPS, WIDTH, SPAN), F32),
            vm((INNER, SPAN), F32), vm((SPAN, INNER), F32),
            vm((SPAN, STATE), F32), vm((SPAN, STATE), F32), row, vm((HEADS, 128), F32), vm((64, MODEL), F32),
            vm((SPAN, MODEL), F32), vm((SPAN, MODEL), F32), vm((SPAN, STATE), F32), vm((SPAN, STATE), F32),
            row, vm((2 * SPAN, MODEL), BF16), *[vm((4, 4, 4, 8, w), F32) for w in wides],
            *[vm((4, 4, 8, w), F32) for w in wides],
            *[vm((4, 8, w), F32) for w in wides],
            *[vm((2, 4, 4, 8, w), F32) for w in wides],
            *[vm((3, 4, 8, w), F32) for w in wides],
            *[vm((3, 8, w), F32) for w in wides],
            *[vm((4, 8, w), F32) for w in wides],
            vm((2, 2, 4, 8, wides[0]), F32), vm((4, 2, 2, 8, wides[1]), F32), vm((4, 2, 2, 8, wides[2]), F32),
            vm((2, HEADS, 128), F32),
            *[vm((4, HEADS, 128), F32)] * 3,
            dma((8,)), dma((6,)), dma((10,)), dma((10,)), dma((4, CHIPS)), dma((4, CHIPS)),
            dma((54,)), dma((54,)), dma((12, 3)), dma((12, 3)),
        ],
        compiler_params=pltpu.CompilerParams(
            vmem_limit_bytes=60 * 1024 * 1024, collective_id=0, has_side_effects=True
        ),
        name="mixer",
    )(x, k, q, dt, dl, sk, out_weight, og)
    gv, gk, gq, gs, decay, skip, gw = pl.pallas_call(
        output_kernel,
        out_shape=(
            sds((SPAN, INNER)), sds((SPAN, STATE)), sds((SPAN, STATE)), sds((HEADS, SPAN)),
            sds((1, HEADS)), sds((1, HEADS)), sds((64, MODEL)),
        ),
        in_specs=[anywhere] * 6,
        out_specs=(anywhere,) * 7,
        scratch_shapes=[
            vm((SPAN, INNER), F32), vm((SPAN, STATE), F32), vm((SPAN, STATE), F32), row,
            vm((HEADS, 128), F32), vm((64, MODEL), F32), vm((1, HEADS), F32), vm((1, HEADS), F32),
            dma((13,)), dma((14,)),
        ],
        compiler_params=pltpu.CompilerParams(vmem_limit_bytes=60 * 1024 * 1024),
        name="output",
    )(*made)
    return gv[None], gk[None], gq[None], gs[None], decay.reshape(HEADS), skip.reshape(HEADS), gw


def solution(mesh):
    by_time = P("rec", "tm", None)
    by_head = P("rec", None, "tm")
    return jax.shard_map(
        local,
        mesh=mesh,
        in_specs=(by_time, by_time, by_time, by_head, P(), P(), P(), by_time),
        out_specs=(by_time, by_time, by_time, by_head, P(), P(), P("tm", None)),
        check_vma=False,
    )
```
